32 devices in a mesh: replica: 4 (over x, core), shard: 8 (over z, y).
Axes of the slice: x: 2, y: 2, z: 4, core: 2. Of those that a mesh axis runs over, the one named last changes fastest.
Arguments:
- tokens: bfloat16 [32, 1024, 1024], P(('replica', 'shard')), may hold values from -6 to 6
- lengths: int32 [32], P(('replica', 'shard')), may hold values from 256 to 1024, as said below
- cotangent: bfloat16 [32, 1024, 1024], P(('replica', 'shard')), may hold values from -6 to 6
- w_qkv: bfloat16 [1024, 3072], P('shard'), may hold values from -0.1875 to 0.1875
- b_qv: bfloat16 [2048], P('shard'), may hold values from -3 to 3
- w_attn_out: bfloat16 [1024, 1024], P('shard'), may hold values from -1.5 to 1.5
- b_attn_out: bfloat16 [1024], P('shard'), may hold values from -3 to 3
- ln1_gain: bfloat16 [1024], P('shard'), may hold values from 0.099609375 to 1.8984375
- ln1_bias: bfloat16 [1024], P('shard'), may hold values from -3 to 3
- w_ffn_in: bfloat16 [1024, 4096], P('shard'), may hold values from -0.1875 to 0.1875
- b_ffn_in: bfloat16 [4096], P('shard'), may hold values from -3 to 3
- w_ffn_out: bfloat16 [4096, 1024], P('shard'), may hold values from -0.09375 to 0.09375
- b_ffn_out: bfloat16 [1024], P('shard'), may hold values from -3 to 3
- ln2_gain: bfloat16 [1024], P('shard'), may hold values from 0.099609375 to 1.8984375
- ln2_bias: bfloat16 [1024], P('shard'), may hold values from -3 to 3
Outputs:
- out: bfloat16 [32, 1024, 1024], P(('replica', 'shard'))
- grad_tokens: bfloat16 [32, 1024, 1024], P(('replica', 'shard'))
- grad_w_qkv: float32 [1024, 3072], P('shard')
- grad_b_qv: float32 [2048], P('shard')
- grad_w_attn_out: float32 [1024, 1024], P('shard')
- grad_b_attn_out: float32 [1024], P('shard')
- grad_ln1_gain: float32 [1024], P('shard')
- grad_ln1_bias: float32 [1024], P('shard')
- grad_w_ffn_in: float32 [1024, 4096], P('shard')
- grad_b_ffn_in: float32 [4096], P('shard')
- grad_w_ffn_out: float32 [4096, 1024], P('shard')
- grad_b_ffn_out: float32 [1024], P('shard')
- grad_ln2_gain: float32 [1024], P('shard')
- grad_ln2_bias: float32 [1024], P('shard')
The draws below stay inside these ranges and needn't reach their ends.
Inputs may be any that keep to these rules, and one draw needn't show every extreme that they name: `lengths`: sequence 0 holds exactly 1024 tokens; the others take any count in the range.
All inputs are finite; a program needn't handle non-finite values.
Results may differ from the reference program's by a relative error of at most 0.017.
Values may be sent and summed in bfloat16 or wider, within the bound.
No kernel may reach another device: no remote copies, remote signals or barrier semaphores. Data moves between devices by JAX's collectives and lax.ppermute only.
A program may use at most 384 MiB of HBM per device.

```python
import math
import jax
import jax.numpy as jnp
from jax import lax

D = 1024
HEADS = 16
HEAD_DIM = 64
FF = 4096
SEQ_LEN = 1024
MIN_LEN = 256
SEQS = 32


def draw_lengths(key, part):
    counts = jax.random.randint(key, (SEQS,), MIN_LEN, SEQ_LEN + 1)
    return counts.at[0].set(SEQ_LEN).astype(jnp.int32)


def levels(key, extent, shards, low, high):
    level = 1.0
    for dim, parts in shards:
        steps = jax.random.uniform(jax.random.fold_in(jax.random.fold_in(key, 6), dim), (parts,), jnp.float32, low / len(shards), high / len(shards))
        level = level * jnp.repeat(jnp.exp(steps), extent[dim] // parts).reshape((-1,) + (1,) * (len(extent) - 1 - dim))
    return level


def gaussian(key, shape, scale, most, pieces=(), kind=jnp.bfloat16):
    array = scale * jax.random.normal(key, shape, jnp.float32)
    if pieces:
        array = array * levels(key, shape, pieces, -0.22, 0.18)
    return jnp.clip(array, -most, most).astype(kind)


def setup_inputs(seed: int = 0) -> dict:
    keys = jax.random.split(jax.random.key(seed), 16)
    tokens = gaussian(keys[0], (SEQS, SEQ_LEN, D), 1.0, 6.0, ((0, 32),))
    lengths = draw_lengths(jax.random.fold_in(keys[15], 71), 0)
    cotangent = gaussian(keys[2], (SEQS, SEQ_LEN, D), 1.0, 6.0, ((0, 32),))
    w_qkv = gaussian(keys[3], (D, 3 * D), D ** -0.5, 0.1875, ((0, 8),))
    b_qv = gaussian(keys[4], (2 * D,), 0.5, 3.0, ((0, 8),))
    w_attn_out = gaussian(keys[5], (D, D), (D // 64) ** -0.5, 1.5, ((0, 8),))
    b_attn_out = gaussian(keys[6], (D,), 0.5, 3.0, ((0, 8),))
    ln1_gain = jnp.clip(1.0 + 0.18 * jax.random.normal(keys[7], (D,), jnp.float32), 0.099609375, 1.8984375).astype(jnp.bfloat16)
    ln1_bias = gaussian(keys[8], (D,), 0.5, 3.0, ((0, 8),))
    w_ffn_in = gaussian(keys[9], (D, FF), D ** -0.5, 0.1875, ((0, 8),))
    b_ffn_in = gaussian(keys[10], (FF,), 0.5, 3.0, ((0, 8),))
    w_ffn_out = gaussian(keys[11], (FF, D), FF ** -0.5, 0.09375, ((0, 8),))
    b_ffn_out = gaussian(keys[12], (D,), 0.5, 3.0, ((0, 8),))
    ln2_gain = jnp.clip(1.0 + 0.18 * jax.random.normal(keys[13], (D,), jnp.float32), 0.099609375, 1.8984375).astype(jnp.bfloat16)
    ln2_bias = gaussian(keys[14], (D,), 0.5, 3.0, ((0, 8),))
    return {"tokens": tokens, "lengths": lengths, "cotangent": cotangent, "w_qkv": w_qkv, "b_qv": b_qv, "w_attn_out": w_attn_out, "b_attn_out": b_attn_out, "ln1_gain": ln1_gain, "ln1_bias": ln1_bias, "w_ffn_in": w_ffn_in, "b_ffn_in": b_ffn_in, "w_ffn_out": w_ffn_out, "b_ffn_out": b_ffn_out, "ln2_gain": ln2_gain, "ln2_bias": ln2_bias}


@jax.custom_vjp
def low(v):
    return lax.optimization_barrier(v.astype(jnp.bfloat16)).astype(jnp.float32)

@jax.custom_vjp
def low_back(v):
    return v

def low_keep(v):
    return (low(v), None)

def low_pass(kept, grad):
    return (grad,)

def back_keep(v):
    return (v, None)

def back_low(kept, grad):
    return (low(grad),)
low.defvjp(low_keep, low_pass)
low_back.defvjp(back_keep, back_low)
HIGH = lax.Precision.HIGHEST
SQRT_HALF = 0.7071067811865476

def normalize(resid, gain, shift):
    mean_row = lax.optimization_barrier(jnp.mean(resid, axis=-1, keepdims=True))
    centred = resid - mean_row
    spread = lax.optimization_barrier(jnp.mean(centred * centred, axis=-1, keepdims=True))
    return centred * lax.rsqrt(spread + 1e-05) * gain + shift

def project(left, right):
    return jnp.einsum('gld,de->gle', left, right, precision=HIGH)

def layer(inputs, valid, params):
    w_qkv, b_qv, w_attn_out, b_attn_out, ln1_gain, ln1_bias, w_ffn_in, b_ffn_in, w_ffn_out, b_ffn_out, ln2_gain, ln2_bias = params
    groups = inputs.shape[0]
    width = inputs.shape[2]
    bias_full = jnp.concatenate([b_qv[:width], jnp.zeros((width,), b_qv.dtype), b_qv[width:]])
    proj_all = low_back(low(project(inputs, w_qkv) + bias_full))
    query_heads = proj_all[..., :width].reshape(groups, SEQ_LEN, HEADS, HEAD_DIM)
    key_heads = proj_all[..., width:2 * width].reshape(groups, SEQ_LEN, HEADS, HEAD_DIM)
    value_heads = proj_all[..., 2 * width:].reshape(groups, SEQ_LEN, HEADS, HEAD_DIM)
    block = min(512, SEQ_LEN)
    nblocks = SEQ_LEN // block
    key_ok = valid[:, None, None, :]

    def attend(query_block):
        raw = jnp.einsum('gqhd,gkhd->ghqk', query_block, key_heads, precision=HIGH) * 0.125
        raw = low_back(raw)
        raw = jnp.where(key_ok, raw, -1e+30)
        top = lax.optimization_barrier(jnp.max(raw, axis=-1, keepdims=True))
        expo = jnp.exp(raw - top)
        probs = expo / lax.optimization_barrier(jnp.sum(expo, axis=-1, keepdims=True))
        return jnp.einsum('ghqk,gkhd->gqhd', low(probs), value_heads, precision=HIGH)
    query_blocks = jnp.moveaxis(query_heads.reshape(groups, nblocks, block, HEADS, HEAD_DIM), 1, 0)
    context = lax.map(jax.checkpoint(attend), query_blocks)
    context = jnp.moveaxis(context, 0, 1).reshape(groups, SEQ_LEN, width)
    context = low_back(low(context))
    attn = low_back(project(context, w_attn_out) + b_attn_out)
    hidden = normalize(inputs + attn, ln1_gain, ln1_bias)
    pre = low_back(project(low(hidden), w_ffn_in) + b_ffn_in)
    act = low(0.5 * pre * (1.0 + jax.scipy.special.erf(pre * SQRT_HALF)))
    ffn = low_back(project(act, w_ffn_out) + b_ffn_out)
    final = normalize(hidden + ffn, ln2_gain, ln2_bias)
    return final * valid[..., None].astype(final.dtype)

def reference(tokens, lengths, cotangent, w_qkv, b_qv, w_attn_out, b_attn_out, ln1_gain, ln1_bias, w_ffn_in, b_ffn_in, w_ffn_out, b_ffn_out, ln2_gain, ln2_bias):
    params = tuple((item.astype(jnp.float32) for item in (w_qkv, b_qv, w_attn_out, b_attn_out, ln1_gain, ln1_bias, w_ffn_in, b_ffn_in, w_ffn_out, b_ffn_out, ln2_gain, ln2_bias)))
    group = math.gcd(SEQS, max(1, 4096 // SEQ_LEN))
    steps_count = SEQS // group
    inputs_all = tokens.astype(jnp.float32).reshape(steps_count, group, SEQ_LEN, D)
    cot_all = cotangent.astype(jnp.float32).reshape(steps_count, group, SEQ_LEN, D)
    lens_all = lengths.reshape(steps_count, group)

    def step_fn(totals, item):
        inputs, lens, cot = item
        valid = lax.broadcasted_iota(jnp.int32, (group, SEQ_LEN), 1) < lens[:, None].astype(jnp.int32)
        result, pull = jax.vjp(lambda x_in, p_in: layer(x_in, valid, p_in), inputs, params)
        grad_in, grad_params = pull(cot)
        return (jax.tree.map(jnp.add, totals, grad_params), (result.astype(jnp.bfloat16), grad_in.astype(jnp.bfloat16)))
    zeros = jax.tree.map(jnp.zeros_like, params)
    totals, (outs, grads_in) = lax.scan(step_fn, zeros, (inputs_all, lens_all, cot_all))
    return (outs.reshape(SEQS, SEQ_LEN, D), grads_in.reshape(SEQS, SEQ_LEN, D), totals[0], totals[1], totals[2], totals[3], totals[4], totals[5], totals[6], totals[7], totals[8], totals[9], totals[10], totals[11])
```

```python
import functools
import jax
import jax.numpy as jnp
from jax import lax
from jax.experimental import pallas as pl
from jax.experimental.pallas import tpu as pltpu
from jax.sharding import PartitionSpec as P

HD = 64
F32 = jnp.float32
BF = jnp.bfloat16
SQRT_HALF = 0.7071067811865476
INV_ROOT_TAU = 0.3989422804014327
MIB = 1 << 20


def params(mib):
    return pltpu.CompilerParams(vmem_limit_bytes=mib * MIB)


def dot_nn(a, b):
    return jnp.dot(a, b, preferred_element_type=F32)


def dot_nt(a, b):
    return lax.dot_general(a, b, (((1,), (1,)), ((), ())), preferred_element_type=F32)


def dot_tn(a, b):
    return lax.dot_general(a, b, (((0,), (0,)), ((), ())), preferred_element_type=F32)


def cost(flops, nbytes, trans=0):
    return pl.CostEstimate(flops=int(flops), bytes_accessed=int(nbytes), transcendentals=int(trans))


def qkv_body(x_ref, w_ref, b_ref, o_ref, w_vm, sem):
    step = pl.program_id(0)
    blocks, width = w_vm.shape[0], w_vm.shape[-1]

    def copy(n):
        return pltpu.make_async_copy(w_ref.at[:, n], w_vm.at[n], sem.at[n])

    @pl.when(step == 0)
    def _():
        for n in range(blocks):
            copy(n).start()

    x = x_ref[...]
    for n in range(blocks):
        @pl.when(step == 0)
        def _():
            copy(n).wait()

        w = w_vm[n].reshape(-1, width)
        bias = b_ref[:, n * width : (n + 1) * width]
        o_ref[:, n * width : (n + 1) * width] = (dot_nn(x, w) + bias).astype(BF)


def qkv_call(x, w1, bias, rows=256):
    slots, width = x.shape
    pieces, total, sub, _ = w1.shape
    return pl.pallas_call(
        qkv_body,
        name="qkv",
        grid=(slots // rows,),
        in_specs=[
            pl.BlockSpec((rows, width), lambda i: (i, 0)),
            pl.BlockSpec(memory_space=pl.ANY),
            pl.BlockSpec((1, 3 * width), lambda i: (0, 0)),
        ],
        out_specs=pl.BlockSpec((rows, 3 * width), lambda i: (i, 0)),
        out_shape=jax.ShapeDtypeStruct((slots, 3 * width), BF),
        scratch_shapes=[
            pltpu.VMEM((3, pieces, sub, width), BF),
            pltpu.SemaphoreType.DMA((3,)),
        ],
        compiler_params=params(48),
        cost_estimate=cost(6 * slots * width * width, 8 * slots * width + 6 * width * width),
    )(x, w1, bias)


def lanes(rows):
    return lax.broadcasted_iota(jnp.int32, (rows, 2 * HD), 1)


def split3(v):
    hi = v.astype(BF).astype(F32)
    mid = (v - hi).astype(BF).astype(F32)
    return hi, mid, v - hi - mid


def attn_fwd_body(rows, len_ref, q_ref, k_ref, v_ref, ctx_ref, qa0_ref, qa1_ref):
    slots = k_ref.shape[0]
    lane = lanes(slots)
    key_row = lax.broadcasted_iota(jnp.int32, (slots, 2 * HD), 0)
    bias = jnp.where(key_row < len_ref[0], 0.0, -1e30)
    k = k_ref[...].astype(F32)
    k_aug = []
    for h in range(2):
        own = (lane // HD) == h
        spare = (1 - h) * HD
        k_aug.append(jnp.where(own, k, jnp.where(lane == spare, bias, 0.0)).astype(BF))
    v = v_ref[...]
    lane_q = lanes(rows)

    for blk in range(slots // rows):
        sl = slice(blk * rows, (blk + 1) * rows)
        q = q_ref[sl, :].astype(F32) * 0.125
        outs = []
        for h, qa_ref in enumerate((qa0_ref, qa1_ref)):
            own = (lane_q // HD) == h
            spare = (1 - h) * HD
            qh = jnp.where(own, q, jnp.where(lane_q == spare, 1.0, 0.0))
            s = dot_nt(qh.astype(BF), k_aug[h])
            top = jnp.max(s, axis=-1, keepdims=True)
            e = jnp.exp(s - top)
            total = jnp.sum(e, axis=-1, keepdims=True)
            o = dot_nn(e.astype(BF), v) / total
            outs.append(o)
            hi, mid, lo = split3(-(top + jnp.log(total)))
            qh = jnp.where(lane_q == spare + 1, hi, qh)
            qh = jnp.where(lane_q == spare + 2, mid, qh)
            qh = jnp.where(lane_q == spare + 3, lo, qh)
            qa_ref[sl, :] = qh.astype(BF)
        ctx_ref[sl, :] = jnp.where(lane_q < HD, outs[0], outs[1]).astype(BF)


def attn_fwd_call(qkv, lengths, rows=256):
    slots, wide = qkv.shape
    width = wide // 3
    pairs = width // (2 * HD)
    col = lambda off: pl.BlockSpec((slots, 2 * HD), lambda j, ln: (0, off * pairs + j))
    out = jax.ShapeDtypeStruct((slots, width), BF)
    return pl.pallas_call(
        functools.partial(attn_fwd_body, rows),
        name="attn_fwd",
        grid_spec=pltpu.PrefetchScalarGridSpec(
            num_scalar_prefetch=1,
            grid=(pairs,),
            in_specs=[col(0), col(1), col(2)],
            out_specs=[col(0)] * 3,
        ),
        out_shape=[out, out, out],
        compiler_params=params(48),
        cost_estimate=cost(16 * slots * slots * width, 12 * slots * width, slots * slots * 2 * pairs),
    )(lengths, qkv, qkv, qkv)


def attn_bwd_body(rows, len_ref, qa0_ref, qa1_ref, k_ref, v_ref, ctx_ref, g_ref, dq_ref, dk_ref, dv_ref, sq_ref, sv_ref):
    slots = k_ref.shape[0]
    lane = lanes(slots)
    key_row = lax.broadcasted_iota(jnp.int32, (slots, 2 * HD), 0)
    bias = jnp.where(key_row < len_ref[0], 0.0, -1e30)
    k = k_ref[...].astype(F32)
    v = v_ref[...].astype(F32)
    k_low = k_ref[...]
    k_aug, v_aug = [], []
    for h in range(2):
        own = (lane // HD) == h
        spare = (1 - h) * HD
        near = (lane > spare) & (lane < spare + 4)
        ones = jnp.where(near, 1.0, 0.0)
        k_aug.append(jnp.where(own, k, jnp.where(lane == spare, bias, ones)).astype(BF))
        v_aug.append(jnp.where(own, v, ones).astype(BF))
    lane_q = lanes(rows)
    dk = [jnp.zeros((slots, 2 * HD), F32)] * 2
    dv = [jnp.zeros((slots, 2 * HD), F32)] * 2
    for blk in range(slots // rows):
        sl = slice(blk * rows, (blk + 1) * rows)
        g_low = g_ref[sl, :]
        g = g_low.astype(F32)
        prod = g * ctx_ref[sl, :].astype(F32)
        dqs = []
        for h, qa_ref in enumerate((qa0_ref, qa1_ref)):
            own = (lane_q // HD) == h
            spare = (1 - h) * HD
            delta = jnp.sum(jnp.where(own, prod, 0.0), axis=-1, keepdims=True)
            hi, mid, lo = split3(-delta)
            ga = jnp.where(own, g, 0.0)
            ga = jnp.where(lane_q == spare + 1, hi, ga)
            ga = jnp.where(lane_q == spare + 2, mid, ga)
            ga = jnp.where(lane_q == spare + 3, lo, ga).astype(BF)
            qa = qa_ref[sl, :]
            p = jnp.exp(dot_nt(k_aug[h], qa))
            ds = (p * dot_nt(v_aug[h], ga)).astype(BF)
            dv[h] = dv[h] + dot_nn(p.astype(BF), g_low)
            dk[h] = dk[h] + dot_nn(ds, qa)
            dqs.append(dot_tn(ds, k_low))
        dq_ref[sl, :] = (jnp.where(lane_q < HD, dqs[0], dqs[1]) * 0.125).astype(BF)
    dk_ref[...] = jnp.where(lane < HD, dk[0], dk[1]).astype(BF)
    dv_low = jnp.where(lane < HD, dv[0], dv[1]).astype(BF)
    dv_ref[...] = dv_low
    sq_ref[...] = jnp.sum(dq_ref[...].astype(F32), axis=0, keepdims=True)
    sv_ref[...] = jnp.sum(dv_low.astype(F32), axis=0, keepdims=True)


def attn_bwd_call(qa0, qa1, qkv, ctx, grad_ctx, lengths, rows=256):
    slots, width = ctx.shape
    pairs = width // (2 * HD)
    col = lambda off: pl.BlockSpec((slots, 2 * HD), lambda j, ln: (0, off * pairs + j))
    row = pl.BlockSpec((1, 2 * HD), lambda j, ln: (0, j))
    out = jax.ShapeDtypeStruct((slots, width), BF)
    vec = jax.ShapeDtypeStruct((1, width), F32)
    return pl.pallas_call(
        functools.partial(attn_bwd_body, rows),
        name="attn_bwd",
        grid_spec=pltpu.PrefetchScalarGridSpec(
            num_scalar_prefetch=1,
            grid=(pairs,),
            in_specs=[col(0), col(0), col(1), col(2), col(0), col(0)],
            out_specs=[col(0)] * 3 + [row] * 2,
        ),
        out_shape=[out, out, out, vec, vec],
        compiler_params=params(48),
        cost_estimate=cost(40 * slots * slots * width, 18 * slots * width, slots * slots * 2 * pairs),
    )(lengths, qa0, qa1, qkv, qkv, ctx, grad_ctx)


def norm_stats(resid):
    mean = jnp.mean(resid, axis=-1, keepdims=True)
    centred = resid - mean
    inv = lax.rsqrt(jnp.mean(centred * centred, axis=-1, keepdims=True) + 1e-5)
    return centred * inv, inv


def norm_back(u, normed, inv):
    return inv * (u - jnp.mean(u, axis=-1, keepdims=True) - normed * jnp.mean(u * normed, axis=-1, keepdims=True))


def colsum(v):
    return jnp.sum(v, axis=0, keepdims=True)


def row_body(
    len_ref, x_ref, ctx_ref, cot_ref, wa_ref, w2_ref, vec_ref, bin_ref,
    out_ref, act_ref, hid_ref, gf_ref, gp_ref, ga_ref, gc_ref, sums_ref, sbin_ref,
    wa, wi, wo, slope, sem,
):
    step = pl.program_id(0)
    rows, width = x_ref.shape
    nblk = wi.shape[0]
    copies = [pltpu.make_async_copy(wa_ref.at[:, 3], wa, sem.at[0])]
    copies += [pltpu.make_async_copy(w2_ref.at[:, n], wi.at[n], sem.at[1 + n]) for n in range(nblk)]
    copies += [pltpu.make_async_copy(w2_ref.at[:, pl.ds(nblk, 4)], wo, sem.at[1 + nblk])]

    @pl.when(step == 0)
    def _():
        for c in copies:
            c.start()
        sums_ref[...] = jnp.zeros_like(sums_ref)
        sbin_ref[...] = jnp.zeros_like(sbin_ref)

    def ready(i):
        @pl.when(step == 0)
        def _():
            copies[i].wait()

    bao, gain1, shift1, bout, gain2, shift2 = [vec_ref[i : i + 1, :] for i in range(6)]
    ready(0)
    w_ao = wa[...].reshape(width, width)
    resid1 = x_ref[...].astype(F32) + dot_nn(ctx_ref[...], w_ao) + bao
    normed1, inv1 = norm_stats(resid1)
    hidden = normed1 * gain1 + shift1
    low = hidden.astype(BF)
    hid_ref[...] = low
    acc = jnp.zeros((rows, width), F32)
    per = wo.shape[0] // nblk
    for n in range(nblk):
        ready(1 + n)
        pre = dot_nn(low, wi[n].reshape(width, width)) + bin_ref[n : n + 1, :]
        phi = 0.5 + 0.5 * lax.erf(pre * SQRT_HALF)
        slope[n] = phi + pre * (INV_ROOT_TAU * jnp.exp(-0.5 * pre * pre))
        act = (pre * phi).astype(BF)
        act_ref[:, n * width : (n + 1) * width] = act
        if n == 0:
            ready(1 + nblk)
        acc = acc + dot_nn(act, wo[n * per : (n + 1) * per].reshape(width, width))
    resid2 = hidden + acc + bout
    normed2, inv2 = norm_stats(resid2)
    row_id = lax.broadcasted_iota(jnp.int32, (rows, 1), 0) + step * rows
    valid = (row_id < len_ref[0]).astype(F32)
    out_ref[...] = ((normed2 * gain2 + shift2) * valid).astype(BF)
    gz = cot_ref[...].astype(F32) * valid
    sums_ref[0:1, :] += colsum(gz * normed2)
    sums_ref[1:2, :] += colsum(gz)
    g_resid2 = norm_back(gz * gain2, normed2, inv2)
    gf = g_resid2.astype(BF)
    gf_ref[...] = gf
    sums_ref[2:3, :] += colsum(gf.astype(F32))
    acc = g_resid2
    for n in range(nblk):
        g_act = dot_nt(gf, wo[n * per : (n + 1) * per].reshape(width, width))
        gp = (g_act * slope[n]).astype(BF)
        gp_ref[:, n * width : (n + 1) * width] = gp
        sbin_ref[n : n + 1, :] += colsum(gp.astype(F32))
        acc = acc + dot_nt(gp, wi[n].reshape(width, width))
    sums_ref[3:4, :] += colsum(acc * normed1)
    sums_ref[4:5, :] += colsum(acc)
    g_attn = norm_back(acc * gain1, normed1, inv1).astype(BF)
    ga_ref[...] = g_attn
    sums_ref[5:6, :] += colsum(g_attn.astype(F32))
    gc_ref[...] = dot_nt(g_attn, w_ao).astype(BF)


def row_call(x, ctx, cot, w1, w2, vecs, b_in, lengths, rows=256):
    slots, width = x.shape
    pieces, _, sub, _ = w1.shape
    nblk = b_in.shape[0]
    ff = nblk * width
    blk = pl.BlockSpec((rows, width), lambda i, ln: (i, 0))
    big = pl.BlockSpec((rows, ff), lambda i, ln: (i, 0))
    const = lambda r: pl.BlockSpec((r, width), lambda i, ln: (0, 0))
    anyb = pl.BlockSpec(memory_space=pl.ANY)
    o = jax.ShapeDtypeStruct((slots, width), BF)
    ob = jax.ShapeDtypeStruct((slots, ff), BF)
    return pl.pallas_call(
        row_body,
        name="row_local",
        grid_spec=pltpu.PrefetchScalarGridSpec(
            num_scalar_prefetch=1,
            grid=(slots // rows,),
            in_specs=[blk, blk, blk, anyb, anyb, const(8), const(nblk)],
            out_specs=[blk, big, blk, blk, big, blk, blk, const(8), const(nblk)],
            scratch_shapes=[
                pltpu.VMEM((pieces, sub, width), BF),
                pltpu.VMEM((nblk, pieces, sub, width), BF),
                pltpu.VMEM((pieces, 4, sub, width), BF),
                pltpu.VMEM((nblk, rows, width), F32),
                pltpu.SemaphoreType.DMA((2 + nblk,)),
            ],
        ),
        out_shape=[
            o, ob, o, o, ob, o, o,
            jax.ShapeDtypeStruct((8, width), F32),
            jax.ShapeDtypeStruct((nblk, width), F32),
        ],
        compiler_params=params(60),
        cost_estimate=cost(36 * slots * width * width, 40 * slots * width + 18 * width * width, 2 * slots * ff),
    )(lengths, x, ctx, cot, w1, w2, vecs, b_in)


def wgrad_body(a_ref, b_ref, o_ref):
    o_ref[...] = dot_tn(a_ref[...], b_ref[...]).astype(BF).reshape(o_ref.shape)


def wgrad_rows(a, b, pieces, tile=256):
    slots, m = a.shape
    width = b.shape[1]
    return pl.pallas_call(
        wgrad_body,
        name="wgrad_rows",
        grid=(m // tile,),
        in_specs=[
            pl.BlockSpec((slots, tile), lambda i: (0, i)),
            pl.BlockSpec((slots, width), lambda i: (0, 0)),
        ],
        out_specs=pl.BlockSpec((tile, width), lambda i: (i, 0)),
        out_shape=jax.ShapeDtypeStruct((m, width), BF),
        compiler_params=params(48),
        cost_estimate=cost(2 * slots * m * width, 2 * (slots * (m + width) + m * width)),
    )(a, b)


def wgrad_cols(a, b, pieces, tile=256):
    slots, m = a.shape
    n = b.shape[1] // m
    sub = m // pieces
    per = tile // sub
    return pl.pallas_call(
        wgrad_body,
        name="wgrad_cols",
        grid=(n, m // tile),
        in_specs=[
            pl.BlockSpec((slots, tile), lambda j, i: (0, i)),
            pl.BlockSpec((slots, m), lambda j, i: (0, j)),
        ],
        out_specs=pl.BlockSpec((per, 1, sub, m), lambda j, i: (i, j, 0, 0)),
        out_shape=jax.ShapeDtypeStruct((pieces, n, sub, m), BF),
        compiler_params=params(48),
        cost_estimate=cost(2 * slots * m * m * n, 2 * (slots * m * (n + 1) + m * m * n)),
    )(a, b)


def wgrad3_body(a_ref, q_ref, k_ref, v_ref, o_ref):
    for n, ref in enumerate((q_ref, k_ref, v_ref)):
        o_ref[:, n] = dot_tn(a_ref[...], ref[...]).astype(BF).reshape(o_ref.shape[0], *o_ref.shape[2:])


def wgrad3(a, dq, dk, dv, pieces, tile=256):
    slots, m = a.shape
    sub = m // pieces
    per = tile // sub
    full = pl.BlockSpec((slots, m), lambda i: (0, 0))
    return pl.pallas_call(
        wgrad3_body,
        name="wgrad3",
        grid=(m // tile,),
        in_specs=[pl.BlockSpec((slots, tile), lambda i: (0, i)), full, full, full],
        out_specs=pl.BlockSpec((per, 3, sub, m), lambda i: (i, 0, 0, 0)),
        out_shape=jax.ShapeDtypeStruct((pieces, 3, sub, m), BF),
        compiler_params=params(48),
        cost_estimate=cost(6 * slots * m * m, 14 * slots * m),
    )(a, dq, dk, dv)


def tok_body(g_ref, dq_ref, dk_ref, dv_ref, w_ref, o_ref, w_vm, sem):
    step = pl.program_id(0)
    width = g_ref.shape[1]
    copies = [pltpu.make_async_copy(w_ref.at[:, n], w_vm.at[n], sem.at[n]) for n in range(3)]

    @pl.when(step == 0)
    def _():
        for c in copies:
            c.start()

    acc = g_ref[...].astype(F32)
    for n, ref in enumerate((dq_ref, dk_ref, dv_ref)):
        @pl.when(step == 0)
        def _():
            copies[n].wait()

        acc = acc + dot_nt(ref[...], w_vm[n].reshape(width, width))
    o_ref[...] = acc.astype(BF)


def tok_call(g, dq, dk, dv, w1, rows=256):
    slots, width = g.shape
    pieces, _, sub, _ = w1.shape
    blk = pl.BlockSpec((rows, width), lambda i: (i, 0))
    return pl.pallas_call(
        tok_body,
        name="grad_tok",
        grid=(slots // rows,),
        in_specs=[blk, blk, blk, blk, pl.BlockSpec(memory_space=pl.ANY)],
        out_specs=blk,
        out_shape=jax.ShapeDtypeStruct((slots, width), BF),
        scratch_shapes=[pltpu.VMEM((3, pieces, sub, width), BF), pltpu.SemaphoreType.DMA((3,))],
        compiler_params=params(48),
        cost_estimate=cost(6 * slots * width * width, 16 * slots * width),
    )(g, dq, dk, dv, w1)


SUB = 32
BOTH = ("shard", "replica")


def mine(w, blocks, wide):
    copies = lax.axis_size("replica")
    share = w.shape[0] // copies
    part = lax.dynamic_slice_in_dim(w, lax.axis_index("replica") * share, share, 0)
    if w.shape[1] == wide:
        return part.reshape(blocks, share // blocks, wide)
    return part.reshape(share, blocks, wide).transpose(1, 0, 2)


def spread(packed):
    blocks, rows, wide = packed.shape
    full = lax.all_gather(packed, BOTH, axis=0)
    if rows == SUB:
        return full
    group = SUB // rows
    full = full.reshape(-1, group, blocks, rows, wide).transpose(0, 2, 1, 3, 4)
    return full.reshape(-1, blocks, SUB, wide)


def spread_rows(packed):
    full = lax.all_gather(packed, BOTH, axis=0)
    return full.reshape(-1, 4, SUB, packed.shape[-1])


def collect(grad, devices):
    pieces, blocks, sub, wide = grad.shape
    group = devices // pieces
    rows = sub // group
    if group > 1:
        grad = grad.reshape(pieces, blocks, group, rows, wide).transpose(0, 2, 1, 3, 4)
    grad = grad.reshape(devices, blocks, rows, wide)
    part = lax.psum_scatter(grad, BOTH, scatter_dimension=0, tiled=True)[0]
    part = lax.all_gather(part, "replica", axis=0)
    return part.transpose(0, 2, 1, 3).reshape(-1, blocks * wide).astype(F32)


def collect_rows(grad, devices):
    m, wide = grad.shape
    part = lax.psum_scatter(grad.reshape(devices, m // devices, wide), BOTH, scatter_dimension=0, tiled=True)[0]
    return lax.all_gather(part, "replica", axis=0).reshape(-1, wide).astype(F32)


def shards(
    tokens, lengths, cotangent, w_qkv, b_qv, w_attn_out, b_attn_out, ln1_gain, ln1_bias,
    w_ffn_in, b_ffn_in, w_ffn_out, b_ffn_out, ln2_gain, ln2_bias,
):
    _, slots, width = tokens.shape
    nblk = w_ffn_in.shape[1] // width
    count = lax.axis_size("shard")
    devices = count * lax.axis_size("replica")
    pieces = width // SUB
    x = tokens.reshape(slots, width)
    cot = cotangent.reshape(slots, width)

    first = jnp.concatenate([mine(w_qkv, 3, width), mine(w_attn_out, 1, width)], 0)
    w1 = spread(first)
    if w_ffn_in.shape[0] // lax.axis_size("replica") == SUB:
        w2 = spread(jnp.concatenate([mine(w_ffn_in, nblk, width), mine(w_ffn_out, 4, width)], 0))
    else:
        w2 = jnp.concatenate([spread(mine(w_ffn_in, nblk, width)), spread_rows(mine(w_ffn_out, 4, width))], 1)

    small = [b_qv, b_attn_out, ln1_gain, ln1_bias, b_ffn_in, b_ffn_out, ln2_gain, ln2_bias]
    sizes = [v.shape[0] for v in small]
    ends = [sum(sizes[: i + 1]) for i in range(len(sizes))]
    table = lax.all_gather(jnp.concatenate(small), "shard", axis=0).astype(F32)
    b_qv, bao, gain1, shift1, b_in, bout, gain2, shift2 = [
        table[:, e - s : e].reshape(-1) for s, e in zip(sizes, ends)
    ]
    bias3 = jnp.concatenate([b_qv[:width], jnp.zeros((width,), F32), b_qv[width:]]).reshape(1, -1)
    zero = jnp.zeros((width,), F32)
    vecs = jnp.stack([bao, gain1, shift1, bout, gain2, shift2, zero, zero])

    qkv = qkv_call(x, w1, bias3)
    ctx, qa0, qa1 = attn_fwd_call(qkv, lengths)
    out, act, low, gf, gp, ga, gc, sums, sbin = row_call(
        x, ctx, cot, w1, w2, vecs, b_in.reshape(nblk, width), lengths
    )
    g_wout = collect_rows(wgrad_rows(act, gf, pieces), devices)
    g_win = collect(wgrad_cols(low, gp, pieces), devices)
    g_wao = collect_rows(wgrad_rows(ctx, ga, pieces), devices)
    dq, dk, dv, sq, sv = attn_bwd_call(qa0, qa1, qkv, ctx, gc, lengths)
    g_wqkv = collect(wgrad3(x, dq, dk, dv, pieces), devices)
    g_tok = tok_call(ga, dq, dk, dv, w1)

    parts = [jnp.concatenate([sq[0], sv[0]]), sums[5], sums[3], sums[4], sbin.reshape(-1), sums[2], sums[0], sums[1]]
    table = jnp.concatenate([v.reshape(count, -1) for v in parts], 1)
    table = lax.psum(table, BOTH)
    own = lax.dynamic_index_in_dim(table, lax.axis_index("shard"), 0, keepdims=False)
    g_bqv, g_bao, g_g1, g_s1, g_bin, g_bout, g_g2, g_s2 = [own[e - s : e] for s, e in zip(sizes, ends)]
    return (
        out[None], g_tok[None], g_wqkv, g_bqv, g_wao, g_bao, g_g1, g_s1,
        g_win, g_bin, g_wout, g_bout, g_g2, g_s2,
    )


def solution(mesh):
    rows = P(("replica", "shard"), None, None)
    mat, vec = P("shard", None), P("shard")
    return jax.shard_map(
        shards,
        mesh=mesh,
        in_specs=(rows, P(("replica", "shard")), rows, mat, vec, mat, vec, vec, vec, mat, vec, mat, vec, vec, vec),
        out_specs=(rows, rows, mat, vec, mat, vec, vec, vec, mat, vec, mat, vec, vec, vec),
        check_vma=False,
    )
```

```python
import functools
import jax
import jax.numpy as jnp
from jax import lax
from jax.experimental import pallas as pl
from jax.experimental.pallas import tpu as pltpu
from jax.sharding import PartitionSpec as P

HD = 64
F32 = jnp.float32
BF = jnp.bfloat16
SQRT_HALF = 0.7071067811865476
INV_ROOT_TAU = 0.3989422804014327


def params():
    return pltpu.CompilerParams(vmem_limit_bytes=60 << 20)


def dot_nn(a, b):
    return jnp.dot(a, b, preferred_element_type=F32)


def dot_nt(a, b):
    return lax.dot_general(a, b, (((1,), (1,)), ((), ())), preferred_element_type=F32)


def dot_tn(a, b):
    return lax.dot_general(a, b, (((0,), (0,)), ((), ())), preferred_element_type=F32)


def cost(flops, nbytes, trans=0):
    return pl.CostEstimate(flops=int(flops), bytes_accessed=int(nbytes), transcendentals=int(trans))


SUB = 32
ANY = pl.BlockSpec(memory_space=pltpu.HBM)


def loads(place, bufs, lo, hi, target, sem):
    found = []
    for buf in bufs:
        for m in range(buf.shape[0]):
            i = len(found)
            found.append(pltpu.make_async_copy(buf.at[m, pl.ds(lo, hi - lo)], target(place[i]), sem.at[i]))
    return found


def start_all(copies):
    for c in copies:
        c.start()


def wait_all(copies):
    for c in copies:
        c.wait()


def qkv_body(count, place, x_ref, b_ref, *rest):
    bufs, (o_ref, w_vm, sem) = rest[:count], rest[count:]
    step = pl.program_id(0)
    blocks, width = w_vm.shape[0], w_vm.shape[-1]
    copies = loads(place, bufs, 0, blocks, lambda p: w_vm.at[:, p], sem)

    @pl.when(step == 0)
    def _():
        start_all(copies)
        wait_all(copies)

    x = x_ref[...]
    for n in range(blocks):
        w = w_vm[n].reshape(-1, width)
        bias = b_ref[:, n * width : (n + 1) * width]
        o_ref[:, n * width : (n + 1) * width] = (dot_nn(x, w) + bias).astype(BF)


def qkv_call(x, place, w1, bias, rows=256):
    slots, width = x.shape
    pieces = width // SUB
    return pl.pallas_call(
        functools.partial(qkv_body, len(w1)),
        name="qkv",
        grid_spec=pltpu.PrefetchScalarGridSpec(
            num_scalar_prefetch=1,
            grid=(slots // rows,),
            in_specs=[
                pl.BlockSpec((rows, width), lambda i, p: (i, 0)),
                pl.BlockSpec((1, 3 * width), lambda i, p: (0, 0)),
            ] + [ANY] * len(w1),
            out_specs=pl.BlockSpec((rows, 3 * width), lambda i, p: (i, 0)),
            scratch_shapes=[
                pltpu.VMEM((3, pieces, SUB, width), BF),
                pltpu.SemaphoreType.DMA((pieces,)),
            ],
        ),
        out_shape=jax.ShapeDtypeStruct((slots, 3 * width), BF),
        compiler_params=params(),
        cost_estimate=cost(6 * slots * width * width, 8 * slots * width + 6 * width * width),
    )(place, x, bias, *w1)


def lanes(rows):
    return lax.broadcasted_iota(jnp.int32, (rows, 2 * HD), 1)


def split3(v):
    hi = v.astype(BF).astype(F32)
    mid = (v - hi).astype(BF).astype(F32)
    return hi, mid, v - hi - mid


def attn_fwd_body(rows, len_ref, q_ref, k_ref, v_ref, *rest):
    ctx_ref, qa0_ref, qa1_ref = rest[-3:]
    slots = k_ref.shape[0]
    lane = lanes(slots)
    key_row = lax.broadcasted_iota(jnp.int32, (slots, 2 * HD), 0)
    bias = jnp.where(key_row < len_ref[0], 0.0, -1e30)
    k = k_ref[...].astype(F32)
    k_aug = []
    for h in range(2):
        own = (lane // HD) == h
        spare = (1 - h) * HD
        k_aug.append(jnp.where(own, k, jnp.where(lane == spare, bias, 0.0)).astype(BF))
    v = v_ref[...]
    lane_q = lanes(rows)

    for blk in range(slots // rows):
        sl = slice(blk * rows, (blk + 1) * rows)
        q = q_ref[sl, :].astype(F32) * 0.125
        outs = []
        for h, qa_ref in enumerate((qa0_ref, qa1_ref)):
            own = (lane_q // HD) == h
            spare = (1 - h) * HD
            qh = jnp.where(own, q, jnp.where(lane_q == spare, 1.0, 0.0))
            s = dot_nt(qh.astype(BF), k_aug[h])
            top = jnp.max(s, axis=-1, keepdims=True)
            e = jnp.exp(s - top)
            total = jnp.sum(e, axis=-1, keepdims=True)
            o = dot_nn(e.astype(BF), v) / total
            outs.append(o)
            hi, mid, lo = split3(-(top + jnp.log(total)))
            qh = jnp.where(lane_q == spare + 1, hi, qh)
            qh = jnp.where(lane_q == spare + 2, mid, qh)
            qh = jnp.where(lane_q == spare + 3, lo, qh)
            qa_ref[sl, :] = qh.astype(BF)
        ctx_ref[sl, :] = jnp.where(lane_q < HD, outs[0], outs[1]).astype(BF)


def attn_fwd_call(qkv, lengths, part, parts, before, rows=256):
    slots, wide = qkv.shape
    width = wide // 3
    pairs = width // (2 * HD)
    each = pairs // parts
    col = lambda off: pl.BlockSpec((slots, 2 * HD), lambda j, ln: (0, off * pairs + part * each + j))
    out = jax.ShapeDtypeStruct((slots, width), BF)
    extra = list(before or ())
    return pl.pallas_call(
        functools.partial(attn_fwd_body, rows),
        name=f"attn_fwd{part}",
        grid_spec=pltpu.PrefetchScalarGridSpec(
            num_scalar_prefetch=1,
            grid=(each,),
            in_specs=[col(0), col(1), col(2)] + [ANY] * len(extra),
            out_specs=[col(0)] * 3,
        ),
        out_shape=[out, out, out],
        input_output_aliases={4 + i: i for i in range(3)} if before else {},
        compiler_params=params(),
        cost_estimate=cost(
            16 * slots * slots * width / parts, 12 * slots * width / parts, slots * slots * 2 * each
        ),
    )(lengths, qkv, qkv, qkv, *extra)


def attn_bwd_body(rows, len_ref, qa0_ref, qa1_ref, k_ref, v_ref, ctx_ref, g_ref, *rest):
    dq_ref, dk_ref, dv_ref, sq_ref, sv_ref = rest[-5:]
    slots = k_ref.shape[0]
    lane = lanes(slots)
    key_row = lax.broadcasted_iota(jnp.int32, (slots, 2 * HD), 0)
    bias = jnp.where(key_row < len_ref[0], 0.0, -1e30)
    k = k_ref[...].astype(F32)
    v = v_ref[...].astype(F32)
    k_low = k_ref[...]
    k_aug, v_aug = [], []
    for h in range(2):
        own = (lane // HD) == h
        spare = (1 - h) * HD
        near = (lane > spare) & (lane < spare + 4)
        ones = jnp.where(near, 1.0, 0.0)
        k_aug.append(jnp.where(own, k, jnp.where(lane == spare, bias, ones)).astype(BF))
        v_aug.append(jnp.where(own, v, ones).astype(BF))
    lane_q = lanes(rows)
    dk = [jnp.zeros((slots, 2 * HD), F32)] * 2
    dv = [jnp.zeros((slots, 2 * HD), F32)] * 2
    for blk in range(slots // rows):
        sl = slice(blk * rows, (blk + 1) * rows)
        g_low = g_ref[sl, :]
        g = g_low.astype(F32)
        prod = g * ctx_ref[sl, :].astype(F32)
        dqs = []
        for h, qa_ref in enumerate((qa0_ref, qa1_ref)):
            own = (lane_q // HD) == h
            spare = (1 - h) * HD
            delta = jnp.sum(jnp.where(own, prod, 0.0), axis=-1, keepdims=True)
            hi, mid, lo = split3(-delta)
            ga = jnp.where(own, g, 0.0)
            ga = jnp.where(lane_q == spare + 1, hi, ga)
            ga = jnp.where(lane_q == spare + 2, mid, ga)
            ga = jnp.where(lane_q == spare + 3, lo, ga).astype(BF)
            qa = qa_ref[sl, :]
            p = jnp.exp(dot_nt(k_aug[h], qa))
            ds = (p * dot_nt(v_aug[h], ga)).astype(BF)
            dv[h] = dv[h] + dot_nn(p.astype(BF), g_low)
            dk[h] = dk[h] + dot_nn(ds, qa)
            dqs.append(dot_tn(ds, k_low))
        dq_ref[sl, :] = (jnp.where(lane_q < HD, dqs[0], dqs[1]) * 0.125).astype(BF)
    dk_ref[...] = jnp.where(lane < HD, dk[0], dk[1]).astype(BF)
    dv_low = jnp.where(lane < HD, dv[0], dv[1]).astype(BF)
    dv_ref[...] = dv_low
    sq_ref[...] = jnp.sum(dq_ref[...].astype(F32), axis=0, keepdims=True)
    sv_ref[...] = jnp.sum(dv_low.astype(F32), axis=0, keepdims=True)


def attn_bwd_call(qa0, qa1, qkv, ctx, grad_ctx, lengths, part, parts, before, rows=256):
    slots, width = ctx.shape
    pairs = width // (2 * HD)
    each = pairs // parts
    col = lambda off: pl.BlockSpec((slots, 2 * HD), lambda j, ln: (0, off * pairs + part * each + j))
    row = pl.BlockSpec((1, 2 * HD), lambda j, ln: (0, part * each + j))
    out = jax.ShapeDtypeStruct((slots, width), BF)
    vec = jax.ShapeDtypeStruct((1, width), F32)
    extra = list(before or ())
    return pl.pallas_call(
        functools.partial(attn_bwd_body, rows),
        name=f"attn_bwd{part}",
        grid_spec=pltpu.PrefetchScalarGridSpec(
            num_scalar_prefetch=1,
            grid=(each,),
            in_specs=[col(0), col(0), col(1), col(2), col(0), col(0)] + [ANY] * len(extra),
            out_specs=[col(0)] * 3 + [row] * 2,
        ),
        out_shape=[out, out, out, vec, vec],
        input_output_aliases={7 + i: i for i in range(5)} if before else {},
        compiler_params=params(),
        cost_estimate=cost(
            40 * slots * slots * width / parts, 18 * slots * width / parts, slots * slots * 2 * each
        ),
    )(lengths, qa0, qa1, qkv, qkv, ctx, grad_ctx, *extra)


def norm_stats(resid):
    mean = jnp.mean(resid, axis=-1, keepdims=True)
    centred = resid - mean
    inv = lax.rsqrt(jnp.mean(centred * centred, axis=-1, keepdims=True) + 1e-5)
    return centred * inv, inv


def norm_back(u, normed, inv):
    return inv * (u - jnp.mean(u, axis=-1, keepdims=True) - normed * jnp.mean(u * normed, axis=-1, keepdims=True))


def colsum(v):
    return jnp.sum(v, axis=0, keepdims=True)


def row_body(n2, len_ref, place, x_ref, ctx_ref, cot_ref, vec_ref, bin_ref, *rest):
    b2 = rest[:n2]
    (
        out_ref, act_ref, hid_ref, gf_ref, gp_ref, ga_ref, gc_ref, sums_ref, sbin_ref,
        wa, wi, wo, slope, sem,
    ) = rest[n2:]
    step = pl.program_id(0)
    rows, width = x_ref.shape
    nblk = wi.shape[0]
    copies = [
        loads(place, b2, 0, 1, lambda p: wa.at[pl.ds(p, 1)], sem.at[0]),
        loads(place, b2, 1, 1 + nblk, lambda p: wi.at[:, p], sem.at[1]),
        loads(place, b2, 1 + nblk, 5 + nblk, lambda p: wo.at[p], sem.at[2]),
    ]

    @pl.when(step == 0)
    def _():
        for c in copies:
            start_all(c)
        sums_ref[...] = jnp.zeros_like(sums_ref)
        sbin_ref[...] = jnp.zeros_like(sbin_ref)

    def ready(i):
        @pl.when(step == 0)
        def _():
            wait_all(copies[i])

    bao, gain1, shift1, bout, gain2, shift2 = [vec_ref[i : i + 1, :] for i in range(6)]
    ready(0)
    w_ao = wa[...].reshape(width, width)
    resid1 = x_ref[...].astype(F32) + dot_nn(ctx_ref[...], w_ao) + bao
    normed1, inv1 = norm_stats(resid1)
    hidden = normed1 * gain1 + shift1
    low = hidden.astype(BF)
    hid_ref[...] = low
    acc = jnp.zeros((rows, width), F32)
    per = wo.shape[0] // nblk
    ready(1)
    for n in range(nblk):
        pre = dot_nn(low, wi[n].reshape(width, width)) + bin_ref[n : n + 1, :]
        phi = 0.5 + 0.5 * lax.erf(pre * SQRT_HALF)
        slope[n] = phi + pre * (INV_ROOT_TAU * jnp.exp(-0.5 * pre * pre))
        act = (pre * phi).astype(BF)
        act_ref[:, n * width : (n + 1) * width] = act
        if n == 0:
            ready(2)
        acc = acc + dot_nn(act, wo[n * per : (n + 1) * per].reshape(width, width))
    resid2 = hidden + acc + bout
    normed2, inv2 = norm_stats(resid2)
    row_id = lax.broadcasted_iota(jnp.int32, (rows, 1), 0) + step * rows
    valid = (row_id < len_ref[0]).astype(F32)
    out_ref[...] = ((normed2 * gain2 + shift2) * valid).astype(BF)
    gz = cot_ref[...].astype(F32) * valid
    sums_ref[0:1, :] += colsum(gz * normed2)
    sums_ref[1:2, :] += colsum(gz)
    g_resid2 = norm_back(gz * gain2, normed2, inv2)
    gf = g_resid2.astype(BF)
    gf_ref[...] = gf
    sums_ref[2:3, :] += colsum(gf.astype(F32))
    acc = g_resid2
    for n in range(nblk):
        g_act = dot_nt(gf, wo[n * per : (n + 1) * per].reshape(width, width))
        gp = (g_act * slope[n]).astype(BF)
        gp_ref[:, n * width : (n + 1) * width] = gp
        sbin_ref[n : n + 1, :] += colsum(gp.astype(F32))
        acc = acc + dot_nt(gp, wi[n].reshape(width, width))
    sums_ref[3:4, :] += colsum(acc * normed1)
    sums_ref[4:5, :] += colsum(acc)
    g_attn = norm_back(acc * gain1, normed1, inv1).astype(BF)
    ga_ref[...] = g_attn
    sums_ref[5:6, :] += colsum(g_attn.astype(F32))
    gc_ref[...] = dot_nt(g_attn, w_ao).astype(BF)


def row_call(x, ctx, cot, place, w2, vecs, b_in, lengths, rows=256):
    slots, width = x.shape
    pieces, sub = width // SUB, SUB
    nblk = b_in.shape[0]
    ff = nblk * width
    blk = pl.BlockSpec((rows, width), lambda i, ln, p: (i, 0))
    big = pl.BlockSpec((rows, ff), lambda i, ln, p: (i, 0))
    const = lambda r: pl.BlockSpec((r, width), lambda i, ln, p: (0, 0))
    o = jax.ShapeDtypeStruct((slots, width), BF)
    ob = jax.ShapeDtypeStruct((slots, ff), BF)
    return pl.pallas_call(
        functools.partial(row_body, len(w2)),
        name="row_local",
        grid_spec=pltpu.PrefetchScalarGridSpec(
            num_scalar_prefetch=2,
            grid=(slots // rows,),
            in_specs=[blk, blk, blk, const(8), const(nblk)] + [ANY] * len(w2),
            out_specs=[blk, big, blk, blk, big, blk, blk, const(8), const(nblk)],
            scratch_shapes=[
                pltpu.VMEM((pieces, sub, width), BF),
                pltpu.VMEM((nblk, pieces, sub, width), BF),
                pltpu.VMEM((pieces, 4, sub, width), BF),
                pltpu.VMEM((nblk, rows, width), F32),
                pltpu.SemaphoreType.DMA((3, pieces)),
            ],
        ),
        out_shape=[
            o, ob, o, o, ob, o, o,
            jax.ShapeDtypeStruct((8, width), F32),
            jax.ShapeDtypeStruct((nblk, width), F32),
        ],
        compiler_params=params(),
        cost_estimate=cost(36 * slots * width * width, 40 * slots * width + 18 * width * width, 2 * slots * ff),
    )(lengths, place, x, ctx, cot, vecs, b_in, *w2)


def halves(core, value, group, keep_ref, send_ref):
    value = value.reshape(-1, 2, group, SUB, value.shape[-1])
    even, odd = value[:, 0], value[:, 1]
    shape = keep_ref.shape

    @pl.when(core == 0)
    def _():
        keep_ref[...] = even.reshape(shape)
        send_ref[...] = odd.reshape(shape)

    @pl.when(core != 0)
    def _():
        keep_ref[...] = odd.reshape(shape)
        send_ref[...] = even.reshape(shape)


def wgrad_body(group, core, a_ref, b_ref, keep_ref, send_ref):
    halves(core[0], dot_tn(a_ref[...], b_ref[...]).astype(BF), group, keep_ref, send_ref)


def wgrad_call(name, core, a, b, by_rows, tile=256):
    slots, m = a.shape
    width = a.shape[1] if not by_rows else b.shape[1]
    blocks = m // width if by_rows else b.shape[1] // m
    pieces = width // SUB
    if by_rows:
        group, grid = blocks, (1, m // tile)
        block = (tile // (2 * SUB * blocks), blocks, SUB, width)
        where = lambda j, i, c: (i, 0, 0, 0)
    else:
        group, grid = 1, (blocks, m // tile)
        block = (tile // (2 * SUB), 1, SUB, width)
        where = lambda j, i, c: (i, j, 0, 0)
    out = jax.ShapeDtypeStruct((pieces // 2, blocks, SUB, width), BF)
    return pl.pallas_call(
        functools.partial(wgrad_body, group),
        name=name,
        grid_spec=pltpu.PrefetchScalarGridSpec(
            num_scalar_prefetch=1,
            grid=grid,
            in_specs=[
                pl.BlockSpec((slots, tile), lambda j, i, c: (0, i)),
                pl.BlockSpec((slots, width), lambda j, i, c: (0, j)),
            ],
            out_specs=[pl.BlockSpec(block, where)] * 2,
        ),
        out_shape=[out, out],
        compiler_params=params(),
        cost_estimate=cost(2 * slots * m * b.shape[1], 2 * (slots * (m + b.shape[1]) + m * b.shape[1])),
    )(core, a, b)


def wgrad3_body(core, a_ref, q_ref, k_ref, v_ref, keep_ref, send_ref):
    for n, ref in enumerate((q_ref, k_ref, v_ref)):
        value = dot_tn(a_ref[...], ref[...]).astype(BF)
        halves(core[0], value, 1, keep_ref.at[:, pl.ds(n, 1)], send_ref.at[:, pl.ds(n, 1)])


def wgrad3(core, a, dq, dk, dv, tile=256):
    slots, m = a.shape
    full = pl.BlockSpec((slots, m), lambda i, c: (0, 0))
    block = pl.BlockSpec((tile // (2 * SUB), 3, SUB, m), lambda i, c: (i, 0, 0, 0))
    out = jax.ShapeDtypeStruct((m // SUB // 2, 3, SUB, m), BF)
    return pl.pallas_call(
        wgrad3_body,
        name="wgrad_qkv",
        grid_spec=pltpu.PrefetchScalarGridSpec(
            num_scalar_prefetch=1,
            grid=(m // tile,),
            in_specs=[pl.BlockSpec((slots, tile), lambda i, c: (0, i)), full, full, full],
            out_specs=[block, block],
        ),
        out_shape=[out, out],
        compiler_params=params(),
        cost_estimate=cost(6 * slots * m * m, 14 * slots * m),
    )(core, a, dq, dk, dv)


def tok_body(count, place, g_ref, dq_ref, dk_ref, dv_ref, *rest):
    bufs, (o_ref, w_vm, sem) = rest[:count], rest[count:]
    step = pl.program_id(0)
    width = g_ref.shape[1]
    copies = loads(place, bufs, 0, 3, lambda p: w_vm.at[:, p], sem)

    @pl.when(step == 0)
    def _():
        start_all(copies)
        wait_all(copies)

    acc = g_ref[...].astype(F32)
    for n, ref in enumerate((dq_ref, dk_ref, dv_ref)):
        acc = acc + dot_nt(ref[...], w_vm[n].reshape(width, width))
    o_ref[...] = acc.astype(BF)


def tok_call(g, dq, dk, dv, place, w1, rows=256):
    slots, width = g.shape
    pieces = width // SUB
    blk = pl.BlockSpec((rows, width), lambda i, p: (i, 0))
    return pl.pallas_call(
        functools.partial(tok_body, len(w1)),
        name="grad_tok",
        grid_spec=pltpu.PrefetchScalarGridSpec(
            num_scalar_prefetch=1,
            grid=(slots // rows,),
            in_specs=[blk, blk, blk, blk] + [ANY] * len(w1),
            out_specs=blk,
            scratch_shapes=[pltpu.VMEM((3, pieces, SUB, width), BF), pltpu.SemaphoreType.DMA((pieces,))],
        ),
        out_shape=jax.ShapeDtypeStruct((slots, width), BF),
        compiler_params=params(),
        cost_estimate=cost(6 * slots * width * width, 16 * slots * width),
    )(place, g, dq, dk, dv, *w1)


def total(*terms):
    acc = terms[0].astype(F32)
    for t in terms[1:]:
        acc = acc + t.astype(F32)
    return acc.astype(BF)


def add1_body(count, here, *refs):
    ins, outs = refs[: 8 * count], refs[8 * count :]
    for view in range(4):
        n0 = 0
        for i in range(count):
            a, b = ins[8 * i + 2 * view], ins[8 * i + 2 * view + 1]
            n = a.shape[3]
            outs[view][0, n0 : n0 + n] = total(a[0, 0, 0], b[0, 0, 0])
            n0 += n


def add1(here, pairs):
    width = pairs[0][0].shape[-1]
    views = []
    for half, own in ((0, 0), (0, 1), (1, 0), (1, 1)):
        def where(t, h, half=half, own=own):
            z, j = 2 * half + t // 2, t % 2
            if half == 0:
                return (z, j, h[0] if own else 1 - h[0], 0, 0, 0)
            return (z, h[1] if own else 1 - h[1], j, 0, 0, 0)
        views.append(where)
    specs, args, blocks = [], [], 0
    for keep, got in pairs:
        n = keep.shape[1]
        blocks += n
        for where in views:
            for arr in (keep, got):
                specs.append(pl.BlockSpec((1, 1, 1, n, SUB, width), where))
                args.append(arr.reshape(4, 2, 2, n, SUB, width))
    out = jax.ShapeDtypeStruct((4, blocks, SUB, width), BF)
    return pl.pallas_call(
        functools.partial(add1_body, len(pairs)),
        name="add_core",
        grid_spec=pltpu.PrefetchScalarGridSpec(
            num_scalar_prefetch=1,
            grid=(4,),
            in_specs=specs,
            out_specs=[pl.BlockSpec((1, blocks, SUB, width), lambda t, h: (t, 0, 0, 0))] * 4,
        ),
        out_shape=[out] * 4,
        compiler_params=params(),
        cost_estimate=cost(16 * blocks * SUB * width, 96 * blocks * SUB * width),
    )(here, *args)


def add2_body(here, *refs):
    ins, outs = refs[:8], refs[-4:]
    for view in range(4):
        outs[view][0] = total(ins[2 * view][0, 0], ins[2 * view + 1][0, 0])


def add2(here, first, second):
    _, blocks, _, width = first[0].shape
    specs, args = [], []
    for axis, pair in ((1, first), (0, second)):
        for own in (0, 1):
            for arr in pair:
                specs.append(pl.BlockSpec(
                    (1, 1, blocks, SUB, width),
                    lambda t, h, axis=axis, own=own: (t, h[axis] if own else 1 - h[axis], 0, 0, 0),
                ))
                args.append(arr.reshape(2, 2, blocks, SUB, width))
    out = jax.ShapeDtypeStruct((2, blocks, SUB, width), BF)
    return pl.pallas_call(
        add2_body,
        name="add_plane",
        grid_spec=pltpu.PrefetchScalarGridSpec(
            num_scalar_prefetch=1,
            grid=(2,),
            in_specs=specs,
            out_specs=[pl.BlockSpec((1, blocks, SUB, width), lambda t, h: (t, 0, 0, 0))] * 4,
        ),
        out_shape=[out] * 4,
        compiler_params=params(),
        cost_estimate=cost(8 * blocks * SUB * width, 48 * blocks * SUB * width),
    )(here, *args)


def add3_body(here, ak, ag, bk, bg, *outs):
    for k, out in enumerate(outs):
        to = lax.rem(here[2] + k, 4)
        spot = lax.rem(to, 2)

        @pl.when(to < 2)
        def _():
            out[0] = total(ak[spot], ag[spot])

        @pl.when(to >= 2)
        def _():
            out[0] = total(bk[spot], bg[spot])


def add3(here, first, second):
    _, blocks, _, width = first[0].shape
    full = pl.BlockSpec((2, blocks, SUB, width), lambda t, h: (0, 0, 0, 0))
    one = pl.BlockSpec((1, blocks, SUB, width), lambda t, h: (0, 0, 0, 0))
    return pl.pallas_call(
        add3_body,
        name="add_z",
        grid_spec=pltpu.PrefetchScalarGridSpec(
            num_scalar_prefetch=1, grid=(1,), in_specs=[full] * 4, out_specs=[one] * 4,
        ),
        out_shape=[jax.ShapeDtypeStruct((1, blocks, SUB, width), BF)] * 4,
        compiler_params=params(),
        cost_estimate=cost(4 * blocks * SUB * width, 24 * blocks * SUB * width),
    )(here, *first, *second)


def add4_body(*refs):
    ins, out = refs[:-1], refs[-1]
    n0 = 0
    for i in range(0, len(ins), 4):
        n = ins[i].shape[1]
        out[:, n0 : n0 + n] = total(*[r[...] for r in ins[i : i + 4]])
        n0 += n


def add4(*groups):
    spec = lambda shape: pl.BlockSpec(shape, lambda t: (0,) * len(shape))
    _, _, sub, width = groups[0][0].shape
    shape = (1, sum(g[0].shape[1] for g in groups), sub, width)
    parts = [v for g in groups for v in g]
    size = shape[1] * sub * width
    return pl.pallas_call(
        add4_body,
        name="add_last",
        grid=(1,),
        in_specs=[spec(v.shape) for v in parts],
        out_specs=spec(shape),
        out_shape=jax.ShapeDtypeStruct(shape, BF),
        compiler_params=params(),
        cost_estimate=cost(3 * size, 10 * size),
    )(*parts)


def final_body(kinds, here, own, core, over_x, both, *outs):
    mine_at = 2 * here[0] + here[3]
    for flip, ref in enumerate((own, core, over_x, both)):
        share = jnp.bitwise_xor(mine_at, flip)
        n0 = 0
        for (blocks, by_rows), out in zip(kinds, outs):
            width = ref.shape[-1]
            for n in range(blocks):
                value = ref[0, n0 + n].astype(F32)
                if by_rows:
                    out[pl.ds(pl.multiple_of(share * blocks * SUB, SUB) + n * SUB, SUB), :] = value
                else:
                    out[pl.ds(pl.multiple_of(share * SUB, SUB), SUB), n * width : (n + 1) * width] = value
            n0 += blocks


def final_call(here, parts, kinds):
    shape = parts[0].shape
    width = shape[-1]
    shapes = [
        (4 * blocks * SUB, width) if by_rows else (4 * SUB, blocks * width) for blocks, by_rows in kinds
    ]
    return pl.pallas_call(
        functools.partial(final_body, kinds),
        name="final",
        grid_spec=pltpu.PrefetchScalarGridSpec(
            num_scalar_prefetch=1,
            grid=(1,),
            in_specs=[pl.BlockSpec(shape, lambda t, h: (0, 0, 0, 0))] * 4,
            out_specs=[pl.BlockSpec(sh, lambda t, h: (0, 0)) for sh in shapes],
        ),
        out_shape=[jax.ShapeDtypeStruct(sh, F32) for sh in shapes],
        compiler_params=params(),
        cost_estimate=cost(1, 24 * parts[0].size),
    )(here, *parts)


BOTH = ("shard", "replica")
AXES = ("replica", "shard")


def table(fn):
    pairs = []
    for r in range(4):
        for s in range(8):
            x, y, z, c = fn(r // 2, s % 2, s // 2, r % 2)
            pairs.append((r * 8 + s, (x * 2 + c) * 8 + z * 2 + y))
    return pairs


TO_CORE = table(lambda x, y, z, c: (x, y, z, 1 - c))
TO_X = table(lambda x, y, z, c: (1 - x, y, z, c))
TO_XCORE = table(lambda x, y, z, c: (1 - x, y, z, 1 - c))
TO_Y = table(lambda x, y, z, c: (x, 1 - y, z, c))
TO_Z = [table(lambda x, y, z, c, k=k: (x, y, (z + k) % 4, c)) for k in range(4)]


def move(v, pairs):
    return lax.ppermute(v, AXES, pairs)


def regular():
    return lax.axis_size("shard") == 8 and lax.axis_size("replica") == 4


def place_of():
    r, s = lax.axis_index("replica"), lax.axis_index("shard")
    return r // 2, s % 2, s // 2, r % 2


def pack_body(count, share, *refs):
    ins, smalls, outs = refs[:count], refs[count:-2], refs[-2:]
    out, line = outs
    width = out.shape[-1]
    n0 = 0
    for ref in ins:
        rows, cols = ref.shape
        if rows > SUB:
            out[0, n0 : n0 + rows // SUB] = ref[...].reshape(rows // SUB, SUB, width)
            n0 += rows // SUB
        else:
            for n in range(cols // width):
                out[0, n0 + n] = ref[:, n * width : (n + 1) * width]
            n0 += cols // width
    n0 = 0
    for ref in smalls:
        line[:, n0 : n0 + ref.shape[1]] = ref[...]
        n0 += ref.shape[1]


def pack(share, mats, smalls, width):
    shapes = [(m.shape[0] // 4, m.shape[1]) for m in mats]
    blocks = sum(r * c for r, c in shapes) // (SUB * width)
    smalls = [v.reshape(1, -1) for v in smalls]
    line = (1, sum(v.shape[1] for v in smalls))
    return pl.pallas_call(
        functools.partial(pack_body, len(mats)),
        name="pack",
        grid_spec=pltpu.PrefetchScalarGridSpec(
            num_scalar_prefetch=1,
            grid=(1,),
            in_specs=[pl.BlockSpec(sh, lambda t, r: (r[0], 0)) for sh in shapes]
            + [pl.BlockSpec(v.shape, lambda t, r: (0, 0)) for v in smalls],
            out_specs=[
                pl.BlockSpec((1, blocks, SUB, width), lambda t, r: (0, 0, 0, 0)),
                pl.BlockSpec(line, lambda t, r: (0, 0)),
            ],
        ),
        out_shape=[jax.ShapeDtypeStruct((1, blocks, SUB, width), BF), jax.ShapeDtypeStruct(line, BF)],
        compiler_params=params(),
        cost_estimate=cost(1, 4 * blocks * SUB * width),
    )(share, *mats, *smalls)


def after(v, *deps):
    return lax.optimization_barrier((v,) + deps)[0]


def gather_z(own):
    near = [move(own, TO_Z[k]) for k in (1, 2, 3)]
    return jnp.concatenate([own, near[0]], 0), jnp.concatenate([near[1], near[2]], 0)


def to_core(bufs):
    return [move(v, TO_CORE) for v in bufs]


def tied(*groups):
    flat = lax.optimization_barrier([v for g in groups for v in g])
    out = []
    for g in groups:
        out.append(flat[: len(g)])
        flat = flat[len(g) :]
    return out


def gather_places(order):
    x, y, z, c = place_of()
    spots = []
    for fc in (0, 1):
        for k0, fx, fy in order:
            for k in (k0, k0 + 1):
                spots.append((((z - k) % 4) * 2 + (y ^ fy)) * 4 + (x ^ fx) * 2 + (c ^ fc))
    return jnp.stack(spots).astype(jnp.int32)


def spread(w, blocks, wide):
    full = lax.all_gather(w, "shard", axis=0, tiled=True)
    if full.shape[1] == wide:
        return full.reshape(-1, blocks, SUB, wide)
    return full.reshape(-1, SUB, blocks, wide).transpose(0, 2, 1, 3)


def sum_core(here, pairs):
    a_send, a_keep, b_send, b_keep = add1(here, pairs)
    return (a_keep, move(a_send, TO_X)), (b_keep, move(b_send, TO_Y))


def sum_plane(here, first, second):
    a_send, a_keep, b_send, b_keep = add2(here, first, second)
    return (a_keep, move(a_send, TO_Y)), (b_keep, move(b_send, TO_X))


def sum_z(here, first, second):
    own, *sends = add3(here, first, second)
    return [own] + [move(v, TO_Z[k + 1]) for k, v in enumerate(sends)]


def copies_of(*groups):
    own = add4(*groups)
    return own, move(own, TO_CORE), move(own, TO_X), move(own, TO_XCORE)


def small_gather(plane):
    x, y, z, c = place_of()
    rows = jnp.concatenate([plane] + [move(plane, TO_Z[k]) for k in (1, 2, 3)], 0)
    spots = jnp.stack([((z - k) % 4) * 2 + (y ^ f) for k in range(4) for f in (0, 1)])
    pick = (jnp.arange(8)[:, None] == spots[None, :]).astype(BF)
    return dot_nn(pick, rows)


def small_sum(rows):
    s = lax.axis_index("shard")
    if not regular():
        return lax.dynamic_index_in_dim(lax.psum(rows, BOTH), s, 0, keepdims=False)
    x, y, z, c = place_of()
    rows = rows + move(rows, TO_CORE)
    rows = rows + move(rows, TO_X)
    rows = rows.reshape(4, 2, -1)
    pick = lambda v, i, axis: lax.dynamic_index_in_dim(v, i, axis, keepdims=False)
    rows = pick(rows, y, 1) + move(pick(rows, 1 - y, 1), TO_Y)
    own = pick(rows, z, 0)
    for k in (1, 2, 3):
        own = own + move(pick(rows, (z + k) % 4, 0)[None], TO_Z[k])[0]
    return own


def reduce_any(keep, send, by_rows):
    half, blocks, _, wide = keep.shape
    full = jnp.stack([keep, send], 1).reshape(2 * half, blocks, SUB, wide)
    full = full.reshape(-1, wide) if by_rows else full.transpose(0, 2, 1, 3).reshape(-1, blocks * wide)
    part = lax.psum_scatter(full, "shard", scatter_dimension=0, tiled=True)
    return lax.psum(part, "replica").astype(F32)


def shards(
    tokens, lengths, cotangent, w_qkv, b_qv, w_attn_out, b_attn_out, ln1_gain, ln1_bias,
    w_ffn_in, b_ffn_in, w_ffn_out, b_ffn_out, ln2_gain, ln2_bias,
):
    _, slots, width = tokens.shape
    nblk = w_ffn_in.shape[1] // width
    count = lax.axis_size("shard")
    x = tokens.reshape(slots, width)
    cot = cotangent.reshape(slots, width)
    small = [b_qv, b_attn_out, ln1_gain, ln1_bias, b_ffn_in, b_ffn_out, ln2_gain, ln2_bias]
    sizes = [v.shape[0] for v in small]
    ends = [sum(sizes[: i + 1]) for i in range(len(sizes))]

    if regular():
        share = lax.axis_index("replica").reshape(1).astype(jnp.int32)
        first, line = pack(share, [w_qkv], small, width)
        plane = jnp.concatenate([line, move(line, TO_Y)], 0)
        a1, b1 = gather_z(first)
        rows = small_gather(after(plane, a1, b1))
        second, _ = pack(share, [w_attn_out, w_ffn_in, w_ffn_out], [b_qv], width)
        second = after(second, a1, b1, rows)
        near = move(second, TO_Z[1])
        plane = [move(a1, TO_Y), move(b1, TO_X), move(a1, TO_X), move(b1, TO_Y)]
        first = [a1, b1]
        cores = to_core(first)
        plane, cores = tied(plane, cores)
        last = [move(plane[0], TO_X), move(plane[1], TO_Y)]
        more = to_core(plane)
        last, more, [near, second] = tied(last, more, [near, second])
        w1 = [*first, *plane, *last, *cores, *more, *to_core(last)]
        far = [move(second, TO_Z[k]) for k in (2, 3)]
        a2 = jnp.concatenate([second, near], 0)
        ya2, xa2 = move(a2, TO_Y), move(a2, TO_X)
        place = gather_places(((0, 0, 0), (2, 0, 0), (0, 0, 1), (2, 1, 0), (0, 1, 0), (2, 0, 1), (0, 1, 1), (2, 1, 1)))
        place2 = gather_places(((0, 0, 0), (0, 0, 1), (0, 1, 0), (2, 0, 0), (2, 1, 0), (2, 0, 1), (0, 1, 1), (2, 1, 1)))
        here = jnp.stack(place_of()).astype(jnp.int32)
    else:
        w1 = [spread(w_qkv, 3, width)]
        w2 = [spread(w_attn_out, 1, width), spread(w_ffn_in, nblk, width), spread(w_ffn_out, 4, width)]
        w2 = [jnp.concatenate(w2, 1)]
        place = place2 = jnp.arange(width // SUB, dtype=jnp.int32)
        here = jnp.zeros((4,), jnp.int32)
    core = here[3:]

    if not regular():
        rows = lax.all_gather(jnp.concatenate(small), "shard", axis=0).astype(F32)
    b_qv, bao, gain1, shift1, b_in, bout, gain2, shift2 = [
        rows[:, e - s : e].reshape(-1) for s, e in zip(sizes, ends)
    ]
    bias3 = jnp.concatenate([b_qv[:width], jnp.zeros((width,), F32), b_qv[width:]]).reshape(1, -1)
    zero = jnp.zeros((width,), F32)
    vecs = jnp.stack([bao, gain1, shift1, bout, gain2, shift2, zero, zero])

    qkv = qkv_call(x, place, w1, bias3)
    parts = 4
    fwd = lambda i, state: attn_fwd_call(qkv, lengths, i, parts, state)
    state = fwd(0, None)
    if regular():
        far, [ya2, xa2], state = tied(far, [ya2, xa2], state)
        b2 = jnp.concatenate(far, 0)
        xb2, yb2 = move(b2, TO_X), move(b2, TO_Y)
        cores = to_core([a2, ya2, xa2])
        state = fwd(1, state)
        cores, state = tied(cores, state)
        state = fwd(2, state)
        [xb2, yb2], state = tied([xb2, yb2], state)
        last = [move(ya2, TO_X), move(xb2, TO_Y)]
        more = to_core([b2, xb2, yb2])
        more, state = tied(more, state)
        state = fwd(3, state)
        last, state = tied(last, state)
        w2 = [a2, ya2, xa2, b2, xb2, yb2, *last, *cores, *more, *to_core(last)]
    else:
        for i in range(1, parts):
            state = fwd(i, state)
    ctx, qa0, qa1 = state
    out, act, low, gf, gp, ga, gc, sums, sbin = row_call(
        x, ctx, cot, place2, w2, vecs, b_in.reshape(nblk, width), lengths
    )
    def small_rows(sq, sv):
        vs = [jnp.concatenate([sq[0], sv[0]]), sums[5], sums[3], sums[4], sbin, sums[2], sums[0], sums[1]]
        return jnp.concatenate([v.reshape(count, -1) for v in vs], 1)

    p_wout = wgrad_call("wgrad_out", core, act, gf, True)
    p_win = wgrad_call("wgrad_in", core, low, gp, False)
    state = None
    bwd = lambda i, state, g: attn_bwd_call(qa0, qa1, qkv, ctx, g, lengths, i, parts, state)
    if regular():
        swap = lambda p: (p[0], move(p[1], TO_CORE))
        r_out = sum_core(here, [swap(p_wout)])
        p_wao = wgrad_call("wgrad_ao", core, ctx, after(ga, r_out[0][0]), False)
        r_in = sum_core(here, [swap(p_win), swap(p_wao)])
        def hold(r, state):
            (k0, g0), second = r
            return (after(k0, state[3]), g0), second

        gc = after(gc, r_in[0][0])
        state = bwd(0, None, gc)
        r_out = sum_plane(here, *hold(r_out, state))
        gc = after(gc, r_out[0][0])
        state = bwd(1, state, gc)
        r_in = sum_plane(here, *hold(r_in, state))
        gc = after(gc, r_in[0][0])
        state = bwd(2, state, gc)
        r_out = sum_z(here, *hold(r_out, state))
        gc = after(gc, r_out[0])
        state = bwd(3, state, gc)
        r_in = sum_z(here, *hold(r_in, state))
        dq, dk, dv, sq, sv = state
        own = small_sum(small_rows(sq, sv))
        p_wqkv = wgrad3(core, after(x, r_in[0]), dq, dk, dv)
        r_qkv = sum_core(here, [swap(p_wqkv)])
        g_tok = tok_call(after(ga, r_qkv[0][0], *r_out[1:]), dq, dk, dv, place, w1)
        (k0, g0), second = r_qkv
        r_qkv = sum_plane(here, (after(k0, g_tok, *r_in[1:]), g0), second)
        r_rest = copies_of([after(r_out[0], r_qkv[0][0]), *r_out[1:]], r_in)
        (k0, g0), second = r_qkv
        r_qkv = sum_z(here, (after(k0, r_rest[0], own), g0), second)
        g_wout, g_win, g_wao = final_call(here, r_rest, [(4, True), (nblk, False), (1, False)])
        (g_wqkv,) = final_call(here, copies_of(r_qkv), [(3, False)])
    else:
        p_wao = wgrad_call("wgrad_ao", core, ctx, ga, False)
        for i in range(parts):
            state = bwd(i, state, gc)
        dq, dk, dv, sq, sv = state
        own = small_sum(small_rows(sq, sv))
        p_wqkv = wgrad3(core, x, dq, dk, dv)
        g_tok = tok_call(ga, dq, dk, dv, place, w1)
        g_wout = reduce_any(*p_wout, True)
        g_win, g_wao, g_wqkv = [reduce_any(*p, False) for p in (p_win, p_wao, p_wqkv)]

    g_bqv, g_bao, g_g1, g_s1, g_bin, g_bout, g_g2, g_s2 = [own[e - s : e] for s, e in zip(sizes, ends)]
    return (
        out[None], g_tok[None], g_wqkv, g_bqv, g_wao, g_bao, g_g1, g_s1,
        g_win, g_bin, g_wout, g_bout, g_g2, g_s2,
    )


def solution(mesh):
    rows = P(("replica", "shard"), None, None)
    mat, vec = P("shard", None), P("shard")
    return jax.shard_map(
        shards,
        mesh=mesh,
        in_specs=(rows, P(("replica", "shard")), rows, mat, vec, mat, vec, vec, vec, mat, vec, mat, vec, vec, vec),
        out_specs=(rows, rows, mat, vec, mat, vec, vec, vec, mat, vec, mat, vec, vec, vec),
        check_vma=False,
    )
```

```python
import functools
import jax
import jax.numpy as jnp
from jax import lax
from jax.experimental import pallas as pl
from jax.experimental.pallas import tpu as pltpu
from jax.sharding import PartitionSpec as P

HD = 64
F32 = jnp.float32
BF = jnp.bfloat16
SQRT_HALF = 0.7071067811865476
INV_ROOT_TAU = 0.3989422804014327


def params():
    return pltpu.CompilerParams(vmem_limit_bytes=60 << 20)


def dot_nn(a, b):
    return jnp.dot(a, b, preferred_element_type=F32)


def dot_nt(a, b):
    return lax.dot_general(a, b, (((1,), (1,)), ((), ())), preferred_element_type=F32)


def dot_tn(a, b):
    return lax.dot_general(a, b, (((0,), (0,)), ((), ())), preferred_element_type=F32)


def cost(flops, nbytes, trans=0):
    return pl.CostEstimate(flops=int(flops), bytes_accessed=int(nbytes), transcendentals=int(trans))


SUB = 32
ANY = pl.BlockSpec(memory_space=pltpu.HBM)


def loads(place, bufs, lo, hi, target, sem):
    found = []
    for buf in bufs:
        for m in range(buf.shape[0]):
            i = len(found)
            found.append(pltpu.make_async_copy(buf.at[m, pl.ds(lo, hi - lo)], target(place[i]), sem.at[i]))
    return found


def start_all(copies):
    for c in copies:
        c.start()


def wait_all(copies):
    for c in copies:
        c.wait()


def qkv_body(count, place, x_ref, b_ref, *rest):
    bufs, (o_ref, w_vm, sem) = rest[:count], rest[count:]
    step = pl.program_id(0)
    blocks, width = w_vm.shape[0], w_vm.shape[-1]
    copies = loads(place, bufs, 0, blocks, lambda p: w_vm.at[:, p], sem)

    @pl.when(step == 0)
    def _():
        start_all(copies)
        wait_all(copies)

    x = x_ref[...]
    for n in range(blocks):
        w = w_vm[n].reshape(-1, width)
        bias = b_ref[:, n * width : (n + 1) * width]
        o_ref[:, n * width : (n + 1) * width] = (dot_nn(x, w) + bias).astype(BF)


def qkv_call(x, place, w1, bias, rows=256):
    slots, width = x.shape
    pieces = width // SUB
    return pl.pallas_call(
        functools.partial(qkv_body, len(w1)),
        name="qkv",
        grid_spec=pltpu.PrefetchScalarGridSpec(
            num_scalar_prefetch=1,
            grid=(slots // rows,),
            in_specs=[
                pl.BlockSpec((rows, width), lambda i, p: (i, 0)),
                pl.BlockSpec((1, 3 * width), lambda i, p: (0, 0)),
            ] + [ANY] * len(w1),
            out_specs=pl.BlockSpec((rows, 3 * width), lambda i, p: (i, 0)),
            scratch_shapes=[
                pltpu.VMEM((3, pieces, SUB, width), BF),
                pltpu.SemaphoreType.DMA((pieces,)),
            ],
        ),
        out_shape=jax.ShapeDtypeStruct((slots, 3 * width), BF),
        compiler_params=params(),
        cost_estimate=cost(6 * slots * width * width, 8 * slots * width + 6 * width * width),
    )(place, x, bias, *w1)


def lanes(rows):
    return lax.broadcasted_iota(jnp.int32, (rows, 2 * HD), 1)


def split3(v):
    hi = v.astype(BF).astype(F32)
    mid = (v - hi).astype(BF).astype(F32)
    return hi, mid, v - hi - mid


def attn_fwd_body(rows, len_ref, q_ref, k_ref, v_ref, *rest):
    ctx_ref, qa0_ref, qa1_ref = rest[-3:]
    slots = k_ref.shape[0]
    lane = lanes(slots)
    key_row = lax.broadcasted_iota(jnp.int32, (slots, 2 * HD), 0)
    bias = jnp.where(key_row < len_ref[0], 0.0, -1e30)
    k = k_ref[...].astype(F32)
    k_aug = []
    for h in range(2):
        own = (lane // HD) == h
        spare = (1 - h) * HD
        k_aug.append(jnp.where(own, k, jnp.where(lane == spare, bias, 0.0)).astype(BF))
    v_aug = [jnp.where((lane // HD) == h, v_ref[...].astype(F32), 1.0).astype(BF) for h in range(2)]
    lane_q = lanes(rows)

    def scores(item):
        blk, h = item
        q = q_ref[blk * rows : (blk + 1) * rows, :].astype(F32) * 0.125
        qh = jnp.where((lane_q // HD) == h, q, jnp.where(lane_q == (1 - h) * HD, 1.0, 0.0))
        return qh, dot_nt(qh.astype(BF), k_aug[h])

    items = [(blk, h) for blk in range(slots // rows) for h in range(2)]
    held = scores(items[0])
    outs = []
    for i, (blk, h) in enumerate(items):
        sl = slice(blk * rows, (blk + 1) * rows)
        qh, s = held
        if i + 1 < len(items):
            held = scores(items[i + 1])
        spare = (1 - h) * HD
        top = jnp.max(s, axis=-1, keepdims=True)
        o = dot_nn(jnp.exp(s - top).astype(BF), v_aug[h])
        norm = o[:, spare : spare + 1]
        outs.append(o / norm)
        hi, mid, lo = split3(-(top + jnp.log(norm)))
        qh = jnp.where(lane_q == spare + 1, hi, qh)
        qh = jnp.where(lane_q == spare + 2, mid, qh)
        qh = jnp.where(lane_q == spare + 3, lo, qh)
        (qa0_ref, qa1_ref)[h][sl, :] = qh.astype(BF)
        if h == 1:
            ctx_ref[sl, :] = jnp.where(lane_q < HD, outs[-2], outs[-1]).astype(BF)


def attn_fwd_call(qkv, lengths, part, parts, before, rows=256):
    slots, wide = qkv.shape
    width = wide // 3
    pairs = width // (2 * HD)
    each = pairs // parts
    col = lambda off: pl.BlockSpec((slots, 2 * HD), lambda j, ln: (0, off * pairs + part * each + j))
    out = jax.ShapeDtypeStruct((slots, width), BF)
    extra = list(before or ())
    return pl.pallas_call(
        functools.partial(attn_fwd_body, rows),
        name=f"attn_fwd{part}",
        grid_spec=pltpu.PrefetchScalarGridSpec(
            num_scalar_prefetch=1,
            grid=(each,),
            in_specs=[col(0), col(1), col(2)] + [ANY] * len(extra),
            out_specs=[col(0)] * 3,
        ),
        out_shape=[out, out, out],
        input_output_aliases={4 + i: i for i in range(3)} if before else {},
        compiler_params=params(),
        cost_estimate=cost(
            16 * slots * slots * width / parts, 12 * slots * width / parts, slots * slots * 2 * each
        ),
    )(lengths, qkv, qkv, qkv, *extra)


def attn_bwd_body(rows, len_ref, qa0_ref, qa1_ref, k_ref, v_ref, ctx_ref, g_ref, *rest):
    dq_ref, dk_ref, dv_ref, sq_ref, sv_ref = rest[-5:]
    slots = k_ref.shape[0]
    lane = lanes(slots)
    key_row = lax.broadcasted_iota(jnp.int32, (slots, 2 * HD), 0)
    bias = jnp.where(key_row < len_ref[0], 0.0, -1e30)
    k = k_ref[...].astype(F32)
    v = v_ref[...].astype(F32)
    k_low = k_ref[...]
    k_aug, v_aug = [], []
    for h in range(2):
        own = (lane // HD) == h
        spare = (1 - h) * HD
        near = (lane > spare) & (lane < spare + 4)
        ones = jnp.where(near, 1.0, 0.0)
        k_aug.append(jnp.where(own, k, jnp.where(lane == spare, bias, ones)).astype(BF))
        v_aug.append(jnp.where(own, v, ones).astype(BF))
    lane_q = lanes(rows)
    items = [(blk, h) for blk in range(slots // rows) for h in range(2)]

    def products(item):
        blk, h = item
        sl = slice(blk * rows, (blk + 1) * rows)
        own = (lane_q // HD) == h
        spare = (1 - h) * HD
        g = g_ref[sl, :].astype(F32)
        delta = jnp.sum(jnp.where(own, g * ctx_ref[sl, :].astype(F32), 0.0), axis=-1, keepdims=True)
        hi, mid, lo = split3(-delta)
        ga = jnp.where(own, g, 0.0)
        ga = jnp.where(lane_q == spare + 1, hi, ga)
        ga = jnp.where(lane_q == spare + 2, mid, ga)
        ga = jnp.where(lane_q == spare + 3, lo, ga).astype(BF)
        return dot_nt(k_aug[h], (qa0_ref, qa1_ref)[h][sl, :]), dot_nt(v_aug[h], ga)

    held = products(items[0])
    dk = [jnp.zeros((slots, 2 * HD), F32)] * 2
    dv = [jnp.zeros((slots, 2 * HD), F32)] * 2
    dqs = []
    for i, (blk, h) in enumerate(items):
        sl = slice(blk * rows, (blk + 1) * rows)
        s, gs = held
        if i + 1 < len(items):
            held = products(items[i + 1])
        p = jnp.exp(s)
        ds = (p * gs).astype(BF)
        dv[h] = dv[h] + dot_nn(p.astype(BF), g_ref[sl, :])
        dk[h] = dk[h] + dot_nn(ds, (qa0_ref, qa1_ref)[h][sl, :])
        dqs.append(dot_tn(ds, k_low))
        if h == 1:
            dq_ref[sl, :] = (jnp.where(lane_q < HD, dqs[-2], dqs[-1]) * 0.125).astype(BF)
    dk_ref[...] = jnp.where(lane < HD, dk[0], dk[1]).astype(BF)
    dv_low = jnp.where(lane < HD, dv[0], dv[1]).astype(BF)
    dv_ref[...] = dv_low
    sq_ref[...] = jnp.sum(dq_ref[...].astype(F32), axis=0, keepdims=True)
    sv_ref[...] = jnp.sum(dv_low.astype(F32), axis=0, keepdims=True)


def attn_bwd_call(qa0, qa1, qkv, ctx, grad_ctx, lengths, part, parts, before, rows=256):
    slots, width = ctx.shape
    pairs = width // (2 * HD)
    each = pairs // parts
    col = lambda off: pl.BlockSpec((slots, 2 * HD), lambda j, ln: (0, off * pairs + part * each + j))
    row = pl.BlockSpec((1, 2 * HD), lambda j, ln: (0, part * each + j))
    out = jax.ShapeDtypeStruct((slots, width), BF)
    vec = jax.ShapeDtypeStruct((1, width), F32)
    extra = list(before or ())
    return pl.pallas_call(
        functools.partial(attn_bwd_body, rows),
        name=f"attn_bwd{part}",
        grid_spec=pltpu.PrefetchScalarGridSpec(
            num_scalar_prefetch=1,
            grid=(each,),
            in_specs=[col(0), col(0), col(1), col(2), col(0), col(0)] + [ANY] * len(extra),
            out_specs=[col(0)] * 3 + [row] * 2,
        ),
        out_shape=[out, out, out, vec, vec],
        input_output_aliases={7 + i: i for i in range(5)} if before else {},
        compiler_params=params(),
        cost_estimate=cost(
            40 * slots * slots * width / parts, 18 * slots * width / parts, slots * slots * 2 * each
        ),
    )(lengths, qa0, qa1, qkv, qkv, ctx, grad_ctx, *extra)


def norm_stats(resid):
    mean = jnp.mean(resid, axis=-1, keepdims=True)
    centred = resid - mean
    inv = lax.rsqrt(jnp.mean(centred * centred, axis=-1, keepdims=True) + 1e-5)
    return centred * inv, inv


def norm_back(u, normed, inv):
    return inv * (u - jnp.mean(u, axis=-1, keepdims=True) - normed * jnp.mean(u * normed, axis=-1, keepdims=True))


def colsum(v):
    return jnp.sum(v, axis=0, keepdims=True)


def row_body(n2, len_ref, place, x_ref, ctx_ref, cot_ref, vec_ref, bin_ref, *rest):
    b2 = rest[:n2]
    (
        out_ref, act_ref, hid_ref, gf_ref, gp_ref, ga_ref, gc_ref, sums_ref, sbin_ref,
        wa, wi, wo, slope, sem,
    ) = rest[n2:]
    step = pl.program_id(0)
    rows, width = x_ref.shape
    nblk = wi.shape[0]
    copies = [
        loads(place, b2, 0, 1, lambda p: wa.at[pl.ds(p, 1)], sem.at[0]),
        loads(place, b2, 1, 1 + nblk, lambda p: wi.at[:, p], sem.at[1]),
        loads(place, b2, 1 + nblk, 5 + nblk, lambda p: wo.at[p], sem.at[2]),
    ]

    @pl.when(step == 0)
    def _():
        for c in copies:
            start_all(c)
        sums_ref[...] = jnp.zeros_like(sums_ref)
        sbin_ref[...] = jnp.zeros_like(sbin_ref)

    def ready(i):
        @pl.when(step == 0)
        def _():
            wait_all(copies[i])

    bao, gain1, shift1, bout, gain2, shift2 = [vec_ref[i : i + 1, :] for i in range(6)]
    ready(0)
    w_ao = wa[...].reshape(width, width)
    resid1 = x_ref[...].astype(F32) + dot_nn(ctx_ref[...], w_ao) + bao
    normed1, inv1 = norm_stats(resid1)
    hidden = normed1 * gain1 + shift1
    low = hidden.astype(BF)
    hid_ref[...] = low
    acc = jnp.zeros((rows, width), F32)
    per = wo.shape[0] // nblk
    ready(1)
    for n in range(nblk):
        pre = dot_nn(low, wi[n].reshape(width, width)) + bin_ref[n : n + 1, :]
        phi = 0.5 + 0.5 * lax.erf(pre * SQRT_HALF)
        slope[n] = (phi + pre * (INV_ROOT_TAU * jnp.exp(-0.5 * pre * pre))).astype(slope.dtype)
        act = (pre * phi).astype(BF)
        act_ref[:, n * width : (n + 1) * width] = act
        if n == 0:
            ready(2)
        acc = acc + dot_nn(act, wo[n * per : (n + 1) * per].reshape(width, width))
    resid2 = hidden + acc + bout
    normed2, inv2 = norm_stats(resid2)
    row_id = lax.broadcasted_iota(jnp.int32, (rows, 1), 0) + step * rows
    valid = (row_id < len_ref[0]).astype(F32)
    out_ref[...] = ((normed2 * gain2 + shift2) * valid).astype(BF)
    gz = cot_ref[...].astype(F32) * valid
    sums_ref[0:1, :] += colsum(gz * normed2)
    sums_ref[1:2, :] += colsum(gz)
    g_resid2 = norm_back(gz * gain2, normed2, inv2)
    gf = g_resid2.astype(BF)
    gf_ref[...] = gf
    sums_ref[2:3, :] += colsum(gf.astype(F32))
    acc = g_resid2
    for n in range(nblk):
        g_act = dot_nt(gf, wo[n * per : (n + 1) * per].reshape(width, width))
        gp = (g_act * slope[n].astype(F32)).astype(BF)
        gp_ref[:, n * width : (n + 1) * width] = gp
        sbin_ref[n : n + 1, :] += colsum(gp.astype(F32))
        acc = acc + dot_nt(gp, wi[n].reshape(width, width))
    sums_ref[3:4, :] += colsum(acc * normed1)
    sums_ref[4:5, :] += colsum(acc)
    g_attn = norm_back(acc * gain1, normed1, inv1).astype(BF)
    ga_ref[...] = g_attn
    sums_ref[5:6, :] += colsum(g_attn.astype(F32))
    gc_ref[...] = dot_nt(g_attn, w_ao).astype(BF)


def row_call(x, ctx, cot, place, w2, vecs, b_in, lengths, rows=256):
    slots, width = x.shape
    pieces, sub = width // SUB, SUB
    nblk = b_in.shape[0]
    ff = nblk * width
    blk = pl.BlockSpec((rows, width), lambda i, ln, p: (i, 0))
    big = pl.BlockSpec((rows, ff), lambda i, ln, p: (i, 0), pipeline_mode=pl.Buffered(1 if rows > 256 else 2))
    const = lambda r: pl.BlockSpec((r, width), lambda i, ln, p: (0, 0))
    o = jax.ShapeDtypeStruct((slots, width), BF)
    ob = jax.ShapeDtypeStruct((slots, ff), BF)
    return pl.pallas_call(
        functools.partial(row_body, len(w2)),
        name="row_local",
        grid_spec=pltpu.PrefetchScalarGridSpec(
            num_scalar_prefetch=2,
            grid=(slots // rows,),
            in_specs=[blk, blk, blk, const(8), const(nblk)] + [ANY] * len(w2),
            out_specs=[blk, big, blk, blk, big, blk, blk, const(8), const(nblk)],
            scratch_shapes=[
                pltpu.VMEM((pieces, sub, width), BF),
                pltpu.VMEM((nblk, pieces, sub, width), BF),
                pltpu.VMEM((pieces, 4, sub, width), BF),
                pltpu.VMEM((nblk, rows, width), BF),
                pltpu.SemaphoreType.DMA((3, pieces)),
            ],
        ),
        out_shape=[
            o, ob, o, o, ob, o, o,
            jax.ShapeDtypeStruct((8, width), F32),
            jax.ShapeDtypeStruct((nblk, width), F32),
        ],
        compiler_params=params(),
        cost_estimate=cost(36 * slots * width * width, 40 * slots * width + 18 * width * width, 2 * slots * ff),
    )(lengths, place, x, ctx, cot, vecs, b_in, *w2)


def halves(core, value, keep_ref, send_ref):
    count, rows, width = keep_ref.shape
    value = value.reshape(count, 2, rows, width)
    even, odd = value[:, 0], value[:, 1]

    @pl.when(core == 0)
    def _():
        keep_ref[...] = even
        send_ref[...] = odd

    @pl.when(core != 0)
    def _():
        keep_ref[...] = odd
        send_ref[...] = even


LINES = 16


def lines_of(*lines):
    width, segments = lines[0][0], [line[1:] for line in lines]
    row = lax.broadcasted_iota(jnp.int32, (LINES, width), 0)
    value = jnp.zeros((LINES, width), F32)
    for i, segs in enumerate(segments):
        used = sum(v.shape[1] for v in segs)
        line = jnp.concatenate([*segs, jnp.zeros((1, width - used), F32)], 1)
        value = jnp.where(row == i, line, value)
    return value.astype(BF)


def wgrad_body(core, a_ref, b_ref, keep_ref, send_ref):
    halves(core[0], dot_tn(a_ref[...], b_ref[...]).astype(BF), keep_ref, send_ref)


def wgrad_call(name, core, a, b, by_rows, tile=1024):
    slots, m = a.shape
    width = a.shape[1] if not by_rows else b.shape[1]
    blocks = m // width if by_rows else b.shape[1] // m
    pieces = width // SUB
    if by_rows:
        grid = (1, m // tile)
        block = (tile // (2 * SUB * blocks), blocks * SUB, width)
        where = lambda j, i, c: (i, 0, 0)
    else:
        grid = (blocks, m // tile)
        block = (tile // (2 * SUB), SUB, width)
        where = lambda j, i, c: (i, j, 0)
    out = jax.ShapeDtypeStruct((pieces // 2, blocks * SUB, width), BF)
    return pl.pallas_call(
        wgrad_body,
        name=name,
        grid_spec=pltpu.PrefetchScalarGridSpec(
            num_scalar_prefetch=1,
            grid=grid,
            in_specs=[
                pl.BlockSpec((slots, tile), lambda j, i, c: (0, i)),
                pl.BlockSpec((slots, width), lambda j, i, c: (0, j)),
            ],
            out_specs=[pl.BlockSpec(block, where)] * 2,
        ),
        out_shape=[out, out],
        compiler_params=params(),
        cost_estimate=cost(2 * slots * m * b.shape[1], 2 * (slots * (m + b.shape[1]) + m * b.shape[1])),
    )(core, a, b)


def wgrad_ao_body(core, a_ref, b_ref, sums_ref, sbin_ref, keep_ref, send_ref):
    value = dot_tn(a_ref[...], b_ref[...]).astype(BF)
    halves(core[0], value, keep_ref.at[:, pl.ds(0, SUB)], send_ref.at[:, pl.ds(0, SUB)])
    count, _, width = keep_ref.shape
    owners = count // 2
    part, four = width // owners, sbin_ref.shape[0] * width // owners
    for s in range(owners):
        segs = [sums_ref[v : v + 1, s * part : (s + 1) * part] for v in (5, 3, 4, 2, 0, 1)]
        row, col = s * four // width, s * four % width
        value = lines_of([width, *segs], [width, sbin_ref[row : row + 1, col : col + four]])
        for ref in (keep_ref, send_ref):
            for x in (0, 1):
                ref[2 * s + x, SUB : SUB + LINES] = value


def wgrad_ao(core, a, b, sums, sbin):
    slots, m = a.shape
    full = lambda v: pl.BlockSpec(v.shape, lambda t, c: (0, 0))
    shape = (m // SUB // 2, SUB + LINES, m)
    return pl.pallas_call(
        wgrad_ao_body,
        name="wgrad_ao",
        grid_spec=pltpu.PrefetchScalarGridSpec(
            num_scalar_prefetch=1,
            grid=(1,),
            in_specs=[full(v) for v in (a, b, sums, sbin)],
            out_specs=[pl.BlockSpec(shape, lambda t, c: (0, 0, 0))] * 2,
        ),
        out_shape=[jax.ShapeDtypeStruct(shape, BF)] * 2,
        compiler_params=params(),
        cost_estimate=cost(2 * slots * m * m, 4 * slots * m + 2 * m * m),
    )(core, a, b, sums, sbin)


def wgrad3_body(core, a_ref, q_ref, k_ref, v_ref, sq_ref, sv_ref, keep_ref, send_ref):
    for n, ref in enumerate((q_ref, k_ref, v_ref)):
        value = dot_tn(a_ref[...], ref[...]).astype(BF)
        rows = pl.ds(n * SUB, SUB)
        halves(core[0], value, keep_ref.at[:, rows], send_ref.at[:, rows])
    count, _, width = keep_ref.shape
    line = jnp.where(pl.program_id(0) == 0, sq_ref[...], sv_ref[...])
    part = 2 * width // count
    for s in range(count // 2):
        value = lines_of([width, line[:, s * part : (s + 1) * part]])
        for ref in (keep_ref, send_ref):
            for x in (0, 1):
                ref[2 * s + x, 3 * SUB : 3 * SUB + LINES] = value


def wgrad3(core, a, dq, dk, dv, sq, sv):
    slots, m = a.shape
    tile = m // 2
    full = pl.BlockSpec((slots, m), lambda i, c: (0, 0))
    vec = pl.BlockSpec((1, m), lambda i, c: (0, 0))
    block = pl.BlockSpec((tile // (2 * SUB), 3 * SUB + LINES, m), lambda i, c: (i, 0, 0))
    out = jax.ShapeDtypeStruct((m // SUB // 2, 3 * SUB + LINES, m), BF)
    return pl.pallas_call(
        wgrad3_body,
        name="wgrad_qkv",
        grid_spec=pltpu.PrefetchScalarGridSpec(
            num_scalar_prefetch=1,
            grid=(2,),
            in_specs=[pl.BlockSpec((slots, tile), lambda i, c: (0, i)), full, full, full, vec, vec],
            out_specs=[block, block],
        ),
        out_shape=[out, out],
        compiler_params=params(),
        cost_estimate=cost(6 * slots * m * m, 14 * slots * m),
    )(core, a, dq, dk, dv, sq, sv)


def tok_body(count, place, g_ref, dq_ref, dk_ref, dv_ref, *rest):
    bufs, (o_ref, w_vm, sem) = rest[:count], rest[count:]
    step = pl.program_id(0)
    width = g_ref.shape[1]
    copies = loads(place, bufs, 0, 3, lambda p: w_vm.at[:, p], sem)

    @pl.when(step == 0)
    def _():
        start_all(copies)
        wait_all(copies)

    acc = g_ref[...].astype(F32)
    for n, ref in enumerate((dq_ref, dk_ref, dv_ref)):
        acc = acc + dot_nt(ref[...], w_vm[n].reshape(width, width))
    o_ref[...] = acc.astype(BF)


def tok_call(g, dq, dk, dv, place, w1, rows=256):
    slots, width = g.shape
    pieces = width // SUB
    blk = pl.BlockSpec((rows, width), lambda i, p: (i, 0))
    return pl.pallas_call(
        functools.partial(tok_body, len(w1)),
        name="grad_tok",
        grid_spec=pltpu.PrefetchScalarGridSpec(
            num_scalar_prefetch=1,
            grid=(slots // rows,),
            in_specs=[blk, blk, blk, blk] + [ANY] * len(w1),
            out_specs=blk,
            scratch_shapes=[pltpu.VMEM((3, pieces, SUB, width), BF), pltpu.SemaphoreType.DMA((pieces,))],
        ),
        out_shape=jax.ShapeDtypeStruct((slots, width), BF),
        compiler_params=params(),
        cost_estimate=cost(6 * slots * width * width, 16 * slots * width),
    )(place, g, dq, dk, dv, *w1)


def total(*terms):
    acc = terms[0].astype(F32)
    for t in terms[1:]:
        acc = acc + t.astype(F32)
    return acc.astype(BF)


def add1_body(count, here, *refs):
    ins, outs = refs[: 8 * count], refs[8 * count :]
    for view in range(4):
        n0 = 0
        for i in range(count):
            a, b = ins[8 * i + 2 * view], ins[8 * i + 2 * view + 1]
            n = a.shape[3]
            outs[view][0, n0 : n0 + n] = total(a[0, 0, 0], b[0, 0, 0])
            n0 += n


def add1(here, pairs):
    width = pairs[0][0].shape[-1]
    views = []
    for half, own in ((0, 0), (0, 1), (1, 0), (1, 1)):
        def where(t, h, half=half, own=own):
            z, j = 2 * half + t // 2, t % 2
            if half == 0:
                return (z, j, h[0] if own else 1 - h[0], 0, 0)
            return (z, h[1] if own else 1 - h[1], j, 0, 0)
        views.append(where)
    specs, args, rows = [], [], 0
    for keep, got in pairs:
        n = keep.shape[1]
        rows += n
        for where in views:
            for arr in (keep, got):
                specs.append(pl.BlockSpec((1, 1, 1, n, width), where))
                args.append(arr.reshape(4, 2, 2, n, width))
    out = jax.ShapeDtypeStruct((4, rows, width), BF)
    return pl.pallas_call(
        functools.partial(add1_body, len(pairs)),
        name="add_core",
        grid_spec=pltpu.PrefetchScalarGridSpec(
            num_scalar_prefetch=1,
            grid=(4,),
            in_specs=specs,
            out_specs=[pl.BlockSpec((1, rows, width), lambda t, h: (t, 0, 0))] * 4,
        ),
        out_shape=[out] * 4,
        compiler_params=params(),
        cost_estimate=cost(16 * rows * width, 96 * rows * width),
    )(here, *args)


def add2_body(here, *refs):
    ins, outs = refs[:8], refs[8:]
    for view in range(4):
        outs[view][0] = total(ins[2 * view][0, 0], ins[2 * view + 1][0, 0])


def add2(here, first, second):
    _, rows, width = first[0].shape
    specs, args = [], []
    for axis, pair in ((1, first), (0, second)):
        for own in (0, 1):
            for arr in pair:
                specs.append(pl.BlockSpec(
                    (1, 1, rows, width),
                    lambda t, h, axis=axis, own=own: (t, h[axis] if own else 1 - h[axis], 0, 0),
                ))
                args.append(arr.reshape(2, 2, rows, width))
    out = jax.ShapeDtypeStruct((2, rows, width), BF)
    return pl.pallas_call(
        add2_body,
        name="add_plane",
        grid_spec=pltpu.PrefetchScalarGridSpec(
            num_scalar_prefetch=1,
            grid=(2,),
            in_specs=specs,
            out_specs=[pl.BlockSpec((1, rows, width), lambda t, h: (t, 0, 0))] * 4,
        ),
        out_shape=[out] * 4,
        compiler_params=params(),
        cost_estimate=cost(8 * rows * width, 48 * rows * width),
    )(here, *args)


def add3_body(here, ak, ag, bk, bg, *outs):
    for k, out in enumerate(outs):
        to = lax.rem(here[2] + k, 4)
        spot = lax.rem(to, 2)

        @pl.when(to < 2)
        def _():
            out[0] = total(ak[spot], ag[spot])

        @pl.when(to >= 2)
        def _():
            out[0] = total(bk[spot], bg[spot])


def add3(here, first, second):
    _, rows, width = first[0].shape
    full = pl.BlockSpec((2, rows, width), lambda t, h: (0, 0, 0))
    one = pl.BlockSpec((1, rows, width), lambda t, h: (0, 0, 0))
    return pl.pallas_call(
        add3_body,
        name="add_z",
        grid_spec=pltpu.PrefetchScalarGridSpec(
            num_scalar_prefetch=1, grid=(1,), in_specs=[full] * 4, out_specs=[one] * 4,
        ),
        out_shape=[jax.ShapeDtypeStruct((1, rows, width), BF)] * 4,
        compiler_params=params(),
        cost_estimate=cost(4 * rows * width, 24 * rows * width),
    )(here, *first, *second)


def add4_body(*refs):
    ins, out = refs[:-1], refs[-1]
    n0 = 0
    for i in range(0, len(ins), 4):
        n = ins[i].shape[1]
        out[:, n0 : n0 + n] = total(*[r[...] for r in ins[i : i + 4]])
        n0 += n


def add4(*groups):
    spec = lambda shape: pl.BlockSpec(shape, lambda t: (0,) * len(shape))
    width = groups[0][0].shape[-1]
    shape = (1, sum(g[0].shape[1] for g in groups), width)
    parts = [v for g in groups for v in g]
    size = shape[1] * width
    return pl.pallas_call(
        add4_body,
        name="add_last",
        grid=(1,),
        in_specs=[spec(v.shape) for v in parts],
        out_specs=spec(shape),
        out_shape=jax.ShapeDtypeStruct(shape, BF),
        compiler_params=params(),
        cost_estimate=cost(3 * size, 10 * size),
    )(*parts)


def final_body(kinds, vectors, here, own, core, over_x, both, *outs):
    mine_at = 2 * here[0] + here[3]
    mats, vecs = outs[: len(kinds)], outs[len(kinds) :]
    for flip, ref in enumerate((own, core, over_x, both)):
        share = jnp.bitwise_xor(mine_at, flip)
        n0 = 0
        for (blocks, by_rows), out in zip(kinds, mats):
            width = ref.shape[-1]
            for n in range(blocks):
                value = ref[0, n0 : n0 + SUB].astype(F32)
                n0 += SUB
                if by_rows:
                    out[pl.ds(pl.multiple_of(share * blocks * SUB, SUB) + n * SUB, SUB), :] = value
                else:
                    out[pl.ds(pl.multiple_of(share * SUB, SUB), SUB), n * width : (n + 1) * width] = value

        @pl.when(share == 0)
        def _():
            lines = ref[0, n0 : n0 + LINES].astype(F32)
            for (row, lane, size), out in zip(vectors, vecs):
                out[...] = lines[row : row + 1, lane : lane + size]


def final_call(here, parts, kinds, vectors):
    shape = parts[0].shape
    width = shape[-1]
    shapes = [
        (4 * blocks * SUB, width) if by_rows else (4 * SUB, blocks * width) for blocks, by_rows in kinds
    ] + [(1, size) for _, _, size in vectors]
    return pl.pallas_call(
        functools.partial(final_body, kinds, vectors),
        name="final",
        grid_spec=pltpu.PrefetchScalarGridSpec(
            num_scalar_prefetch=1,
            grid=(1,),
            in_specs=[pl.BlockSpec(shape, lambda t, h: (0, 0, 0))] * 4,
            out_specs=[pl.BlockSpec(sh, lambda t, h: (0, 0)) for sh in shapes],
        ),
        out_shape=[jax.ShapeDtypeStruct(sh, F32) for sh in shapes],
        compiler_params=params(),
        cost_estimate=cost(1, 24 * parts[0].size),
    )(here, *parts)


BOTH = ("shard", "replica")
AXES = ("replica", "shard")


def table(fn):
    pairs = []
    for r in range(4):
        for s in range(8):
            x, y, z, c = fn(r // 2, s % 2, s // 2, r % 2)
            pairs.append((r * 8 + s, (x * 2 + c) * 8 + z * 2 + y))
    return pairs


TO_CORE = table(lambda x, y, z, c: (x, y, z, 1 - c))
TO_X = table(lambda x, y, z, c: (1 - x, y, z, c))
TO_XCORE = table(lambda x, y, z, c: (1 - x, y, z, 1 - c))
TO_Y = table(lambda x, y, z, c: (x, 1 - y, z, c))
TO_Z = [table(lambda x, y, z, c, k=k: (x, y, (z + k) % 4, c)) for k in range(4)]


def move(v, pairs):
    return lax.ppermute(v, AXES, pairs)


def regular():
    return lax.axis_size("shard") == 8 and lax.axis_size("replica") == 4


def place_of():
    r, s = lax.axis_index("replica"), lax.axis_index("shard")
    return r // 2, s % 2, s // 2, r % 2


def pack_body(count, share, *refs):
    ins, smalls, outs = refs[:count], refs[count:-2], refs[-2:]
    out, line = outs
    width = out.shape[-1]
    n0 = 0
    for ref in ins:
        rows, cols = ref.shape
        if rows > SUB:
            out[0, n0 : n0 + rows // SUB] = ref[...].reshape(rows // SUB, SUB, width)
            n0 += rows // SUB
        else:
            for n in range(cols // width):
                out[0, n0 + n] = ref[:, n * width : (n + 1) * width]
            n0 += cols // width
    n0 = 0
    for ref in smalls:
        line[:, n0 : n0 + ref.shape[1]] = ref[...]
        n0 += ref.shape[1]


def pack(share, mats, smalls, width):
    shapes = [(m.shape[0] // 4, m.shape[1]) for m in mats]
    blocks = sum(r * c for r, c in shapes) // (SUB * width)
    smalls = [v.reshape(1, -1) for v in smalls]
    line = (1, sum(v.shape[1] for v in smalls))
    return pl.pallas_call(
        functools.partial(pack_body, len(mats)),
        name="pack",
        grid_spec=pltpu.PrefetchScalarGridSpec(
            num_scalar_prefetch=1,
            grid=(1,),
            in_specs=[pl.BlockSpec(sh, lambda t, r: (r[0], 0)) for sh in shapes]
            + [pl.BlockSpec(v.shape, lambda t, r: (0, 0)) for v in smalls],
            out_specs=[
                pl.BlockSpec((1, blocks, SUB, width), lambda t, r: (0, 0, 0, 0)),
                pl.BlockSpec(line, lambda t, r: (0, 0)),
            ],
        ),
        out_shape=[jax.ShapeDtypeStruct((1, blocks, SUB, width), BF), jax.ShapeDtypeStruct(line, BF)],
        compiler_params=params(),
        cost_estimate=cost(1, 4 * blocks * SUB * width),
    )(share, *mats, *smalls)


def after(v, *deps):
    return lax.optimization_barrier((v,) + deps)[0]


def gather_z(own):
    near = [move(own, TO_Z[k]) for k in (1, 2, 3)]
    return jnp.concatenate([own, near[0]], 0), jnp.concatenate([near[1], near[2]], 0)


def to_core(bufs):
    return [move(v, TO_CORE) for v in bufs]


def tied(*groups):
    flat = lax.optimization_barrier([v for g in groups for v in g])
    out = []
    for g in groups:
        out.append(flat[: len(g)])
        flat = flat[len(g) :]
    return out


def gather_places(order):
    x, y, z, c = place_of()
    spots = []
    for fc in (0, 1):
        for k0, fx, fy in order:
            for k in (k0, k0 + 1):
                spots.append((((z - k) % 4) * 2 + (y ^ fy)) * 4 + (x ^ fx) * 2 + (c ^ fc))
    return jnp.stack(spots).astype(jnp.int32)


def spread(w, blocks, wide):
    full = lax.all_gather(w, "shard", axis=0, tiled=True)
    if full.shape[1] == wide:
        return full.reshape(-1, blocks, SUB, wide)
    return full.reshape(-1, SUB, blocks, wide).transpose(0, 2, 1, 3)


def sum_core(here, pairs):
    a_send, a_keep, b_send, b_keep = add1(here, pairs)
    return (a_keep, move(a_send, TO_X)), (b_keep, move(b_send, TO_Y))


def sum_plane(here, first, second):
    a_send, a_keep, b_send, b_keep = add2(here, first, second)
    return (a_keep, move(a_send, TO_Y)), (b_keep, move(b_send, TO_X))


def sum_z(here, first, second):
    own, *sends = add3(here, first, second)
    return [own] + [move(v, TO_Z[k + 1]) for k, v in enumerate(sends)]


def small_gather(plane):
    x, y, z, c = place_of()
    rows = jnp.concatenate([plane] + [move(plane, TO_Z[k]) for k in (1, 2, 3)], 0)
    spots = jnp.stack([((z - k) % 4) * 2 + (y ^ f) for k in range(4) for f in (0, 1)])
    pick = (jnp.arange(8)[:, None] == spots[None, :]).astype(BF)
    return dot_nn(pick, rows)


def small_sum(rows):
    return lax.dynamic_index_in_dim(lax.psum(rows, BOTH), lax.axis_index("shard"), 0, keepdims=False)


def reduce_any(keep, send, by_rows):
    half, rows, wide = keep.shape
    full = jnp.stack([keep, send], 1).reshape(2 * half, rows // SUB, SUB, wide)
    full = full.reshape(-1, wide) if by_rows else full.transpose(0, 2, 1, 3).reshape(2 * half * SUB, -1)
    part = lax.psum_scatter(full, "shard", scatter_dimension=0, tiled=True)
    return lax.psum(part, "replica").astype(F32)


def shards(
    tokens, lengths, cotangent, w_qkv, b_qv, w_attn_out, b_attn_out, ln1_gain, ln1_bias,
    w_ffn_in, b_ffn_in, w_ffn_out, b_ffn_out, ln2_gain, ln2_bias,
):
    _, slots, width = tokens.shape
    nblk = w_ffn_in.shape[1] // width
    count = lax.axis_size("shard")
    x = tokens.reshape(slots, width)
    cot = cotangent.reshape(slots, width)
    small = [b_qv, b_attn_out, ln1_gain, ln1_bias, b_ffn_in, b_ffn_out, ln2_gain, ln2_bias]
    sizes = [v.shape[0] for v in small]
    ends = [sum(sizes[: i + 1]) for i in range(len(sizes))]

    if regular():
        share = lax.axis_index("replica").reshape(1).astype(jnp.int32)
        first, line = pack(share, [w_qkv], small, width)
        plane = jnp.concatenate([line, move(line, TO_Y)], 0)
        a1, b1 = gather_z(first)
        rows = small_gather(after(plane, a1, b1))
        second, _ = pack(share, [w_attn_out, w_ffn_in, w_ffn_out], [b_qv], width)
        second = after(second, a1, b1, rows)
        near, *far = [move(second, TO_Z[k]) for k in (1, 2, 3)]
        plane = [move(a1, TO_Y), move(b1, TO_X), move(a1, TO_X), move(b1, TO_Y)]
        first = [a1, b1]
        cores = to_core(first)
        plane, cores = tied(plane, cores)
        last = [move(plane[0], TO_X), move(plane[1], TO_Y)]
        more = to_core(plane)
        _, [near, far[1]] = tied(last, [near, far[1]])
        w1 = [*first, *plane, *last, *cores, *more, *to_core(last)]
        a2 = jnp.concatenate([second, near], 0)
        ya2, xa2 = move(a2, TO_Y), move(a2, TO_X)
        place = gather_places(((0, 0, 0), (2, 0, 0), (0, 0, 1), (2, 1, 0), (0, 1, 0), (2, 0, 1), (0, 1, 1), (2, 1, 1)))
        place2 = gather_places(((0, 0, 0), (0, 0, 1), (0, 1, 0), (2, 0, 0), (2, 1, 0), (2, 0, 1), (0, 1, 1), (2, 1, 1)))
        here = jnp.stack(place_of()).astype(jnp.int32)
    else:
        w1 = [spread(w_qkv, 3, width)]
        w2 = [spread(w_attn_out, 1, width), spread(w_ffn_in, nblk, width), spread(w_ffn_out, 4, width)]
        w2 = [jnp.concatenate(w2, 1)]
        place = place2 = jnp.arange(width // SUB, dtype=jnp.int32)
        here = jnp.zeros((4,), jnp.int32)
    core = here[3:]

    if not regular():
        rows = lax.all_gather(jnp.concatenate(small), "shard", axis=0).astype(F32)
    b_qv, bao, gain1, shift1, b_in, bout, gain2, shift2 = [
        rows[:, e - s : e].reshape(-1) for s, e in zip(sizes, ends)
    ]
    bias3 = jnp.concatenate([b_qv[:width], jnp.zeros((width,), F32), b_qv[width:]]).reshape(1, -1)
    zero = jnp.zeros((width,), F32)
    vecs = jnp.stack([bao, gain1, shift1, bout, gain2, shift2, zero, zero])

    qkv = qkv_call(x, place, w1, bias3)
    parts = 4
    fwd = lambda i, state: attn_fwd_call(qkv, lengths, i, parts, state)
    state = fwd(0, None)
    if regular():
        far, [ya2, xa2], state = tied(far, [ya2, xa2], state)
        b2 = jnp.concatenate(far, 0)
        xb2, yb2 = move(b2, TO_X), move(b2, TO_Y)
        cores = to_core([a2, ya2, xa2])
        state = fwd(1, state)
        cores, state = tied(cores, state)
        state = fwd(2, state)
        [xb2, yb2], state = tied([xb2, yb2], state)
        last = [move(ya2, TO_X), move(xb2, TO_Y)]
        more = to_core([b2, xb2, yb2])
        more, state = tied(more, state)
        state = fwd(3, state)
        last, state = tied(last, state)
        w2 = [a2, ya2, xa2, b2, xb2, yb2, *last, *cores, *more, *to_core(last)]
    else:
        for i in range(1, parts):
            state = fwd(i, state)
    ctx, qa0, qa1 = state
    out, act, low, gf, gp, ga, gc, sums, sbin = row_call(
        x, ctx, cot, place2, w2, vecs, b_in.reshape(nblk, width), lengths
    )
    p_wout = wgrad_call("wgrad_out", core, act, gf, True)
    p_win = wgrad_call("wgrad_in", core, low, gp, False)
    state = None
    bwd = lambda i, state, g: attn_bwd_call(qa0, qa1, qkv, ctx, g, lengths, i, parts, state)
    if regular():
        swap = lambda p: (p[0], move(p[1], TO_CORE))
        r_out = sum_core(here, [swap(p_wout)])
        p_wao = wgrad_ao(core, ctx, after(ga, r_out[0][0]), sums, sbin)
        r_in = sum_core(here, [swap(p_win), swap(p_wao)])
        def hold(r, state):
            (k0, g0), second = r
            return (after(k0, state[3]), g0), second

        gc = after(gc, r_in[0][0])
        state = bwd(0, None, gc)
        r_out = sum_plane(here, *hold(r_out, state))
        gc = after(gc, r_out[0][0])
        state = bwd(1, state, gc)
        r_in = sum_plane(here, *hold(r_in, state))
        gc = after(gc, r_in[0][0])
        state = bwd(2, state, gc)
        r_out = sum_z(here, *hold(r_out, state))
        gc = after(gc, r_out[0])
        state = bwd(3, state, gc)
        r_in = sum_z(here, *hold(r_in, state))
        dq, dk, dv, sq, sv = state
        p_wqkv = wgrad3(core, after(x, r_in[0], *r_out[1:]), dq, dk, dv, sq, sv)
        keep, send = p_wqkv
        r_qkv = sum_core(here, [swap((keep, after(send, r_in[1], r_in[3])))])
        g_tok = tok_call(after(ga, r_qkv[0][0]), dq, dk, dv, place, w1)
        (k0, g0), second = r_qkv
        r_qkv = sum_plane(here, (after(k0, g_tok, r_in[2]), g0), second)
        rest = add4(r_out, [after(r_in[0], r_qkv[0][0]), *r_in[1:]])
        own, *far = sum_z(here, *r_qkv)
        over_x = move(after(rest, own), TO_X)
        own = add4([own, *far])
        [rest, over_x], [own] = tied([rest, over_x], [own])
        vectors = [(0, 128 * i, 128) for i in range(6)] + [(1, 0, nblk * 128)]
        g_wout, g_win, g_wao, g_bao, g_g1, g_s1, g_bout, g_g2, g_s2, g_bin = final_call(
            here,
            (rest, move(rest, TO_CORE), over_x, move(over_x, TO_CORE)),
            [(4, True), (nblk, False), (1, False)],
            vectors,
        )
        over_x = move(own, TO_X)
        over_x, g_wout = lax.optimization_barrier((over_x, g_wout))
        shares = (own, move(own, TO_CORE), over_x, move(over_x, TO_CORE))
        g_wqkv, g_bqv = final_call(here, shares, [(3, False)], [(0, 0, 256)])
        vecs = [v.reshape(-1) for v in (g_bqv, g_bao, g_g1, g_s1, g_bin, g_bout, g_g2, g_s2)]
    else:
        p_wao = wgrad_call("wgrad_ao", core, ctx, ga, False)
        for i in range(parts):
            state = bwd(i, state, gc)
        dq, dk, dv, sq, sv = state
        p_wqkv = [v[:, : 3 * SUB] for v in wgrad3(core, x, dq, dk, dv, sq, sv)]
        g_tok = tok_call(ga, dq, dk, dv, place, w1)
        g_wout = reduce_any(*p_wout, True)
        g_win, g_wao, g_wqkv = [reduce_any(*p, False) for p in (p_win, p_wao, p_wqkv)]
        vecs = [jnp.concatenate([sq[0], sv[0]]), sums[5], sums[3], sums[4], sbin, sums[2], sums[0], sums[1]]
        own = small_sum(jnp.concatenate([v.reshape(count, -1) for v in vecs], 1))
        vecs = [own[e - s : e] for s, e in zip(sizes, ends)]
    g_bqv, g_bao, g_g1, g_s1, g_bin, g_bout, g_g2, g_s2 = vecs
    return (
        out[None], g_tok[None], g_wqkv, g_bqv, g_wao, g_bao, g_g1, g_s1,
        g_win, g_bin, g_wout, g_bout, g_g2, g_s2,
    )


def solution(mesh):
    rows = P(("replica", "shard"), None, None)
    mat, vec = P("shard", None), P("shard")
    return jax.shard_map(
        shards,
        mesh=mesh,
        in_specs=(rows, P(("replica", "shard")), rows, mat, vec, mat, vec, vec, vec, mat, vec, mat, vec, vec, vec),
        out_specs=(rows, rows, mat, vec, mat, vec, vec, vec, mat, vec, mat, vec, vec, vec),
        check_vma=False,
    )
```

```python
import functools
import jax
import jax.numpy as jnp
from jax import lax
from jax.experimental import pallas as pl
from jax.experimental.pallas import tpu as pltpu
from jax.sharding import PartitionSpec as P

HD = 64
F32 = jnp.float32
BF = jnp.bfloat16
SQRT_HALF = 0.7071067811865476
INV_ROOT_TAU = 0.3989422804014327


def params():
    return pltpu.CompilerParams(vmem_limit_bytes=60 << 20)


def dot_nn(a, b):
    return jnp.dot(a, b, preferred_element_type=F32)


def dot_nt(a, b):
    return lax.dot_general(a, b, (((1,), (1,)), ((), ())), preferred_element_type=F32)


def dot_tn(a, b):
    return lax.dot_general(a, b, (((0,), (0,)), ((), ())), preferred_element_type=F32)


def cost(flops, nbytes, trans=0):
    return pl.CostEstimate(flops=int(flops), bytes_accessed=int(nbytes), transcendentals=int(trans))


SUB = 32
ANY = pl.BlockSpec(memory_space=pltpu.HBM)


def loads(place, bufs, lo, hi, target, sem):
    found = []
    for buf in bufs:
        for m in range(buf.shape[0]):
            i = len(found)
            found.append(pltpu.make_async_copy(buf.at[m, pl.ds(lo, hi - lo)], target(place[i]), sem.at[i]))
    return found


def start_all(copies):
    for c in copies:
        c.start()


def wait_all(copies):
    for c in copies:
        c.wait()


def qkv_body(count, place, x_ref, b_ref, *rest):
    bufs, (o_ref, w_vm, sem) = rest[:count], rest[count:]
    step = pl.program_id(0)
    blocks, width = w_vm.shape[0], w_vm.shape[-1]
    copies = loads(place, bufs, 0, blocks, lambda p: w_vm.at[:, p], sem)

    @pl.when(step == 0)
    def _():
        start_all(copies)
        wait_all(copies)

    x = x_ref[...]
    for n in range(blocks):
        w = w_vm[n].reshape(-1, width)
        bias = b_ref[:, n * width : (n + 1) * width]
        o_ref[:, n * width : (n + 1) * width] = (dot_nn(x, w) + bias).astype(BF)


def qkv_call(x, place, w1, bias, rows=256):
    slots, width = x.shape
    pieces = width // SUB
    return pl.pallas_call(
        functools.partial(qkv_body, len(w1)),
        name="qkv",
        grid_spec=pltpu.PrefetchScalarGridSpec(
            num_scalar_prefetch=1,
            grid=(slots // rows,),
            in_specs=[
                pl.BlockSpec((rows, width), lambda i, p: (i, 0)),
                pl.BlockSpec((1, 3 * width), lambda i, p: (0, 0)),
            ] + [ANY] * len(w1),
            out_specs=pl.BlockSpec((rows, 3 * width), lambda i, p: (i, 0)),
            scratch_shapes=[
                pltpu.VMEM((3, pieces, SUB, width), BF),
                pltpu.SemaphoreType.DMA((pieces,)),
            ],
        ),
        out_shape=jax.ShapeDtypeStruct((slots, 3 * width), BF),
        compiler_params=params(),
        cost_estimate=cost(6 * slots * width * width, 8 * slots * width + 6 * width * width),
    )(place, x, bias, *w1)


def lanes(rows):
    return lax.broadcasted_iota(jnp.int32, (rows, 2 * HD), 1)


def split3(v):
    hi = v.astype(BF).astype(F32)
    mid = (v - hi).astype(BF).astype(F32)
    return hi, mid, v - hi - mid


def attn_fwd_body(rows, len_ref, q_ref, k_ref, v_ref, *rest):
    ctx_ref, qa0_ref, qa1_ref = rest[-3:]
    slots = k_ref.shape[0]
    lane = lanes(slots)
    key_row = lax.broadcasted_iota(jnp.int32, (slots, 2 * HD), 0)
    bias = jnp.where(key_row < len_ref[0], 0.0, -1e30)
    k = k_ref[...].astype(F32)
    k_aug = []
    for h in range(2):
        own = (lane // HD) == h
        spare = (1 - h) * HD
        k_aug.append(jnp.where(own, k, jnp.where(lane == spare, bias, 0.0)).astype(BF))
    v_aug = [jnp.where((lane // HD) == h, v_ref[...].astype(F32), 1.0).astype(BF) for h in range(2)]
    lane_q = lanes(rows)

    def scores(item):
        blk, h = item
        q = q_ref[blk * rows : (blk + 1) * rows, :].astype(F32) * 0.125
        qh = jnp.where((lane_q // HD) == h, q, jnp.where(lane_q == (1 - h) * HD, 1.0, 0.0))
        return qh, dot_nt(qh.astype(BF), k_aug[h])

    items = [(blk, h) for blk in range(slots // rows) for h in range(2)]
    held = scores(items[0])
    outs = []
    for i, (blk, h) in enumerate(items):
        sl = slice(blk * rows, (blk + 1) * rows)
        qh, s = held
        if i + 1 < len(items):
            held = scores(items[i + 1])
        spare = (1 - h) * HD
        top = jnp.max(s, axis=-1, keepdims=True)
        o = dot_nn(jnp.exp(s - top).astype(BF), v_aug[h])
        norm = o[:, spare : spare + 1]
        outs.append(o / norm)
        hi, mid, lo = split3(-(top + jnp.log(norm)))
        qh = jnp.where(lane_q == spare + 1, hi, qh)
        qh = jnp.where(lane_q == spare + 2, mid, qh)
        qh = jnp.where(lane_q == spare + 3, lo, qh)
        (qa0_ref, qa1_ref)[h][sl, :] = qh.astype(BF)
        if h == 1:
            ctx_ref[sl, :] = jnp.where(lane_q < HD, outs[-2], outs[-1]).astype(BF)


def attn_fwd_call(qkv, lengths, part, parts, before, rows=256):
    slots, wide = qkv.shape
    width = wide // 3
    pairs = width // (2 * HD)
    each = pairs // parts
    col = lambda off: pl.BlockSpec((slots, 2 * HD), lambda j, ln: (0, off * pairs + part * each + j))
    out = jax.ShapeDtypeStruct((slots, width), BF)
    extra = list(before or ())
    return pl.pallas_call(
        functools.partial(attn_fwd_body, rows),
        name=f"attn_fwd{part}",
        grid_spec=pltpu.PrefetchScalarGridSpec(
            num_scalar_prefetch=1,
            grid=(each,),
            in_specs=[col(0), col(1), col(2)] + [ANY] * len(extra),
            out_specs=[col(0)] * 3,
        ),
        out_shape=[out, out, out],
        input_output_aliases={4 + i: i for i in range(3)} if before else {},
        compiler_params=params(),
        cost_estimate=cost(
            16 * slots * slots * width / parts, 12 * slots * width / parts, slots * slots * 2 * each
        ),
    )(lengths, qkv, qkv, qkv, *extra)


def attn_bwd_body(rows, len_ref, qa0_ref, qa1_ref, k_ref, v_ref, ctx_ref, g_ref, *rest):
    dq_ref, dk_ref, dv_ref, sq_ref, sv_ref = rest[-5:]
    slots = k_ref.shape[0]
    lane = lanes(slots)
    key_row = lax.broadcasted_iota(jnp.int32, (slots, 2 * HD), 0)
    bias = jnp.where(key_row < len_ref[0], 0.0, -1e30)
    k = k_ref[...].astype(F32)
    v = v_ref[...].astype(F32)
    k_low = k_ref[...]
    k_aug, v_aug = [], []
    for h in range(2):
        own = (lane // HD) == h
        spare = (1 - h) * HD
        near = (lane > spare) & (lane < spare + 4)
        ones = jnp.where(near, 1.0, 0.0)
        k_aug.append(jnp.where(own, k, jnp.where(lane == spare, bias, ones)).astype(BF))
        v_aug.append(jnp.where(own, v, ones).astype(BF))
    lane_q = lanes(rows)
    items = [(blk, h) for blk in range(slots // rows) for h in range(2)]

    def products(item):
        blk, h = item
        sl = slice(blk * rows, (blk + 1) * rows)
        own = (lane_q // HD) == h
        spare = (1 - h) * HD
        g = g_ref[sl, :].astype(F32)
        delta = jnp.sum(jnp.where(own, g * ctx_ref[sl, :].astype(F32), 0.0), axis=-1, keepdims=True)
        hi, mid, lo = split3(-delta)
        ga = jnp.where(own, g, 0.0)
        ga = jnp.where(lane_q == spare + 1, hi, ga)
        ga = jnp.where(lane_q == spare + 2, mid, ga)
        ga = jnp.where(lane_q == spare + 3, lo, ga).astype(BF)
        return dot_nt(k_aug[h], (qa0_ref, qa1_ref)[h][sl, :]), dot_nt(v_aug[h], ga)

    held = products(items[0])
    dk = [jnp.zeros((slots, 2 * HD), F32)] * 2
    dv = [jnp.zeros((slots, 2 * HD), F32)] * 2
    dqs = []
    for i, (blk, h) in enumerate(items):
        sl = slice(blk * rows, (blk + 1) * rows)
        s, gs = held
        if i + 1 < len(items):
            held = products(items[i + 1])
        p = jnp.exp(s)
        ds = (p * gs).astype(BF)
        dv[h] = dv[h] + dot_nn(p.astype(BF), g_ref[sl, :])
        dk[h] = dk[h] + dot_nn(ds, (qa0_ref, qa1_ref)[h][sl, :])
        dqs.append(dot_tn(ds, k_low))
        if h == 1:
            dq_ref[sl, :] = (jnp.where(lane_q < HD, dqs[-2], dqs[-1]) * 0.125).astype(BF)
    dk_ref[...] = jnp.where(lane < HD, dk[0], dk[1]).astype(BF)
    dv_low = jnp.where(lane < HD, dv[0], dv[1]).astype(BF)
    dv_ref[...] = dv_low
    sq_ref[...] = jnp.sum(dq_ref[...].astype(F32), axis=0, keepdims=True)
    sv_ref[...] = jnp.sum(dv_low.astype(F32), axis=0, keepdims=True)


def attn_bwd_call(qa0, qa1, qkv, ctx, grad_ctx, lengths, part, parts, before, rows=256):
    slots, width = ctx.shape
    pairs = width // (2 * HD)
    each = pairs // parts
    col = lambda off: pl.BlockSpec((slots, 2 * HD), lambda j, ln: (0, off * pairs + part * each + j))
    row = pl.BlockSpec((1, 2 * HD), lambda j, ln: (0, part * each + j))
    out = jax.ShapeDtypeStruct((slots, width), BF)
    vec = jax.ShapeDtypeStruct((1, width), F32)
    extra = list(before or ())
    return pl.pallas_call(
        functools.partial(attn_bwd_body, rows),
        name=f"attn_bwd{part}",
        grid_spec=pltpu.PrefetchScalarGridSpec(
            num_scalar_prefetch=1,
            grid=(each,),
            in_specs=[col(0), col(0), col(1), col(2), col(0), col(0)] + [ANY] * len(extra),
            out_specs=[col(0)] * 3 + [row] * 2,
        ),
        out_shape=[out, out, out, vec, vec],
        input_output_aliases={7 + i: i for i in range(5)} if before else {},
        compiler_params=params(),
        cost_estimate=cost(
            40 * slots * slots * width / parts, 18 * slots * width / parts, slots * slots * 2 * each
        ),
    )(lengths, qa0, qa1, qkv, qkv, ctx, grad_ctx, *extra)


def norm_stats(resid):
    mean = jnp.mean(resid, axis=-1, keepdims=True)
    centred = resid - mean
    inv = lax.rsqrt(jnp.mean(centred * centred, axis=-1, keepdims=True) + 1e-5)
    return centred * inv, inv


def norm_back(u, normed, inv):
    return inv * (u - jnp.mean(u, axis=-1, keepdims=True) - normed * jnp.mean(u * normed, axis=-1, keepdims=True))


def colsum(v):
    return jnp.sum(v, axis=0, keepdims=True)


def row_body(n2, len_ref, place, x_ref, ctx_ref, cot_ref, vec_ref, bin_ref, *rest):
    b2 = rest[:n2]
    (
        out_ref, act_ref, hid_ref, gf_ref, gp_ref, ga_ref, gc_ref, sums_ref, sbin_ref,
        wa, wi, wo, slope, sem,
    ) = rest[n2:]
    step = pl.program_id(0)
    rows, width = x_ref.shape
    nblk = wi.shape[0]
    copies = [
        loads(place, b2, 0, 1, lambda p: wa.at[pl.ds(p, 1)], sem.at[0]),
        loads(place, b2, 1, 1 + nblk, lambda p: wi.at[:, p], sem.at[1]),
        loads(place, b2, 1 + nblk, 5 + nblk, lambda p: wo.at[p], sem.at[2]),
    ]

    @pl.when(step == 0)
    def _():
        for c in copies:
            start_all(c)
        sums_ref[...] = jnp.zeros_like(sums_ref)
        sbin_ref[...] = jnp.zeros_like(sbin_ref)

    def ready(i):
        @pl.when(step == 0)
        def _():
            wait_all(copies[i])

    bao, gain1, shift1, bout, gain2, shift2 = [vec_ref[i : i + 1, :] for i in range(6)]
    ready(0)
    w_ao = wa[...].reshape(width, width)
    resid1 = x_ref[...].astype(F32) + dot_nn(ctx_ref[...], w_ao) + bao
    normed1, inv1 = norm_stats(resid1)
    hidden = normed1 * gain1 + shift1
    low = hidden.astype(BF)
    hid_ref[...] = low
    acc = jnp.zeros((rows, width), F32)
    per = wo.shape[0] // nblk
    ready(1)
    for n in range(nblk):
        pre = dot_nn(low, wi[n].reshape(width, width)) + bin_ref[n : n + 1, :]
        phi = 0.5 + 0.5 * lax.erf(pre * SQRT_HALF)
        slope[n] = (phi + pre * (INV_ROOT_TAU * jnp.exp(-0.5 * pre * pre))).astype(slope.dtype)
        act = (pre * phi).astype(BF)
        act_ref[:, n * width : (n + 1) * width] = act
        if n == 0:
            ready(2)
        acc = acc + dot_nn(act, wo[n * per : (n + 1) * per].reshape(width, width))
    resid2 = hidden + acc + bout
    normed2, inv2 = norm_stats(resid2)
    row_id = lax.broadcasted_iota(jnp.int32, (rows, 1), 0) + step * rows
    valid = (row_id < len_ref[0]).astype(F32)
    out_ref[...] = ((normed2 * gain2 + shift2) * valid).astype(BF)
    gz = cot_ref[...].astype(F32) * valid
    sums_ref[0:1, :] += colsum(gz * normed2)
    sums_ref[1:2, :] += colsum(gz)
    g_resid2 = norm_back(gz * gain2, normed2, inv2)
    gf = g_resid2.astype(BF)
    gf_ref[...] = gf
    sums_ref[2:3, :] += colsum(gf.astype(F32))
    acc = g_resid2
    for n in range(nblk):
        g_act = dot_nt(gf, wo[n * per : (n + 1) * per].reshape(width, width))
        gp = (g_act * slope[n].astype(F32)).astype(BF)
        gp_ref[:, n * width : (n + 1) * width] = gp
        sbin_ref[n : n + 1, :] += colsum(gp.astype(F32))
        acc = acc + dot_nt(gp, wi[n].reshape(width, width))
    sums_ref[3:4, :] += colsum(acc * normed1)
    sums_ref[4:5, :] += colsum(acc)
    g_attn = norm_back(acc * gain1, normed1, inv1).astype(BF)
    ga_ref[...] = g_attn
    sums_ref[5:6, :] += colsum(g_attn.astype(F32))
    gc_ref[...] = dot_nt(g_attn, w_ao).astype(BF)


def row_call(x, ctx, cot, place, w2, vecs, b_in, lengths, rows=256):
    slots, width = x.shape
    pieces, sub = width // SUB, SUB
    nblk = b_in.shape[0]
    ff = nblk * width
    blk = pl.BlockSpec((rows, width), lambda i, ln, p: (i, 0))
    big = pl.BlockSpec((rows, ff), lambda i, ln, p: (i, 0), pipeline_mode=pl.Buffered(1 if rows > 256 else 2))
    const = lambda r: pl.BlockSpec((r, width), lambda i, ln, p: (0, 0))
    o = jax.ShapeDtypeStruct((slots, width), BF)
    ob = jax.ShapeDtypeStruct((slots, ff), BF)
    return pl.pallas_call(
        functools.partial(row_body, len(w2)),
        name="row_local",
        grid_spec=pltpu.PrefetchScalarGridSpec(
            num_scalar_prefetch=2,
            grid=(slots // rows,),
            in_specs=[blk, blk, blk, const(8), const(nblk)] + [ANY] * len(w2),
            out_specs=[blk, big, blk, blk, big, blk, blk, const(8), const(nblk)],
            scratch_shapes=[
                pltpu.VMEM((pieces, sub, width), BF),
                pltpu.VMEM((nblk, pieces, sub, width), BF),
                pltpu.VMEM((pieces, 4, sub, width), BF),
                pltpu.VMEM((nblk, rows, width), BF),
                pltpu.SemaphoreType.DMA((3, pieces)),
            ],
        ),
        out_shape=[
            o, ob, o, o, ob, o, o,
            jax.ShapeDtypeStruct((8, width), F32),
            jax.ShapeDtypeStruct((nblk, width), F32),
        ],
        compiler_params=params(),
        cost_estimate=cost(36 * slots * width * width, 40 * slots * width + 18 * width * width, 2 * slots * ff),
    )(lengths, place, x, ctx, cot, vecs, b_in, *w2)


def halves(core, value, keep_ref, send_ref):
    count, rows, width = keep_ref.shape
    value = value.reshape(count, 2, rows, width)
    even, odd = value[:, 0], value[:, 1]

    @pl.when(core == 0)
    def _():
        keep_ref[...] = even
        send_ref[...] = odd

    @pl.when(core != 0)
    def _():
        keep_ref[...] = odd
        send_ref[...] = even


LINES = 16


def lines_of(*lines):
    width, segments = lines[0][0], [line[1:] for line in lines]
    row = lax.broadcasted_iota(jnp.int32, (LINES, width), 0)
    value = jnp.zeros((LINES, width), F32)
    for i, segs in enumerate(segments):
        used = sum(v.shape[1] for v in segs)
        line = jnp.concatenate(segs + [jnp.zeros((1, width - used), F32)] * (used < width), 1)
        value = jnp.where(row == i, line, value)
    return value.astype(BF)


def wgrad_body(core, a_ref, b_ref, keep_ref, send_ref):
    halves(core[0], dot_tn(a_ref[...], b_ref[...]).astype(BF), keep_ref, send_ref)


def wgrad_call(name, core, a, b, by_rows, tile=1024):
    slots, m = a.shape
    width = a.shape[1] if not by_rows else b.shape[1]
    blocks = m // width if by_rows else b.shape[1] // m
    pieces = width // SUB
    if by_rows:
        grid = (1, m // tile)
        block = (tile // (2 * SUB * blocks), blocks * SUB, width)
        where = lambda j, i, c: (i, 0, 0)
    else:
        grid = (blocks, m // tile)
        block = (tile // (2 * SUB), SUB, width)
        where = lambda j, i, c: (i, j, 0)
    out = jax.ShapeDtypeStruct((pieces // 2, blocks * SUB, width), BF)
    return pl.pallas_call(
        wgrad_body,
        name=name,
        grid_spec=pltpu.PrefetchScalarGridSpec(
            num_scalar_prefetch=1,
            grid=grid,
            in_specs=[
                pl.BlockSpec((slots, tile), lambda j, i, c: (0, i)),
                pl.BlockSpec((slots, width), lambda j, i, c: (0, j)),
            ],
            out_specs=[pl.BlockSpec(block, where)] * 2,
        ),
        out_shape=[out, out],
        compiler_params=params(),
        cost_estimate=cost(2 * slots * m * b.shape[1], 2 * (slots * (m + b.shape[1]) + m * b.shape[1])),
    )(core, a, b)


def wgrad_ao_body(core, a_ref, b_ref, sums_ref, sbin_ref, keep_ref, send_ref):
    value = dot_tn(a_ref[...], b_ref[...]).astype(BF)
    halves(core[0], value, keep_ref.at[:, pl.ds(0, SUB)], send_ref.at[:, pl.ds(0, SUB)])
    count, _, width = keep_ref.shape
    owners = count // 2
    part, four = width // owners, sbin_ref.shape[0] * width // owners
    for s in range(owners):
        segs = [sums_ref[v : v + 1, s * part : (s + 1) * part] for v in (5, 3, 4, 2, 0, 1)]
        row, col = s * four // width, s * four % width
        value = lines_of([width, *segs], [width, sbin_ref[row : row + 1, col : col + four]])
        for ref in (keep_ref, send_ref):
            for x in (0, 1):
                ref[2 * s + x, SUB : SUB + LINES] = value


def wgrad_ao(core, a, b, sums, sbin):
    slots, m = a.shape
    full = lambda v: pl.BlockSpec(v.shape, lambda t, c: (0, 0))
    shape = (m // SUB // 2, SUB + LINES, m)
    return pl.pallas_call(
        wgrad_ao_body,
        name="wgrad_ao",
        grid_spec=pltpu.PrefetchScalarGridSpec(
            num_scalar_prefetch=1,
            grid=(1,),
            in_specs=[full(v) for v in (a, b, sums, sbin)],
            out_specs=[pl.BlockSpec(shape, lambda t, c: (0, 0, 0))] * 2,
        ),
        out_shape=[jax.ShapeDtypeStruct(shape, BF)] * 2,
        compiler_params=params(),
        cost_estimate=cost(2 * slots * m * m, 4 * slots * m + 2 * m * m),
    )(core, a, b, sums, sbin)


def wgrad3_body(core, a_ref, q_ref, k_ref, v_ref, sq_ref, sv_ref, keep_ref, send_ref):
    for n, ref in enumerate((q_ref, k_ref, v_ref)):
        value = dot_tn(a_ref[...], ref[...]).astype(BF)
        rows = pl.ds(n * SUB, SUB)
        halves(core[0], value, keep_ref.at[:, rows], send_ref.at[:, rows])
    count, _, width = keep_ref.shape
    line = jnp.where(pl.program_id(0) == 0, sq_ref[...], sv_ref[...])
    part = 2 * width // count
    for s in range(count // 2):
        value = lines_of([width, line[:, s * part : (s + 1) * part]])
        for ref in (keep_ref, send_ref):
            for x in (0, 1):
                ref[2 * s + x, 3 * SUB : 3 * SUB + LINES] = value


def wgrad3(core, a, dq, dk, dv, sq, sv):
    slots, m = a.shape
    tile = m // 2
    full = pl.BlockSpec((slots, m), lambda i, c: (0, 0))
    vec = pl.BlockSpec((1, m), lambda i, c: (0, 0))
    block = pl.BlockSpec((tile // (2 * SUB), 3 * SUB + LINES, m), lambda i, c: (i, 0, 0))
    out = jax.ShapeDtypeStruct((m // SUB // 2, 3 * SUB + LINES, m), BF)
    return pl.pallas_call(
        wgrad3_body,
        name="wgrad_qkv",
        grid_spec=pltpu.PrefetchScalarGridSpec(
            num_scalar_prefetch=1,
            grid=(2,),
            in_specs=[pl.BlockSpec((slots, tile), lambda i, c: (0, i)), full, full, full, vec, vec],
            out_specs=[block, block],
        ),
        out_shape=[out, out],
        compiler_params=params(),
        cost_estimate=cost(6 * slots * m * m, 14 * slots * m),
    )(core, a, dq, dk, dv, sq, sv)


def tok_body(count, place, g_ref, dq_ref, dk_ref, dv_ref, *rest):
    bufs, (o_ref, w_vm, sem) = rest[:count], rest[count:]
    step = pl.program_id(0)
    width = g_ref.shape[1]
    copies = loads(place, bufs, 0, 3, lambda p: w_vm.at[:, p], sem)

    @pl.when(step == 0)
    def _():
        start_all(copies)
        wait_all(copies)

    acc = g_ref[...].astype(F32)
    for n, ref in enumerate((dq_ref, dk_ref, dv_ref)):
        acc = acc + dot_nt(ref[...], w_vm[n].reshape(width, width))
    o_ref[...] = acc.astype(BF)


def tok_call(g, dq, dk, dv, place, w1, rows=256):
    slots, width = g.shape
    pieces = width // SUB
    blk = pl.BlockSpec((rows, width), lambda i, p: (i, 0))
    return pl.pallas_call(
        functools.partial(tok_body, len(w1)),
        name="grad_tok",
        grid_spec=pltpu.PrefetchScalarGridSpec(
            num_scalar_prefetch=1,
            grid=(slots // rows,),
            in_specs=[blk, blk, blk, blk] + [ANY] * len(w1),
            out_specs=blk,
            scratch_shapes=[pltpu.VMEM((3, pieces, SUB, width), BF), pltpu.SemaphoreType.DMA((pieces,))],
        ),
        out_shape=jax.ShapeDtypeStruct((slots, width), BF),
        compiler_params=params(),
        cost_estimate=cost(6 * slots * width * width, 16 * slots * width),
    )(place, g, dq, dk, dv, *w1)


def total(*terms):
    acc = terms[0].astype(F32)
    for t in terms[1:]:
        acc = acc + t.astype(F32)
    return acc.astype(BF)


def add1_body(count, here, *refs):
    ins, outs = refs[: 8 * count], refs[8 * count :]
    for view in range(4):
        n0 = 0
        for i in range(count):
            a, b = ins[8 * i + 2 * view], ins[8 * i + 2 * view + 1]
            n = a.shape[3]
            outs[view][0, n0 : n0 + n] = total(a[0, 0, 0], b[0, 0, 0])
            n0 += n


def add1(here, pairs):
    width = pairs[0][0].shape[-1]
    views = []
    for half, own in ((0, 0), (0, 1), (1, 0), (1, 1)):
        def where(t, h, half=half, own=own):
            z, j = 2 * half + t // 2, t % 2
            if half == 0:
                return (z, j, h[0] if own else 1 - h[0], 0, 0)
            return (z, h[1] if own else 1 - h[1], j, 0, 0)
        views.append(where)
    specs, args, rows = [], [], 0
    for keep, got in pairs:
        n = keep.shape[1]
        rows += n
        for where in views:
            for arr in (keep, got):
                specs.append(pl.BlockSpec((1, 1, 1, n, width), where))
                args.append(arr.reshape(4, 2, 2, n, width))
    out = jax.ShapeDtypeStruct((4, rows, width), BF)
    return pl.pallas_call(
        functools.partial(add1_body, len(pairs)),
        name="add_core",
        grid_spec=pltpu.PrefetchScalarGridSpec(
            num_scalar_prefetch=1,
            grid=(4,),
            in_specs=specs,
            out_specs=[pl.BlockSpec((1, rows, width), lambda t, h: (t, 0, 0))] * 4,
        ),
        out_shape=[out] * 4,
        compiler_params=params(),
        cost_estimate=cost(16 * rows * width, 96 * rows * width),
    )(here, *args)


def add2_body(here, *refs):
    ins, outs = refs[:8], refs[8:]
    for view in range(4):
        outs[view][0] = total(ins[2 * view][0, 0], ins[2 * view + 1][0, 0])


def add2(here, first, second):
    _, rows, width = first[0].shape
    specs, args = [], []
    for axis, pair in ((1, first), (0, second)):
        for own in (0, 1):
            for arr in pair:
                specs.append(pl.BlockSpec(
                    (1, 1, rows, width),
                    lambda t, h, axis=axis, own=own: (t, h[axis] if own else 1 - h[axis], 0, 0),
                ))
                args.append(arr.reshape(2, 2, rows, width))
    out = jax.ShapeDtypeStruct((2, rows, width), BF)
    return pl.pallas_call(
        add2_body,
        name="add_plane",
        grid_spec=pltpu.PrefetchScalarGridSpec(
            num_scalar_prefetch=1,
            grid=(2,),
            in_specs=specs,
            out_specs=[pl.BlockSpec((1, rows, width), lambda t, h: (t, 0, 0))] * 4,
        ),
        out_shape=[out] * 4,
        compiler_params=params(),
        cost_estimate=cost(8 * rows * width, 48 * rows * width),
    )(here, *args)


def add3_body(here, ak, ag, bk, bg, *outs):
    for k, out in enumerate(outs):
        to = lax.rem(here[2] + k, 4)
        spot = lax.rem(to, 2)

        @pl.when(to < 2)
        def _():
            out[0] = total(ak[spot], ag[spot])

        @pl.when(to >= 2)
        def _():
            out[0] = total(bk[spot], bg[spot])


def add3(here, first, second):
    _, rows, width = first[0].shape
    full = pl.BlockSpec((2, rows, width), lambda t, h: (0, 0, 0))
    one = pl.BlockSpec((1, rows, width), lambda t, h: (0, 0, 0))
    return pl.pallas_call(
        add3_body,
        name="add_z",
        grid_spec=pltpu.PrefetchScalarGridSpec(
            num_scalar_prefetch=1, grid=(1,), in_specs=[full] * 4, out_specs=[one] * 4,
        ),
        out_shape=[jax.ShapeDtypeStruct((1, rows, width), BF)] * 4,
        compiler_params=params(),
        cost_estimate=cost(4 * rows * width, 24 * rows * width),
    )(here, *first, *second)


def add4_body(*refs):
    ins, out = refs[:-1], refs[-1]
    n0 = 0
    for i in range(0, len(ins), 4):
        n = ins[i].shape[1]
        out[:, n0 : n0 + n] = total(*[r[...] for r in ins[i : i + 4]])
        n0 += n


def add4(*groups):
    spec = lambda shape: pl.BlockSpec(shape, lambda t: (0,) * len(shape))
    width = groups[0][0].shape[-1]
    shape = (1, sum(g[0].shape[1] for g in groups), width)
    parts = [v for g in groups for v in g]
    size = shape[1] * width
    return pl.pallas_call(
        add4_body,
        name="add_last",
        grid=(1,),
        in_specs=[spec(v.shape) for v in parts],
        out_specs=spec(shape),
        out_shape=jax.ShapeDtypeStruct(shape, BF),
        compiler_params=params(),
        cost_estimate=cost(3 * size, 10 * size),
    )(*parts)


def final_body(kinds, vectors, here, own, core, over_x, both, *outs):
    mine_at = 2 * here[0] + here[3]
    mats, vecs = outs[: len(kinds)], outs[len(kinds) :]
    for flip, ref in enumerate((own, core, over_x, both)):
        share = jnp.bitwise_xor(mine_at, flip)
        n0 = 0
        for (blocks, by_rows), out in zip(kinds, mats):
            width = ref.shape[-1]
            for n in range(blocks):
                value = ref[0, n0 : n0 + SUB].astype(F32)
                n0 += SUB
                if by_rows:
                    out[pl.ds(pl.multiple_of(share * blocks * SUB, SUB) + n * SUB, SUB), :] = value
                else:
                    out[pl.ds(pl.multiple_of(share * SUB, SUB), SUB), n * width : (n + 1) * width] = value

        @pl.when(share == 0)
        def _():
            lines = ref[0, n0 : n0 + LINES].astype(F32)
            for (row, lane, size), out in zip(vectors, vecs):
                out[...] = lines[row : row + 1, lane : lane + size]


def final_call(here, parts, kinds, vectors):
    shape = parts[0].shape
    width = shape[-1]
    shapes = [
        (4 * blocks * SUB, width) if by_rows else (4 * SUB, blocks * width) for blocks, by_rows in kinds
    ] + [(1, size) for _, _, size in vectors]
    return pl.pallas_call(
        functools.partial(final_body, kinds, vectors),
        name="final",
        grid_spec=pltpu.PrefetchScalarGridSpec(
            num_scalar_prefetch=1,
            grid=(1,),
            in_specs=[pl.BlockSpec(shape, lambda t, h: (0, 0, 0))] * 4,
            out_specs=[pl.BlockSpec(sh, lambda t, h: (0, 0)) for sh in shapes],
        ),
        out_shape=[jax.ShapeDtypeStruct(sh, F32) for sh in shapes],
        compiler_params=params(),
        cost_estimate=cost(1, 24 * parts[0].size),
    )(here, *parts)


BOTH = ("shard", "replica")
AXES = ("replica", "shard")


def table(fn):
    pairs = []
    for r in range(4):
        for s in range(8):
            x, y, z, c = fn(r // 2, s % 2, s // 2, r % 2)
            pairs.append((r * 8 + s, (x * 2 + c) * 8 + z * 2 + y))
    return pairs


TO_CORE = table(lambda x, y, z, c: (x, y, z, 1 - c))
TO_X = table(lambda x, y, z, c: (1 - x, y, z, c))
TO_XCORE = table(lambda x, y, z, c: (1 - x, y, z, 1 - c))
TO_Y = table(lambda x, y, z, c: (x, 1 - y, z, c))
TO_Z = [table(lambda x, y, z, c, k=k: (x, y, (z + k) % 4, c)) for k in range(4)]


def move(v, pairs):
    return lax.ppermute(v, AXES, pairs)


def regular():
    return lax.axis_size("shard") == 8 and lax.axis_size("replica") == 4


def place_of():
    r, s = lax.axis_index("replica"), lax.axis_index("shard")
    return r // 2, s % 2, s // 2, r % 2


def pack_body(share, *refs):
    ins, out = refs[:-1], refs[-1]
    width = out.shape[-1]
    n0 = 0
    for ref in ins:
        rows, cols = ref.shape
        if rows > SUB:
            out[0, n0 : n0 + rows // SUB] = ref[...].reshape(rows // SUB, SUB, width)
            n0 += rows // SUB
        else:
            for n in range(cols // width):
                out[0, n0 + n] = ref[:, n * width : (n + 1) * width]
            n0 += cols // width


def pack(share, mats, width):
    shapes = [(m.shape[0] // 4, m.shape[1]) for m in mats]
    blocks = sum(r * c for r, c in shapes) // (SUB * width)
    return pl.pallas_call(
        pack_body,
        name="pack",
        grid_spec=pltpu.PrefetchScalarGridSpec(
            num_scalar_prefetch=1,
            grid=(1,),
            in_specs=[pl.BlockSpec(sh, lambda t, r: (r[0], 0)) for sh in shapes],
            out_specs=pl.BlockSpec((1, blocks, SUB, width), lambda t, r: (0, 0, 0, 0)),
        ),
        out_shape=jax.ShapeDtypeStruct((1, blocks, SUB, width), BF),
        compiler_params=params(),
        cost_estimate=cost(1, 4 * blocks * SUB * width),
    )(share, *mats)


def pack_first_body(share, w_ref, *refs):
    vecs, out = refs[:-1], refs[-1]
    rows, width = 3 * SUB, out.shape[-1]
    for n in range(3):
        out[0, n * SUB : (n + 1) * SUB] = w_ref[:, n * width : (n + 1) * width]
    segs = [v[...].astype(F32) for v in vecs]
    out[0, rows : rows + LINES] = lines_of([width, *segs[:-1]], [width, segs[-1]])


def pack_first(share, w_qkv, vecs, width):
    rows = w_qkv.shape[0] // 4
    vecs = [v.reshape(1, -1) for v in vecs]
    shape = (1, 3 * rows + LINES, width)
    return pl.pallas_call(
        pack_first_body,
        name="pack_first",
        grid_spec=pltpu.PrefetchScalarGridSpec(
            num_scalar_prefetch=1,
            grid=(1,),
            in_specs=[pl.BlockSpec((rows, 3 * width), lambda t, r: (r[0], 0))]
            + [pl.BlockSpec(v.shape, lambda t, r: (0, 0)) for v in vecs],
            out_specs=pl.BlockSpec(shape, lambda t, r: (0, 0, 0)),
        ),
        out_shape=jax.ShapeDtypeStruct(shape, BF),
        compiler_params=params(),
        cost_estimate=cost(1, 12 * rows * width),
    )(share, w_qkv, *vecs)


def after(v, *deps):
    return lax.optimization_barrier((v,) + deps)[0]


def to_core(bufs):
    return [move(v, TO_CORE) for v in bufs]


def tied(*groups):
    flat = lax.optimization_barrier([v for g in groups for v in g])
    out = []
    for g in groups:
        out.append(flat[: len(g)])
        flat = flat[len(g) :]
    return out


def gather_places(order):
    x, y, z, c = place_of()
    spots = []
    for fc in (0, 1):
        for k, fx, fy in order:
            spots.append((((z - k) % 4) * 2 + (y ^ fy)) * 4 + (x ^ fx) * 2 + (c ^ fc))
    return jnp.stack(spots).astype(jnp.int32)


FIRST = [
    (k0 + k, fx, fy)
    for k0, fx, fy in ((0, 0, 0), (2, 0, 0), (0, 0, 1), (2, 1, 0), (0, 1, 0), (2, 0, 1), (0, 1, 1), (2, 1, 1))
    for k in (0, 1)
]
SECOND = [
    (0, 0, 0), (0, 1, 0), (1, 0, 0), (3, 0, 0), (2, 0, 0), (0, 0, 1), (1, 1, 0), (3, 1, 0),
    (1, 0, 1), (3, 0, 1), (2, 1, 0), (0, 1, 1), (2, 0, 1), (3, 1, 1), (1, 1, 1), (2, 1, 1),
]


def spread(w, blocks, wide):
    full = lax.all_gather(w, "shard", axis=0, tiled=True)
    if full.shape[1] == wide:
        return full.reshape(-1, blocks, SUB, wide)
    return full.reshape(-1, SUB, blocks, wide).transpose(0, 2, 1, 3)


def sum_core(here, pairs):
    a_send, a_keep, b_send, b_keep = add1(here, pairs)
    return (a_keep, move(a_send, TO_X)), (b_keep, move(b_send, TO_Y))


def sum_plane(here, first, second):
    a_send, a_keep, b_send, b_keep = add2(here, first, second)
    return (a_keep, move(a_send, TO_Y)), (b_keep, move(b_send, TO_X))


def sum_z(here, first, second):
    own, *sends = add3(here, first, second)
    return [own] + [move(v, TO_Z[k + 1]) for k, v in enumerate(sends)]


def small_gather(lines):
    x, y, z, c = place_of()
    rows = jnp.concatenate([lines, move(lines, TO_Y)], 0)
    spots = jnp.stack([((z - k) % 4) * 2 + (y ^ f) for f in (0, 1) for k in range(4)])
    pick = (jnp.arange(8)[:, None] == spots[None, :]).astype(BF)
    return dot_nn(pick, rows)


def small_sum(rows):
    return lax.dynamic_index_in_dim(lax.psum(rows, BOTH), lax.axis_index("shard"), 0, keepdims=False)


def reduce_any(keep, send, by_rows):
    half, rows, wide = keep.shape
    full = jnp.stack([keep, send], 1).reshape(2 * half, rows // SUB, SUB, wide)
    full = full.reshape(-1, wide) if by_rows else full.transpose(0, 2, 1, 3).reshape(2 * half * SUB, -1)
    part = lax.psum_scatter(full, "shard", scatter_dimension=0, tiled=True)
    return lax.psum(part, "replica").astype(F32)


def shards(
    tokens, lengths, cotangent, w_qkv, b_qv, w_attn_out, b_attn_out, ln1_gain, ln1_bias,
    w_ffn_in, b_ffn_in, w_ffn_out, b_ffn_out, ln2_gain, ln2_bias,
):
    _, slots, width = tokens.shape
    nblk = w_ffn_in.shape[1] // width
    count = lax.axis_size("shard")
    x = tokens.reshape(slots, width)
    cot = cotangent.reshape(slots, width)
    small = [b_qv, b_attn_out, ln1_gain, ln1_bias, b_ffn_out, ln2_gain, ln2_bias, b_ffn_in]
    sizes = [v.shape[0] for v in small]
    ends = [sum(sizes[: i + 1]) for i in range(len(sizes))]

    if regular():
        share = lax.axis_index("replica").reshape(1).astype(jnp.int32)
        first = pack_first(share, w_qkv, small, width)
        second = pack(share, [after(w_attn_out, first), w_ffn_in, w_ffn_out], width)
        xo, yo = move(second, TO_X), move(second, TO_Y)
        along = [first] + [move(first, TO_Z[k]) for k in (1, 2, 3)]
        *along, xo, yo = lax.optimization_barrier((*along, xo, yo))
        a1, b1 = [
            jnp.concatenate([v[:, : 3 * SUB] for v in pair], 0).reshape(2, 3, SUB, width)
            for pair in (along[:2], along[2:])
        ]
        lines = jnp.concatenate([v[:, 3 * SUB : 3 * SUB + 2] for v in along], 0)
        rows = small_gather(lines.reshape(4, 2 * width)[:, : ends[-1]])
        second = after(second, along[3])
        near, *far = [move(second, TO_Z[k]) for k in (1, 2, 3)]
        plane = [move(a1, TO_Y), move(b1, TO_X), move(a1, TO_X), move(b1, TO_Y)]
        first = [a1, b1]
        cores = to_core(first)
        plane, cores = tied(plane, cores)
        last = [move(plane[0], TO_X), move(plane[1], TO_Y)]
        more = to_core(plane)
        _, [near, far[1]] = tied(last, [near, far[1]])
        w1 = [*first, *plane, *last, *cores, *more, *to_core(last)]
        r13 = jnp.concatenate([near, far[1]], 0)
        x1, y1 = move(r13, TO_X), move(r13, TO_Y)
        place, place2 = gather_places(FIRST), gather_places(SECOND)
        here = jnp.stack(place_of()).astype(jnp.int32)
    else:
        w1 = [spread(w_qkv, 3, width)]
        w2 = [spread(w_attn_out, 1, width), spread(w_ffn_in, nblk, width), spread(w_ffn_out, 4, width)]
        w2 = [jnp.concatenate(w2, 1)]
        place = place2 = jnp.arange(width // SUB, dtype=jnp.int32)
        here = jnp.zeros((4,), jnp.int32)
    core = here[3:]

    if not regular():
        rows = lax.all_gather(jnp.concatenate(small), "shard", axis=0).astype(F32)
    b_qv, bao, gain1, shift1, bout, gain2, shift2, b_in = [
        rows[:, e - s : e].reshape(-1) for s, e in zip(sizes, ends)
    ]
    bias3 = jnp.concatenate([b_qv[:width], jnp.zeros((width,), F32), b_qv[width:]]).reshape(1, -1)
    zero = jnp.zeros((width,), F32)
    vecs = jnp.stack([bao, gain1, shift1, bout, gain2, shift2, zero, zero])

    qkv = qkv_call(x, place, w1, bias3)
    parts = 4
    fwd = lambda i, state: attn_fwd_call(qkv, lengths, i, parts, state)
    state = fwd(0, None)
    if regular():
        [r2], [x1, y1], state = tied([far[0]], [x1, y1], state)
        c2 = jnp.concatenate([r2, yo], 0)
        x2, y2 = move(c2, TO_X), move(jnp.concatenate([r2, x1[1:]], 0), TO_Y)
        cores = to_core([second, xo, r13, x1, y1])
        state = fwd(1, state)
        cores, state = tied(cores, state)
        state = fwd(2, state)
        [x2, y2], state = tied([x2, y2], state)
        x3, y3 = move(y1[:1], TO_X), move(x2[:1], TO_Y)
        more = to_core([c2, x2, y2])
        more, state = tied(more, state)
        state = fwd(3, state)
        last, state = tied([x3, y3], state)
        w2 = [second, xo, r13, c2, x1, y1, x2, y2, *last]
        w2 += [*cores[:3], more[0], *cores[3:], *more[1:], *to_core(last)]
    else:
        for i in range(1, parts):
            state = fwd(i, state)
    ctx, qa0, qa1 = state
    out, act, low, gf, gp, ga, gc, sums, sbin = row_call(
        x, ctx, cot, place2, w2, vecs, b_in.reshape(nblk, width), lengths
    )
    p_wout = wgrad_call("wgrad_out", core, act, gf, True)
    p_win = wgrad_call("wgrad_in", core, low, gp, False)
    state = None
    bwd = lambda i, state, g: attn_bwd_call(qa0, qa1, qkv, ctx, g, lengths, i, parts, state)
    if regular():
        swap = lambda p: (p[0], move(p[1], TO_CORE))
        r_out = sum_core(here, [swap(p_wout)])
        p_wao = wgrad_ao(core, ctx, after(ga, r_out[0][0]), sums, sbin)
        r_in = sum_core(here, [swap(p_win), swap(p_wao)])
        def hold(r, state):
            (k0, g0), second = r
            return (after(k0, state[3]), g0), second

        gc = after(gc, r_in[0][0])
        state = bwd(0, None, gc)
        r_out = sum_plane(here, *hold(r_out, state))
        gc = after(gc, r_out[0][0])
        state = bwd(1, state, gc)
        r_in = sum_plane(here, *hold(r_in, state))
        gc = after(gc, r_in[0][0])
        state = bwd(2, state, gc)
        r_out = sum_z(here, *hold(r_out, state))
        gc = after(gc, r_out[0])
        state = bwd(3, state, gc)
        r_in = sum_z(here, *hold(r_in, state))
        dq, dk, dv, sq, sv = state
        p_wqkv = wgrad3(core, after(x, r_in[0], *r_out[1:]), dq, dk, dv, sq, sv)
        keep, send = p_wqkv
        r_qkv = sum_core(here, [swap((keep, after(send, r_in[1], r_in[3])))])
        g_tok = tok_call(after(ga, r_qkv[0][0]), dq, dk, dv, place, w1)
        (k0, g0), second = r_qkv
        r_qkv = sum_plane(here, (after(k0, g_tok, r_in[2]), g0), second)
        rest = add4(r_out, [after(r_in[0], r_qkv[0][0]), *r_in[1:]])
        own, *far = sum_z(here, *r_qkv)
        over_x = move(after(rest, own), TO_X)
        own = add4([own, *far])
        [rest, over_x], [own] = tied([rest, over_x], [own])
        vectors = [(0, 128 * i, 128) for i in range(6)] + [(1, 0, nblk * 128)]
        g_wout, g_win, g_wao, g_bao, g_g1, g_s1, g_bout, g_g2, g_s2, g_bin = final_call(
            here,
            (rest, move(rest, TO_CORE), over_x, move(over_x, TO_CORE)),
            [(4, True), (nblk, False), (1, False)],
            vectors,
        )
        over_x = move(own, TO_X)
        over_x, g_wout = lax.optimization_barrier((over_x, g_wout))
        shares = (own, move(own, TO_CORE), over_x, move(over_x, TO_CORE))
        g_wqkv, g_bqv = final_call(here, shares, [(3, False)], [(0, 0, 256)])
        vecs = [v.reshape(-1) for v in (g_bqv, g_bao, g_g1, g_s1, g_bin, g_bout, g_g2, g_s2)]
    else:
        p_wao = wgrad_call("wgrad_ao", core, ctx, ga, False)
        for i in range(parts):
            state = bwd(i, state, gc)
        dq, dk, dv, sq, sv = state
        p_wqkv = [v[:, : 3 * SUB] for v in wgrad3(core, x, dq, dk, dv, sq, sv)]
        g_tok = tok_call(ga, dq, dk, dv, place, w1)
        g_wout = reduce_any(*p_wout, True)
        g_win, g_wao, g_wqkv = [reduce_any(*p, False) for p in (p_win, p_wao, p_wqkv)]
        vecs = [jnp.concatenate([sq[0], sv[0]]), sums[5], sums[3], sums[4], sums[2], sums[0], sums[1], sbin]
        own = small_sum(jnp.concatenate([v.reshape(count, -1) for v in vecs], 1))
        vecs = [own[e - s : e] for s, e in zip(sizes, ends)]
        vecs.insert(4, vecs.pop())
    g_bqv, g_bao, g_g1, g_s1, g_bin, g_bout, g_g2, g_s2 = vecs
    return (
        out[None], g_tok[None], g_wqkv, g_bqv, g_wao, g_bao, g_g1, g_s1,
        g_win, g_bin, g_wout, g_bout, g_g2, g_s2,
    )


def solution(mesh):
    rows = P(("replica", "shard"), None, None)
    mat, vec = P("shard", None), P("shard")
    return jax.shard_map(
        shards,
        mesh=mesh,
        in_specs=(rows, P(("replica", "shard")), rows, mat, vec, mat, vec, vec, vec, mat, vec, mat, vec, vec, vec),
        out_specs=(rows, rows, mat, vec, mat, vec, vec, vec, mat, vec, mat, vec, vec, vec),
        check_vma=False,
    )
```

```python
import functools
import jax
import jax.numpy as jnp
from jax import lax
from jax.experimental import pallas as pl
from jax.experimental.pallas import tpu as pltpu
from jax.sharding import PartitionSpec as P

HD = 64
F32 = jnp.float32
BF = jnp.bfloat16
SQRT_HALF = 0.7071067811865476
INV_ROOT_TAU = 0.3989422804014327


def params(mib=60):
    return pltpu.CompilerParams(vmem_limit_bytes=mib << 20)


def dot_nn(a, b):
    return jnp.dot(a, b, preferred_element_type=F32)


def dot_nt(a, b):
    return lax.dot_general(a, b, (((1,), (1,)), ((), ())), preferred_element_type=F32)


def dot_tn(a, b):
    return lax.dot_general(a, b, (((0,), (0,)), ((), ())), preferred_element_type=F32)


def cost(flops, nbytes, trans=0):
    return pl.CostEstimate(flops=int(flops), bytes_accessed=int(nbytes), transcendentals=int(trans))


SUB = 32
ANY = pl.BlockSpec(memory_space=pltpu.HBM)


def loads(place, bufs, lo, hi, target, sem):
    found = []
    for buf in bufs:
        for m in range(buf.shape[0]):
            i = len(found)
            found.append(pltpu.make_async_copy(buf.at[m, pl.ds(lo, hi - lo)], target(place[i]), sem.at[i]))
    return found


def start_all(copies):
    for c in copies:
        c.start()


def wait_all(copies):
    for c in copies:
        c.wait()


def qkv_body(count, place, x_ref, b_ref, *rest):
    bufs, (o_ref, w_vm, sem) = rest[:count], rest[count:]
    step = pl.program_id(0)
    blocks, width = w_vm.shape[0], w_vm.shape[-1]
    copies = loads(place, bufs, 0, blocks, lambda p: w_vm.at[:, p], sem)

    @pl.when(step == 0)
    def _():
        start_all(copies)
        wait_all(copies)

    x = x_ref[...]
    for n in range(blocks):
        w = w_vm[n].reshape(-1, width)
        bias = b_ref[:, n * width : (n + 1) * width]
        o_ref[:, n * width : (n + 1) * width] = (dot_nn(x, w) + bias).astype(BF)


def qkv_call(x, place, w1, bias, rows=256):
    slots, width = x.shape
    pieces = width // SUB
    return pl.pallas_call(
        functools.partial(qkv_body, len(w1)),
        name="qkv",
        grid_spec=pltpu.PrefetchScalarGridSpec(
            num_scalar_prefetch=1,
            grid=(slots // rows,),
            in_specs=[
                pl.BlockSpec((rows, width), lambda i, p: (i, 0)),
                pl.BlockSpec((1, 3 * width), lambda i, p: (0, 0)),
            ] + [ANY] * len(w1),
            out_specs=pl.BlockSpec((rows, 3 * width), lambda i, p: (i, 0)),
            scratch_shapes=[
                pltpu.VMEM((3, pieces, SUB, width), BF),
                pltpu.SemaphoreType.DMA((pieces,)),
            ],
        ),
        out_shape=jax.ShapeDtypeStruct((slots, 3 * width), BF),
        compiler_params=params(40),
        cost_estimate=cost(6 * slots * width * width, 8 * slots * width + 6 * width * width),
    )(place, x, bias, *w1)


def lanes(rows):
    return lax.broadcasted_iota(jnp.int32, (rows, 2 * HD), 1)


def split3(v):
    hi = v.astype(BF).astype(F32)
    mid = (v - hi).astype(BF).astype(F32)
    return hi, mid, v - hi - mid


def attn_fwd_body(rows, len_ref, q_ref, k_ref, v_ref, *rest):
    ctx_ref, qa0_ref, qa1_ref = rest[-3:]
    slots = k_ref.shape[0]
    lane = lanes(slots)
    key_row = lax.broadcasted_iota(jnp.int32, (slots, 2 * HD), 0)
    bias = jnp.where(key_row < len_ref[0], 0.0, -1e30)
    k = k_ref[...].astype(F32)
    k_aug = []
    for h in range(2):
        own = (lane // HD) == h
        spare = (1 - h) * HD
        k_aug.append(jnp.where(own, k, jnp.where(lane == spare, bias, 0.0)).astype(BF))
    v_aug = [jnp.where((lane // HD) == h, v_ref[...].astype(F32), 1.0).astype(BF) for h in range(2)]
    lane_q = lanes(rows)

    def scores(item):
        blk, h = item
        q = q_ref[blk * rows : (blk + 1) * rows, :].astype(F32) * 0.125
        qh = jnp.where((lane_q // HD) == h, q, jnp.where(lane_q == (1 - h) * HD, 1.0, 0.0))
        return qh, dot_nt(qh.astype(BF), k_aug[h])

    items = [(blk, h) for blk in range(slots // rows) for h in range(2)]
    held = scores(items[0])
    outs = []
    for i, (blk, h) in enumerate(items):
        sl = slice(blk * rows, (blk + 1) * rows)
        qh, s = held
        if i + 1 < len(items):
            held = scores(items[i + 1])
        spare = (1 - h) * HD
        top = jnp.max(s, axis=-1, keepdims=True)
        o = dot_nn(jnp.exp(s - top).astype(BF), v_aug[h])
        norm = o[:, spare : spare + 1]
        outs.append(o / norm)
        hi, mid, lo = split3(-(top + jnp.log(norm)))
        qh = jnp.where(lane_q == spare + 1, hi, qh)
        qh = jnp.where(lane_q == spare + 2, mid, qh)
        qh = jnp.where(lane_q == spare + 3, lo, qh)
        (qa0_ref, qa1_ref)[h][sl, :] = qh.astype(BF)
        if h == 1:
            ctx_ref[sl, :] = jnp.where(lane_q < HD, outs[-2], outs[-1]).astype(BF)


def attn_fwd_call(qkv, lengths, part, parts, before, rows=256):
    slots, wide = qkv.shape
    width = wide // 3
    pairs = width // (2 * HD)
    each = pairs // parts
    col = lambda off: pl.BlockSpec((slots, 2 * HD), lambda j, ln: (0, off * pairs + part * each + j))
    out = jax.ShapeDtypeStruct((slots, width), BF)
    extra = list(before or ())
    return pl.pallas_call(
        functools.partial(attn_fwd_body, rows),
        name=f"attn_fwd{part}",
        grid_spec=pltpu.PrefetchScalarGridSpec(
            num_scalar_prefetch=1,
            grid=(each,),
            in_specs=[col(0), col(1), col(2)] + [ANY] * len(extra),
            out_specs=[col(0)] * 3,
        ),
        out_shape=[out, out, out],
        input_output_aliases={4 + i: i for i in range(3)} if before else {},
        compiler_params=params(32),
        cost_estimate=cost(
            16 * slots * slots * width / parts, 12 * slots * width / parts, slots * slots * 2 * each
        ),
    )(lengths, qkv, qkv, qkv, *extra)


def attn_bwd_body(rows, len_ref, qa0_ref, qa1_ref, k_ref, v_ref, ctx_ref, g_ref, *rest):
    dq_ref, dk_ref, dv_ref, sq_ref, sv_ref = rest[-5:]
    slots = k_ref.shape[0]
    lane = lanes(slots)
    key_row = lax.broadcasted_iota(jnp.int32, (slots, 2 * HD), 0)
    bias = jnp.where(key_row < len_ref[0], 0.0, -1e30)
    k = k_ref[...].astype(F32)
    v = v_ref[...].astype(F32)
    k_low = k_ref[...]
    k_aug, v_aug = [], []
    for h in range(2):
        own = (lane // HD) == h
        spare = (1 - h) * HD
        near = (lane > spare) & (lane < spare + 4)
        ones = jnp.where(near, 1.0, 0.0)
        k_aug.append(jnp.where(own, k, jnp.where(lane == spare, bias, ones)).astype(BF))
        v_aug.append(jnp.where(own, v, ones).astype(BF))
    lane_q = lanes(rows)
    items = [(blk, h) for blk in range(slots // rows) for h in range(2)]

    def products(item):
        blk, h = item
        sl = slice(blk * rows, (blk + 1) * rows)
        own = (lane_q // HD) == h
        spare = (1 - h) * HD
        g = g_ref[sl, :].astype(F32)
        delta = jnp.sum(jnp.where(own, g * ctx_ref[sl, :].astype(F32), 0.0), axis=-1, keepdims=True)
        hi, mid, lo = split3(-delta)
        ga = jnp.where(own, g, 0.0)
        ga = jnp.where(lane_q == spare + 1, hi, ga)
        ga = jnp.where(lane_q == spare + 2, mid, ga)
        ga = jnp.where(lane_q == spare + 3, lo, ga).astype(BF)
        return dot_nt(k_aug[h], (qa0_ref, qa1_ref)[h][sl, :]), dot_nt(v_aug[h], ga)

    held = products(items[0])
    dk = [jnp.zeros((slots, 2 * HD), F32)] * 2
    dv = [jnp.zeros((slots, 2 * HD), F32)] * 2
    dqs = []
    for i, (blk, h) in enumerate(items):
        sl = slice(blk * rows, (blk + 1) * rows)
        s, gs = held
        if i + 1 < len(items):
            held = products(items[i + 1])
        p = jnp.exp(s)
        ds = (p * gs).astype(BF)
        dv[h] = dv[h] + dot_nn(p.astype(BF), g_ref[sl, :])
        dk[h] = dk[h] + dot_nn(ds, (qa0_ref, qa1_ref)[h][sl, :])
        dqs.append(dot_tn(ds, k_low))
        if h == 1:
            dq_ref[sl, :] = (jnp.where(lane_q < HD, dqs[-2], dqs[-1]) * 0.125).astype(BF)
    dk_ref[...] = jnp.where(lane < HD, dk[0], dk[1]).astype(BF)
    dv_low = jnp.where(lane < HD, dv[0], dv[1]).astype(BF)
    dv_ref[...] = dv_low
    sq_ref[...] = jnp.sum(dq_ref[...].astype(F32), axis=0, keepdims=True)
    sv_ref[...] = jnp.sum(dv_low.astype(F32), axis=0, keepdims=True)


def attn_bwd_call(qa0, qa1, qkv, ctx, grad_ctx, lengths, part, parts, before, rows=256):
    slots, width = ctx.shape
    pairs = width // (2 * HD)
    each = pairs // parts
    col = lambda off: pl.BlockSpec((slots, 2 * HD), lambda j, ln: (0, off * pairs + part * each + j))
    row = pl.BlockSpec((1, 2 * HD), lambda j, ln: (0, part * each + j))
    out = jax.ShapeDtypeStruct((slots, width), BF)
    vec = jax.ShapeDtypeStruct((1, width), F32)
    extra = list(before or ())
    return pl.pallas_call(
        functools.partial(attn_bwd_body, rows),
        name=f"attn_bwd{part}",
        grid_spec=pltpu.PrefetchScalarGridSpec(
            num_scalar_prefetch=1,
            grid=(each,),
            in_specs=[col(0), col(0), col(1), col(2), col(0), col(0)] + [ANY] * len(extra),
            out_specs=[col(0)] * 3 + [row] * 2,
        ),
        out_shape=[out, out, out, vec, vec],
        input_output_aliases={7 + i: i for i in range(5)} if before else {},
        compiler_params=params(32),
        cost_estimate=cost(
            40 * slots * slots * width / parts, 18 * slots * width / parts, slots * slots * 2 * each
        ),
    )(lengths, qa0, qa1, qkv, qkv, ctx, grad_ctx, *extra)


def norm_stats(resid):
    mean = jnp.mean(resid, axis=-1, keepdims=True)
    centred = resid - mean
    inv = lax.rsqrt(jnp.mean(centred * centred, axis=-1, keepdims=True) + 1e-5)
    return centred * inv, inv


def norm_back(u, normed, inv):
    return inv * (u - jnp.mean(u, axis=-1, keepdims=True) - normed * jnp.mean(u * normed, axis=-1, keepdims=True))


def colsum(v):
    return jnp.sum(v, axis=0, keepdims=True)


def row_body(n2, len_ref, place, x_ref, ctx_ref, cot_ref, vec_ref, bin_ref, *rest):
    b2 = rest[:n2]
    (
        out_ref, act_ref, hid_ref, gf_ref, gp_ref, ga_ref, gc_ref, sums_ref, sbin_ref,
        wa, wi, wo, slope, sem,
    ) = rest[n2:]
    step = pl.program_id(0)
    rows, width = x_ref.shape
    nblk = wi.shape[0]
    copies = [
        loads(place, b2, 0, 1, lambda p: wa.at[pl.ds(p, 1)], sem.at[0]),
        loads(place, b2, 1, 1 + nblk, lambda p: wi.at[:, p], sem.at[1]),
        loads(place, b2, 1 + nblk, 5 + nblk, lambda p: wo.at[p], sem.at[2]),
    ]

    @pl.when(step == 0)
    def _():
        for c in copies:
            start_all(c)
        sums_ref[...] = jnp.zeros_like(sums_ref)
        sbin_ref[...] = jnp.zeros_like(sbin_ref)

    def ready(i):
        @pl.when(step == 0)
        def _():
            wait_all(copies[i])

    bao, gain1, shift1, bout, gain2, shift2 = [vec_ref[i : i + 1, :] for i in range(6)]
    ready(0)
    w_ao = wa[...].reshape(width, width)
    resid1 = x_ref[...].astype(F32) + dot_nn(ctx_ref[...], w_ao) + bao
    normed1, inv1 = norm_stats(resid1)
    hidden = normed1 * gain1 + shift1
    low = hidden.astype(BF)
    hid_ref[...] = low
    acc = jnp.zeros((rows, width), F32)
    per = wo.shape[0] // nblk
    ready(1)
    for n in range(nblk):
        pre = dot_nn(low, wi[n].reshape(width, width)) + bin_ref[n : n + 1, :]
        phi = 0.5 + 0.5 * lax.erf(pre * SQRT_HALF)
        slope[n] = (phi + pre * (INV_ROOT_TAU * jnp.exp(-0.5 * pre * pre))).astype(slope.dtype)
        act = (pre * phi).astype(BF)
        act_ref[:, n * width : (n + 1) * width] = act
        if n == 0:
            ready(2)
        acc = acc + dot_nn(act, wo[n * per : (n + 1) * per].reshape(width, width))
    resid2 = hidden + acc + bout
    normed2, inv2 = norm_stats(resid2)
    row_id = lax.broadcasted_iota(jnp.int32, (rows, 1), 0) + step * rows
    valid = (row_id < len_ref[0]).astype(F32)
    out_ref[...] = ((normed2 * gain2 + shift2) * valid).astype(BF)
    gz = cot_ref[...].astype(F32) * valid
    sums_ref[0:1, :] += colsum(gz * normed2)
    sums_ref[1:2, :] += colsum(gz)
    g_resid2 = norm_back(gz * gain2, normed2, inv2)
    gf = g_resid2.astype(BF)
    gf_ref[...] = gf
    sums_ref[2:3, :] += colsum(gf.astype(F32))
    acc = g_resid2
    for n in range(nblk):
        g_act = dot_nt(gf, wo[n * per : (n + 1) * per].reshape(width, width))
        gp = (g_act * slope[n].astype(F32)).astype(BF)
        gp_ref[:, n * width : (n + 1) * width] = gp
        sbin_ref[n : n + 1, :] += colsum(gp.astype(F32))
        acc = acc + dot_nt(gp, wi[n].reshape(width, width))
    sums_ref[3:4, :] += colsum(acc * normed1)
    sums_ref[4:5, :] += colsum(acc)
    g_attn = norm_back(acc * gain1, normed1, inv1).astype(BF)
    ga_ref[...] = g_attn
    sums_ref[5:6, :] += colsum(g_attn.astype(F32))
    gc_ref[...] = dot_nt(g_attn, w_ao).astype(BF)


def row_call(x, ctx, cot, place, w2, vecs, b_in, lengths, rows=256):
    slots, width = x.shape
    pieces, sub = width // SUB, SUB
    nblk = b_in.shape[0]
    ff = nblk * width
    blk = pl.BlockSpec((rows, width), lambda i, ln, p: (i, 0))
    big = pl.BlockSpec((rows, ff), lambda i, ln, p: (i, 0), pipeline_mode=pl.Buffered(1 if rows > 256 else 2))
    const = lambda r: pl.BlockSpec((r, width), lambda i, ln, p: (0, 0))
    o = jax.ShapeDtypeStruct((slots, width), BF)
    ob = jax.ShapeDtypeStruct((slots, ff), BF)
    return pl.pallas_call(
        functools.partial(row_body, len(w2)),
        name="row_local",
        grid_spec=pltpu.PrefetchScalarGridSpec(
            num_scalar_prefetch=2,
            grid=(slots // rows,),
            in_specs=[blk, blk, blk, const(8), const(nblk)] + [ANY] * len(w2),
            out_specs=[blk, big, blk, blk, big, blk, blk, const(8), const(nblk)],
            scratch_shapes=[
                pltpu.VMEM((pieces, sub, width), BF),
                pltpu.VMEM((nblk, pieces, sub, width), BF),
                pltpu.VMEM((pieces, 4, sub, width), BF),
                pltpu.VMEM((nblk, rows, width), BF),
                pltpu.SemaphoreType.DMA((3, pieces)),
            ],
        ),
        out_shape=[
            o, ob, o, o, ob, o, o,
            jax.ShapeDtypeStruct((8, width), F32),
            jax.ShapeDtypeStruct((nblk, width), F32),
        ],
        compiler_params=params(),
        cost_estimate=cost(36 * slots * width * width, 40 * slots * width + 18 * width * width, 2 * slots * ff),
    )(lengths, place, x, ctx, cot, vecs, b_in, *w2)


def halves(core, value, keep_ref, send_ref):
    count, rows, width = keep_ref.shape
    value = value.reshape(count, 2, rows, width)
    even, odd = value[:, 0], value[:, 1]

    @pl.when(core == 0)
    def _():
        keep_ref[...] = even
        send_ref[...] = odd

    @pl.when(core != 0)
    def _():
        keep_ref[...] = odd
        send_ref[...] = even


LINES = 16


def lines_of(*lines):
    width, segments = lines[0][0], [line[1:] for line in lines]
    row = lax.broadcasted_iota(jnp.int32, (LINES, width), 0)
    value = jnp.zeros((LINES, width), F32)
    for i, segs in enumerate(segments):
        used = sum(v.shape[1] for v in segs)
        line = jnp.concatenate(segs + [jnp.zeros((1, width - used), F32)] * (used < width), 1)
        value = jnp.where(row == i, line, value)
    return value.astype(BF)


def wgrad_body(core, a_ref, b_ref, keep_ref, send_ref):
    halves(core[0], dot_tn(a_ref[...], b_ref[...]).astype(BF), keep_ref, send_ref)


def wgrad_call(name, core, a, b, by_rows, tile=1024):
    slots, m = a.shape
    width = a.shape[1] if not by_rows else b.shape[1]
    blocks = m // width if by_rows else b.shape[1] // m
    pieces = width // SUB
    if by_rows:
        grid = (1, m // tile)
        block = (tile // (2 * SUB * blocks), blocks * SUB, width)
        where = lambda j, i, c: (i, 0, 0)
    else:
        grid = (blocks, m // tile)
        block = (tile // (2 * SUB), SUB, width)
        where = lambda j, i, c: (i, j, 0)
    out = jax.ShapeDtypeStruct((pieces // 2, blocks * SUB, width), BF)
    return pl.pallas_call(
        wgrad_body,
        name=name,
        grid_spec=pltpu.PrefetchScalarGridSpec(
            num_scalar_prefetch=1,
            grid=grid,
            in_specs=[
                pl.BlockSpec((slots, tile), lambda j, i, c: (0, i)),
                pl.BlockSpec((slots, width), lambda j, i, c: (0, j)),
            ],
            out_specs=[pl.BlockSpec(block, where)] * 2,
        ),
        out_shape=[out, out],
        compiler_params=params(40),
        cost_estimate=cost(2 * slots * m * b.shape[1], 2 * (slots * (m + b.shape[1]) + m * b.shape[1])),
    )(core, a, b)


def wgrad_ao_body(core, a_ref, b_ref, sums_ref, sbin_ref, keep_ref, send_ref):
    value = dot_tn(a_ref[...], b_ref[...]).astype(BF)
    halves(core[0], value, keep_ref.at[:, pl.ds(0, SUB)], send_ref.at[:, pl.ds(0, SUB)])
    count, _, width = keep_ref.shape
    owners = count // 2
    part, four = width // owners, sbin_ref.shape[0] * width // owners
    for s in range(owners):
        segs = [sums_ref[v : v + 1, s * part : (s + 1) * part] for v in (5, 3, 4, 2, 0, 1)]
        row, col = s * four // width, s * four % width
        value = lines_of([width, *segs], [width, sbin_ref[row : row + 1, col : col + four]])
        for ref in (keep_ref, send_ref):
            for x in (0, 1):
                ref[2 * s + x, SUB : SUB + LINES] = value


def wgrad_ao(core, a, b, sums, sbin):
    slots, m = a.shape
    full = lambda v: pl.BlockSpec(v.shape, lambda t, c: (0, 0))
    shape = (m // SUB // 2, SUB + LINES, m)
    return pl.pallas_call(
        wgrad_ao_body,
        name="wgrad_ao",
        grid_spec=pltpu.PrefetchScalarGridSpec(
            num_scalar_prefetch=1,
            grid=(1,),
            in_specs=[full(v) for v in (a, b, sums, sbin)],
            out_specs=[pl.BlockSpec(shape, lambda t, c: (0, 0, 0))] * 2,
        ),
        out_shape=[jax.ShapeDtypeStruct(shape, BF)] * 2,
        compiler_params=params(40),
        cost_estimate=cost(2 * slots * m * m, 4 * slots * m + 2 * m * m),
    )(core, a, b, sums, sbin)


def wgrad3_body(core, a_ref, q_ref, k_ref, v_ref, sq_ref, sv_ref, keep_ref, send_ref):
    for n, ref in enumerate((q_ref, k_ref, v_ref)):
        value = dot_tn(a_ref[...], ref[...]).astype(BF)
        rows = pl.ds(n * SUB, SUB)
        halves(core[0], value, keep_ref.at[:, rows], send_ref.at[:, rows])
    count, _, width = keep_ref.shape
    line = jnp.where(pl.program_id(0) == 0, sq_ref[...], sv_ref[...])
    part = 2 * width // count
    for s in range(count // 2):
        value = lines_of([width, line[:, s * part : (s + 1) * part]])
        for ref in (keep_ref, send_ref):
            for x in (0, 1):
                ref[2 * s + x, 3 * SUB : 3 * SUB + LINES] = value


def wgrad3(core, a, dq, dk, dv, sq, sv):
    slots, m = a.shape
    tile = m // 2
    full = pl.BlockSpec((slots, m), lambda i, c: (0, 0))
    vec = pl.BlockSpec((1, m), lambda i, c: (0, 0))
    block = pl.BlockSpec((tile // (2 * SUB), 3 * SUB + LINES, m), lambda i, c: (i, 0, 0))
    out = jax.ShapeDtypeStruct((m // SUB // 2, 3 * SUB + LINES, m), BF)
    return pl.pallas_call(
        wgrad3_body,
        name="wgrad_qkv",
        grid_spec=pltpu.PrefetchScalarGridSpec(
            num_scalar_prefetch=1,
            grid=(2,),
            in_specs=[pl.BlockSpec((slots, tile), lambda i, c: (0, i)), full, full, full, vec, vec],
            out_specs=[block, block],
        ),
        out_shape=[out, out],
        compiler_params=params(40),
        cost_estimate=cost(6 * slots * m * m, 14 * slots * m),
    )(core, a, dq, dk, dv, sq, sv)


def tok_body(count, place, g_ref, dq_ref, dk_ref, dv_ref, *rest):
    bufs, (o_ref, w_vm, sem) = rest[:count], rest[count:]
    step = pl.program_id(0)
    width = g_ref.shape[1]
    copies = loads(place, bufs, 0, 3, lambda p: w_vm.at[:, p], sem)

    @pl.when(step == 0)
    def _():
        start_all(copies)
        wait_all(copies)

    acc = g_ref[...].astype(F32)
    for n, ref in enumerate((dq_ref, dk_ref, dv_ref)):
        acc = acc + dot_nt(ref[...], w_vm[n].reshape(width, width))
    o_ref[...] = acc.astype(BF)


def tok_call(g, dq, dk, dv, place, w1, rows=256):
    slots, width = g.shape
    pieces = width // SUB
    blk = pl.BlockSpec((rows, width), lambda i, p: (i, 0))
    return pl.pallas_call(
        functools.partial(tok_body, len(w1)),
        name="grad_tok",
        grid_spec=pltpu.PrefetchScalarGridSpec(
            num_scalar_prefetch=1,
            grid=(slots // rows,),
            in_specs=[blk, blk, blk, blk] + [ANY] * len(w1),
            out_specs=blk,
            scratch_shapes=[pltpu.VMEM((3, pieces, SUB, width), BF), pltpu.SemaphoreType.DMA((pieces,))],
        ),
        out_shape=jax.ShapeDtypeStruct((slots, width), BF),
        compiler_params=params(40),
        cost_estimate=cost(6 * slots * width * width, 16 * slots * width),
    )(place, g, dq, dk, dv, *w1)


def total(*terms):
    acc = terms[0].astype(F32)
    for t in terms[1:]:
        acc = acc + t.astype(F32)
    return acc.astype(BF)


def add1_body(count, here, *refs):
    ins, outs = refs[: 8 * count], refs[8 * count :]
    for view in range(4):
        n0 = 0
        for i in range(count):
            a, b = ins[8 * i + 2 * view], ins[8 * i + 2 * view + 1]
            n = a.shape[3]
            outs[view][0, n0 : n0 + n] = total(a[0, 0, 0], b[0, 0, 0])
            n0 += n


def add1(here, pairs):
    width = pairs[0][0].shape[-1]
    views = []
    for half, own in ((0, 0), (0, 1), (1, 0), (1, 1)):
        def where(t, h, half=half, own=own):
            z, j = 2 * half + t // 2, t % 2
            if half == 0:
                return (z, j, h[0] if own else 1 - h[0], 0, 0)
            return (z, h[1] if own else 1 - h[1], j, 0, 0)
        views.append(where)
    specs, args, rows = [], [], 0
    for keep, got in pairs:
        n = keep.shape[1]
        rows += n
        for where in views:
            for arr in (keep, got):
                specs.append(pl.BlockSpec((1, 1, 1, n, width), where))
                args.append(arr.reshape(4, 2, 2, n, width))
    out = jax.ShapeDtypeStruct((4, rows, width), BF)
    return pl.pallas_call(
        functools.partial(add1_body, len(pairs)),
        name="add_core",
        grid_spec=pltpu.PrefetchScalarGridSpec(
            num_scalar_prefetch=1,
            grid=(4,),
            in_specs=specs,
            out_specs=[pl.BlockSpec((1, rows, width), lambda t, h: (t, 0, 0))] * 4,
        ),
        out_shape=[out] * 4,
        compiler_params=params(28),
        cost_estimate=cost(16 * rows * width, 96 * rows * width),
    )(here, *args)


def add2_body(here, *refs):
    ins, outs = refs[:8], refs[8:]
    for view in range(4):
        outs[view][0] = total(ins[2 * view][0, 0], ins[2 * view + 1][0, 0])


def add2(here, first, second):
    _, rows, width = first[0].shape
    specs, args = [], []
    for axis, pair in ((1, first), (0, second)):
        for own in (0, 1):
            for arr in pair:
                specs.append(pl.BlockSpec(
                    (1, 1, rows, width),
                    lambda t, h, axis=axis, own=own: (t, h[axis] if own else 1 - h[axis], 0, 0),
                ))
                args.append(arr.reshape(2, 2, rows, width))
    out = jax.ShapeDtypeStruct((2, rows, width), BF)
    return pl.pallas_call(
        add2_body,
        name="add_plane",
        grid_spec=pltpu.PrefetchScalarGridSpec(
            num_scalar_prefetch=1,
            grid=(2,),
            in_specs=specs,
            out_specs=[pl.BlockSpec((1, rows, width), lambda t, h: (t, 0, 0))] * 4,
        ),
        out_shape=[out] * 4,
        compiler_params=params(28),
        cost_estimate=cost(8 * rows * width, 48 * rows * width),
    )(here, *args)


def add3_body(here, ak, ag, bk, bg, *outs):
    for k, out in enumerate(outs):
        to = lax.rem(here[2] + k, 4)
        spot = lax.rem(to, 2)

        @pl.when(to < 2)
        def _():
            out[0] = total(ak[spot], ag[spot])

        @pl.when(to >= 2)
        def _():
            out[0] = total(bk[spot], bg[spot])


def add3(here, first, second):
    _, rows, width = first[0].shape
    full = pl.BlockSpec((2, rows, width), lambda t, h: (0, 0, 0))
    one = pl.BlockSpec((1, rows, width), lambda t, h: (0, 0, 0))
    return pl.pallas_call(
        add3_body,
        name="add_z",
        grid_spec=pltpu.PrefetchScalarGridSpec(
            num_scalar_prefetch=1, grid=(1,), in_specs=[full] * 4, out_specs=[one] * 4,
        ),
        out_shape=[jax.ShapeDtypeStruct((1, rows, width), BF)] * 4,
        compiler_params=params(28),
        cost_estimate=cost(4 * rows * width, 24 * rows * width),
    )(here, *first, *second)


def add4_body(*refs):
    ins, out = refs[:-1], refs[-1]
    n0 = 0
    for i in range(0, len(ins), 4):
        n = ins[i].shape[1]
        out[:, n0 : n0 + n] = total(*[r[...] for r in ins[i : i + 4]])
        n0 += n


def add4(*groups):
    spec = lambda shape: pl.BlockSpec(shape, lambda t: (0,) * len(shape))
    width = groups[0][0].shape[-1]
    shape = (1, sum(g[0].shape[1] for g in groups), width)
    parts = [v for g in groups for v in g]
    size = shape[1] * width
    return pl.pallas_call(
        add4_body,
        name="add_last",
        grid=(1,),
        in_specs=[spec(v.shape) for v in parts],
        out_specs=spec(shape),
        out_shape=jax.ShapeDtypeStruct(shape, BF),
        compiler_params=params(28),
        cost_estimate=cost(3 * size, 10 * size),
    )(*parts)


def final_body(kinds, vectors, here, own, core, over_x, both, *outs):
    mine_at = 2 * here[0] + here[3]
    mats, vecs = outs[: len(kinds)], outs[len(kinds) :]
    for flip, ref in enumerate((own, core, over_x, both)):
        share = jnp.bitwise_xor(mine_at, flip)
        n0 = 0
        for (blocks, by_rows), out in zip(kinds, mats):
            width = ref.shape[-1]
            for n in range(blocks):
                value = ref[0, n0 : n0 + SUB].astype(F32)
                n0 += SUB
                if by_rows:
                    out[pl.ds(pl.multiple_of(share * blocks * SUB, SUB) + n * SUB, SUB), :] = value
                else:
                    out[pl.ds(pl.multiple_of(share * SUB, SUB), SUB), n * width : (n + 1) * width] = value

        @pl.when(share == 0)
        def _():
            lines = ref[0, n0 : n0 + LINES].astype(F32)
            for (row, lane, size), out in zip(vectors, vecs):
                out[...] = lines[row : row + 1, lane : lane + size]


def final_call(here, parts, kinds, vectors):
    shape = parts[0].shape
    width = shape[-1]
    shapes = [
        (4 * blocks * SUB, width) if by_rows else (4 * SUB, blocks * width) for blocks, by_rows in kinds
    ] + [(1, size) for _, _, size in vectors]
    return pl.pallas_call(
        functools.partial(final_body, kinds, vectors),
        name="final",
        grid_spec=pltpu.PrefetchScalarGridSpec(
            num_scalar_prefetch=1,
            grid=(1,),
            in_specs=[pl.BlockSpec(shape, lambda t, h: (0, 0, 0))] * 4,
            out_specs=[pl.BlockSpec(sh, lambda t, h: (0, 0)) for sh in shapes],
        ),
        out_shape=[jax.ShapeDtypeStruct(sh, F32) for sh in shapes],
        compiler_params=params(28),
        cost_estimate=cost(1, 24 * parts[0].size),
    )(here, *parts)


BOTH = ("shard", "replica")
AXES = ("replica", "shard")


def table(fn):
    pairs = []
    for r in range(4):
        for s in range(8):
            x, y, z, c = fn(r // 2, s % 2, s // 2, r % 2)
            pairs.append((r * 8 + s, (x * 2 + c) * 8 + z * 2 + y))
    return pairs


TO_CORE = table(lambda x, y, z, c: (x, y, z, 1 - c))
TO_X = table(lambda x, y, z, c: (1 - x, y, z, c))
TO_XCORE = table(lambda x, y, z, c: (1 - x, y, z, 1 - c))
TO_Y = table(lambda x, y, z, c: (x, 1 - y, z, c))
TO_Z = [table(lambda x, y, z, c, k=k: (x, y, (z + k) % 4, c)) for k in range(4)]


def move(v, pairs):
    return lax.ppermute(v, AXES, pairs)


def regular():
    return lax.axis_size("shard") == 8 and lax.axis_size("replica") == 4


def place_of():
    r, s = lax.axis_index("replica"), lax.axis_index("shard")
    return r // 2, s % 2, s // 2, r % 2


def pack_body(share, *refs):
    ins, out = refs[:-1], refs[-1]
    width = out.shape[-1]
    n0 = 0
    for ref in ins:
        rows, cols = ref.shape
        if rows > SUB:
            out[0, n0 : n0 + rows // SUB] = ref[...].reshape(rows // SUB, SUB, width)
            n0 += rows // SUB
        else:
            for n in range(cols // width):
                out[0, n0 + n] = ref[:, n * width : (n + 1) * width]
            n0 += cols // width


def pack(share, mats, width):
    shapes = [(m.shape[0] // 4, m.shape[1]) for m in mats]
    blocks = sum(r * c for r, c in shapes) // (SUB * width)
    return pl.pallas_call(
        pack_body,
        name="pack",
        grid_spec=pltpu.PrefetchScalarGridSpec(
            num_scalar_prefetch=1,
            grid=(1,),
            in_specs=[pl.BlockSpec(sh, lambda t, r: (r[0], 0)) for sh in shapes],
            out_specs=pl.BlockSpec((1, blocks, SUB, width), lambda t, r: (0, 0, 0, 0)),
        ),
        out_shape=jax.ShapeDtypeStruct((1, blocks, SUB, width), BF),
        compiler_params=params(),
        cost_estimate=cost(1, 4 * blocks * SUB * width),
    )(share, *mats)


def pack_first_body(share, w_ref, *refs):
    vecs, out = refs[:-1], refs[-1]
    rows, width = 3 * SUB, out.shape[-1]
    for n in range(3):
        out[0, n * SUB : (n + 1) * SUB] = w_ref[:, n * width : (n + 1) * width]
    segs = [v[...].astype(F32) for v in vecs]
    out[0, rows : rows + LINES] = lines_of([width, *segs[:-1]], [width, segs[-1]])


def pack_first(share, w_qkv, vecs, width):
    rows = w_qkv.shape[0] // 4
    vecs = [v.reshape(1, -1) for v in vecs]
    shape = (1, 3 * rows + LINES, width)
    return pl.pallas_call(
        pack_first_body,
        name="pack_first",
        grid_spec=pltpu.PrefetchScalarGridSpec(
            num_scalar_prefetch=1,
            grid=(1,),
            in_specs=[pl.BlockSpec((rows, 3 * width), lambda t, r: (r[0], 0))]
            + [pl.BlockSpec(v.shape, lambda t, r: (0, 0)) for v in vecs],
            out_specs=pl.BlockSpec(shape, lambda t, r: (0, 0, 0)),
        ),
        out_shape=jax.ShapeDtypeStruct(shape, BF),
        compiler_params=params(),
        cost_estimate=cost(1, 12 * rows * width),
    )(share, w_qkv, *vecs)


def after(v, *deps):
    return lax.optimization_barrier((v,) + deps)[0]


def to_core(bufs):
    return [move(v, TO_CORE) for v in bufs]


def tied(*groups):
    flat = lax.optimization_barrier([v for g in groups for v in g])
    out = []
    for g in groups:
        out.append(flat[: len(g)])
        flat = flat[len(g) :]
    return out


def gather_places(order):
    x, y, z, c = place_of()
    spots = []
    for fc in (0, 1):
        for k, fx, fy in order:
            spots.append((((z - k) % 4) * 2 + (y ^ fy)) * 4 + (x ^ fx) * 2 + (c ^ fc))
    return jnp.stack(spots).astype(jnp.int32)


FIRST = [
    (k0 + k, fx, fy)
    for k0, fx, fy in ((0, 0, 0), (2, 0, 0), (0, 0, 1), (2, 1, 0), (0, 1, 0), (2, 0, 1), (0, 1, 1), (2, 1, 1))
    for k in (0, 1)
]
SECOND = [
    (0, 0, 0), (0, 1, 0), (1, 0, 0), (3, 0, 0), (2, 0, 0), (0, 0, 1), (1, 1, 0), (3, 1, 0),
    (1, 0, 1), (3, 0, 1), (2, 1, 0), (0, 1, 1), (2, 0, 1), (3, 1, 1), (1, 1, 1), (2, 1, 1),
]


def spread(w, blocks, wide):
    full = lax.all_gather(w, "shard", axis=0, tiled=True)
    if full.shape[1] == wide:
        return full.reshape(-1, blocks, SUB, wide)
    return full.reshape(-1, SUB, blocks, wide).transpose(0, 2, 1, 3)


def sum_core(here, pairs):
    a_send, a_keep, b_send, b_keep = add1(here, pairs)
    return (a_keep, move(a_send, TO_X)), (b_keep, move(b_send, TO_Y))


def sum_plane(here, first, second):
    a_send, a_keep, b_send, b_keep = add2(here, first, second)
    return (a_keep, move(a_send, TO_Y)), (b_keep, move(b_send, TO_X))


def sum_z(here, first, second):
    own, *sends = add3(here, first, second)
    return [own] + [move(v, TO_Z[k + 1]) for k, v in enumerate(sends)]


def small_gather(lines):
    x, y, z, c = place_of()
    rows = jnp.concatenate([lines, move(lines, TO_Y)], 0)
    spots = jnp.stack([((z - k) % 4) * 2 + (y ^ f) for f in (0, 1) for k in range(4)])
    pick = (jnp.arange(8)[:, None] == spots[None, :]).astype(BF)
    return dot_nn(pick, rows)


def small_sum(rows):
    return lax.dynamic_index_in_dim(lax.psum(rows, BOTH), lax.axis_index("shard"), 0, keepdims=False)


def reduce_any(keep, send, by_rows):
    half, rows, wide = keep.shape
    full = jnp.stack([keep, send], 1).reshape(2 * half, rows // SUB, SUB, wide)
    full = full.reshape(-1, wide) if by_rows else full.transpose(0, 2, 1, 3).reshape(2 * half * SUB, -1)
    part = lax.psum_scatter(full, "shard", scatter_dimension=0, tiled=True)
    return lax.psum(part, "replica").astype(F32)


def shards(
    tokens, lengths, cotangent, w_qkv, b_qv, w_attn_out, b_attn_out, ln1_gain, ln1_bias,
    w_ffn_in, b_ffn_in, w_ffn_out, b_ffn_out, ln2_gain, ln2_bias,
):
    _, slots, width = tokens.shape
    nblk = w_ffn_in.shape[1] // width
    count = lax.axis_size("shard")
    x = tokens.reshape(slots, width)
    cot = cotangent.reshape(slots, width)
    small = [b_qv, b_attn_out, ln1_gain, ln1_bias, b_ffn_out, ln2_gain, ln2_bias, b_ffn_in]
    sizes = [v.shape[0] for v in small]
    ends = [sum(sizes[: i + 1]) for i in range(len(sizes))]

    if regular():
        share = lax.axis_index("replica").reshape(1).astype(jnp.int32)
        first = pack_first(share, w_qkv, small, width)
        second = pack(share, [after(w_attn_out, first), w_ffn_in, w_ffn_out], width)
        xo, yo = move(second, TO_X), move(second, TO_Y)
        along = [first] + [move(first, TO_Z[k]) for k in (1, 2, 3)]
        *along, xo, yo = lax.optimization_barrier((*along, xo, yo))
        a1, b1 = [
            jnp.concatenate([v[:, : 3 * SUB] for v in pair], 0).reshape(2, 3, SUB, width)
            for pair in (along[:2], along[2:])
        ]
        lines = jnp.concatenate([v[:, 3 * SUB : 3 * SUB + 2] for v in along], 0)
        rows = small_gather(lines.reshape(4, 2 * width)[:, : ends[-1]])
        second = after(second, along[3])
        near, *far = [move(second, TO_Z[k]) for k in (1, 2, 3)]
        plane = [move(a1, TO_Y), move(b1, TO_X), move(a1, TO_X), move(b1, TO_Y)]
        first = [a1, b1]
        cores = to_core(first)
        plane, cores = tied(plane, cores)
        last = [move(plane[0], TO_X), move(plane[1], TO_Y)]
        more = to_core(plane)
        _, [near, far[1]] = tied(last, [near, far[1]])
        w1 = [*first, *plane, *last, *cores, *more, *to_core(last)]
        r13 = jnp.concatenate([near, far[1]], 0)
        x1, y1 = move(r13, TO_X), move(r13, TO_Y)
        place, place2 = gather_places(FIRST), gather_places(SECOND)
        here = jnp.stack(place_of()).astype(jnp.int32)
    else:
        w1 = [spread(w_qkv, 3, width)]
        w2 = [spread(w_attn_out, 1, width), spread(w_ffn_in, nblk, width), spread(w_ffn_out, 4, width)]
        w2 = [jnp.concatenate(w2, 1)]
        place = place2 = jnp.arange(width // SUB, dtype=jnp.int32)
        here = jnp.zeros((4,), jnp.int32)
    core = here[3:]

    if not regular():
        rows = lax.all_gather(jnp.concatenate(small), "shard", axis=0).astype(F32)
    b_qv, bao, gain1, shift1, bout, gain2, shift2, b_in = [
        rows[:, e - s : e].reshape(-1) for s, e in zip(sizes, ends)
    ]
    bias3 = jnp.concatenate([b_qv[:width], jnp.zeros((width,), F32), b_qv[width:]]).reshape(1, -1)
    zero = jnp.zeros((width,), F32)
    vecs = jnp.stack([bao, gain1, shift1, bout, gain2, shift2, zero, zero])

    qkv = qkv_call(x, place, w1, bias3)
    parts = 4
    fwd = lambda i, state: attn_fwd_call(qkv, lengths, i, parts, state)
    state = fwd(0, None)
    if regular():
        [r2], [x1, y1], state = tied([far[0]], [x1, y1], state)
        c2 = jnp.concatenate([r2, yo], 0)
        x2, y2 = move(c2, TO_X), move(jnp.concatenate([r2, x1[1:]], 0), TO_Y)
        cores = to_core([second, xo, r13, x1, y1])
        state = fwd(1, state)
        cores, state = tied(cores, state)
        state = fwd(2, state)
        [x2, y2], state = tied([x2, y2], state)
        x3, y3 = move(y1[:1], TO_X), move(x2[:1], TO_Y)
        more = to_core([c2, x2, y2])
        more, state = tied(more, state)
        state = fwd(3, state)
        last, state = tied([x3, y3], state)
        w2 = [second, xo, r13, c2, x1, y1, x2, y2, *last]
        w2 += [*cores[:3], more[0], *cores[3:], *more[1:], *to_core(last)]
    else:
        for i in range(1, parts):
            state = fwd(i, state)
    ctx, qa0, qa1 = state
    out, act, low, gf, gp, ga, gc, sums, sbin = row_call(
        x, ctx, cot, place2, w2, vecs, b_in.reshape(nblk, width), lengths
    )
    p_wout = wgrad_call("wgrad_out", core, act, gf, True)
    p_win = wgrad_call("wgrad_in", core, low, gp, False)
    state = None
    bwd = lambda i, state, g: attn_bwd_call(qa0, qa1, qkv, ctx, g, lengths, i, parts, state)
    if regular():
        swap = lambda p: (p[0], move(p[1], TO_CORE))
        r_out = sum_core(here, [swap(p_wout)])
        p_wao = wgrad_ao(core, ctx, after(ga, r_out[0][0]), sums, sbin)
        r_in = sum_core(here, [swap(p_win), swap(p_wao)])
        def hold(r, state):
            (k0, g0), second = r
            return (after(k0, state[3]), g0), second

        gc = after(gc, r_in[0][0])
        state = bwd(0, None, gc)
        r_out = sum_plane(here, *hold(r_out, state))
        gc = after(gc, r_out[0][0])
        state = bwd(1, state, gc)
        state = bwd(2, state, gc)
        r_in = sum_plane(here, *hold(r_in, state))
        r_out = sum_z(here, *hold(r_out, state))
        gc = after(gc, r_out[0], r_in[0][0])
        state = bwd(3, state, gc)
        r_in = sum_z(here, *hold(r_in, state))
        dq, dk, dv, sq, sv = state
        p_wqkv = wgrad3(core, after(x, r_in[0], *r_out[1:]), dq, dk, dv, sq, sv)
        keep, send = p_wqkv
        r_qkv = sum_core(here, [swap((keep, after(send, r_in[1], r_in[3])))])
        g_tok = tok_call(after(ga, r_qkv[0][0]), dq, dk, dv, place, w1)
        (k0, g0), second = r_qkv
        r_qkv = sum_plane(here, (after(k0, g_tok, r_in[2]), g0), second)
        rest = add4(r_out, [after(r_in[0], r_qkv[0][0]), *r_in[1:]])
        own, *far = sum_z(here, *r_qkv)
        over_x = move(after(rest, own), TO_X)
        own = add4([own, *far])
        [rest, over_x], [own] = tied([rest, over_x], [own])
        vectors = [(0, 128 * i, 128) for i in range(6)] + [(1, 0, nblk * 128)]
        g_wout, g_win, g_wao, g_bao, g_g1, g_s1, g_bout, g_g2, g_s2, g_bin = final_call(
            here,
            (rest, move(rest, TO_CORE), over_x, move(over_x, TO_CORE)),
            [(4, True), (nblk, False), (1, False)],
            vectors,
        )
        over_x = move(own, TO_X)
        over_x, g_wout = lax.optimization_barrier((over_x, g_wout))
        shares = (own, move(own, TO_CORE), over_x, move(over_x, TO_CORE))
        g_wqkv, g_bqv = final_call(here, shares, [(3, False)], [(0, 0, 256)])
        vecs = [v.reshape(-1) for v in (g_bqv, g_bao, g_g1, g_s1, g_bin, g_bout, g_g2, g_s2)]
    else:
        p_wao = wgrad_call("wgrad_ao", core, ctx, ga, False)
        for i in range(parts):
            state = bwd(i, state, gc)
        dq, dk, dv, sq, sv = state
        p_wqkv = [v[:, : 3 * SUB] for v in wgrad3(core, x, dq, dk, dv, sq, sv)]
        g_tok = tok_call(ga, dq, dk, dv, place, w1)
        g_wout = reduce_any(*p_wout, True)
        g_win, g_wao, g_wqkv = [reduce_any(*p, False) for p in (p_win, p_wao, p_wqkv)]
        vecs = [jnp.concatenate([sq[0], sv[0]]), sums[5], sums[3], sums[4], sums[2], sums[0], sums[1], sbin]
        own = small_sum(jnp.concatenate([v.reshape(count, -1) for v in vecs], 1))
        vecs = [own[e - s : e] for s, e in zip(sizes, ends)]
        vecs.insert(4, vecs.pop())
    g_bqv, g_bao, g_g1, g_s1, g_bin, g_bout, g_g2, g_s2 = vecs
    return (
        out[None], g_tok[None], g_wqkv, g_bqv, g_wao, g_bao, g_g1, g_s1,
        g_win, g_bin, g_wout, g_bout, g_g2, g_s2,
    )


def solution(mesh):
    rows = P(("replica", "shard"), None, None)
    mat, vec = P("shard", None), P("shard")
    return jax.shard_map(
        shards,
        mesh=mesh,
        in_specs=(rows, P(("replica", "shard")), rows, mat, vec, mat, vec, vec, vec, mat, vec, mat, vec, vec, vec),
        out_specs=(rows, rows, mat, vec, mat, vec, vec, vec, mat, vec, mat, vec, vec, vec),
        check_vma=False,
    )
```

```python
import functools
import jax
import jax.numpy as jnp
from jax import lax
from jax.experimental import pallas as pl
from jax.experimental.pallas import tpu as pltpu
from jax.sharding import PartitionSpec as P

HD = 64
F32 = jnp.float32
BF = jnp.bfloat16
SQRT_HALF = 0.7071067811865476
INV_ROOT_TAU = 0.3989422804014327


def params(mib=60):
    return pltpu.CompilerParams(vmem_limit_bytes=mib << 20)


def dot_nn(a, b):
    return jnp.dot(a, b, preferred_element_type=F32)


def dot_nt(a, b):
    return lax.dot_general(a, b, (((1,), (1,)), ((), ())), preferred_element_type=F32)


def dot_tn(a, b):
    return lax.dot_general(a, b, (((0,), (0,)), ((), ())), preferred_element_type=F32)


def cost(flops, nbytes, trans=0):
    return pl.CostEstimate(flops=int(flops), bytes_accessed=int(nbytes), transcendentals=int(trans))


SUB = 32
ANY = pl.BlockSpec(memory_space=pltpu.HBM)


def loads(place, bufs, lo, hi, target, sem):
    found = []
    for buf in bufs:
        for m in range(buf.shape[0]):
            i = len(found)
            found.append(pltpu.make_async_copy(buf.at[m, pl.ds(lo, hi - lo)], target(place[i]), sem.at[i]))
    return found


def start_all(copies):
    for c in copies:
        c.start()


def wait_all(copies):
    for c in copies:
        c.wait()


def qkv_body(count, place, x_ref, b_ref, *rest):
    bufs, (o_ref, w_vm, sem) = rest[:count], rest[count:]
    step = pl.program_id(0)
    blocks, width = w_vm.shape[0], w_vm.shape[-1]
    copies = loads(place, bufs, 0, blocks, lambda p: w_vm.at[:, p], sem)

    @pl.when(step == 0)
    def _():
        start_all(copies)
        wait_all(copies)

    x = x_ref[...]
    for n in range(blocks):
        w = w_vm[n].reshape(-1, width)
        bias = b_ref[:, n * width : (n + 1) * width]
        o_ref[:, n * width : (n + 1) * width] = (dot_nn(x, w) + bias).astype(BF)


def qkv_call(x, place, w1, bias, rows=256):
    slots, width = x.shape
    pieces = width // SUB
    return pl.pallas_call(
        functools.partial(qkv_body, len(w1)),
        name="qkv",
        grid_spec=pltpu.PrefetchScalarGridSpec(
            num_scalar_prefetch=1,
            grid=(slots // rows,),
            in_specs=[
                pl.BlockSpec((rows, width), lambda i, p: (i, 0)),
                pl.BlockSpec((1, 3 * width), lambda i, p: (0, 0)),
            ] + [ANY] * len(w1),
            out_specs=pl.BlockSpec((rows, 3 * width), lambda i, p: (i, 0)),
            scratch_shapes=[
                pltpu.VMEM((3, pieces, SUB, width), BF),
                pltpu.SemaphoreType.DMA((pieces,)),
            ],
        ),
        out_shape=jax.ShapeDtypeStruct((slots, 3 * width), BF),
        compiler_params=params(32),
        cost_estimate=cost(6 * slots * width * width, 8 * slots * width + 6 * width * width),
    )(place, x, bias, *w1)


def lanes(rows):
    return lax.broadcasted_iota(jnp.int32, (rows, 2 * HD), 1)


def split3(v):
    hi = v.astype(BF).astype(F32)
    mid = (v - hi).astype(BF).astype(F32)
    return hi, mid, v - hi - mid


def attn_fwd_body(rows, len_ref, q_ref, k_ref, v_ref, *rest):
    ctx_ref, qa0_ref, qa1_ref = rest[-3:]
    slots = k_ref.shape[0]
    lane = lanes(slots)
    key_row = lax.broadcasted_iota(jnp.int32, (slots, 2 * HD), 0)
    bias = jnp.where(key_row < len_ref[0], 0.0, -1e30)
    k = k_ref[...].astype(F32)
    k_aug = []
    for h in range(2):
        own = (lane // HD) == h
        spare = (1 - h) * HD
        k_aug.append(jnp.where(own, k, jnp.where(lane == spare, bias, 0.0)).astype(BF))
    v_aug = [jnp.where((lane // HD) == h, v_ref[...].astype(F32), 1.0).astype(BF) for h in range(2)]
    lane_q = lanes(rows)

    def scores(item):
        blk, h = item
        q = q_ref[blk * rows : (blk + 1) * rows, :].astype(F32) * 0.125
        qh = jnp.where((lane_q // HD) == h, q, jnp.where(lane_q == (1 - h) * HD, 1.0, 0.0))
        return qh, dot_nt(qh.astype(BF), k_aug[h])

    items = [(blk, h) for blk in range(slots // rows) for h in range(2)]
    held = scores(items[0])
    outs = []
    for i, (blk, h) in enumerate(items):
        sl = slice(blk * rows, (blk + 1) * rows)
        qh, s = held
        if i + 1 < len(items):
            held = scores(items[i + 1])
        spare = (1 - h) * HD
        top = jnp.max(s, axis=-1, keepdims=True)
        o = dot_nn(jnp.exp(s - top).astype(BF), v_aug[h])
        norm = o[:, spare : spare + 1]
        outs.append(o / norm)
        hi, mid, lo = split3(-(top + jnp.log(norm)))
        qh = jnp.where(lane_q == spare + 1, hi, qh)
        qh = jnp.where(lane_q == spare + 2, mid, qh)
        qh = jnp.where(lane_q == spare + 3, lo, qh)
        (qa0_ref, qa1_ref)[h][sl, :] = qh.astype(BF)
        if h == 1:
            ctx_ref[sl, :] = jnp.where(lane_q < HD, outs[-2], outs[-1]).astype(BF)


def attn_fwd_call(qkv, lengths, part, parts, before, rows=256):
    slots, wide = qkv.shape
    width = wide // 3
    pairs = width // (2 * HD)
    each = pairs // parts
    col = lambda off: pl.BlockSpec((slots, 2 * HD), lambda j, ln: (0, off * pairs + part * each + j))
    out = jax.ShapeDtypeStruct((slots, width), BF)
    extra = list(before or ())
    return pl.pallas_call(
        functools.partial(attn_fwd_body, rows),
        name=f"attn_fwd{part}",
        grid_spec=pltpu.PrefetchScalarGridSpec(
            num_scalar_prefetch=1,
            grid=(each,),
            in_specs=[col(0), col(1), col(2)] + [ANY] * len(extra),
            out_specs=[col(0)] * 3,
        ),
        out_shape=[out, out, out],
        input_output_aliases={4 + i: i for i in range(3)} if before else {},
        compiler_params=params(32),
        cost_estimate=cost(
            16 * slots * slots * width / parts, 12 * slots * width / parts, slots * slots * 2 * each
        ),
    )(lengths, qkv, qkv, qkv, *extra)


def attn_bwd_body(rows, len_ref, qa0_ref, qa1_ref, k_ref, v_ref, ctx_ref, g_ref, *rest):
    dq_ref, dk_ref, dv_ref, sq_ref, sv_ref = rest[-5:]
    slots = k_ref.shape[0]
    lane = lanes(slots)
    key_row = lax.broadcasted_iota(jnp.int32, (slots, 2 * HD), 0)
    bias = jnp.where(key_row < len_ref[0], 0.0, -1e30)
    k = k_ref[...].astype(F32)
    v = v_ref[...].astype(F32)
    k_low = k_ref[...]
    k_aug, v_aug = [], []
    for h in range(2):
        own = (lane // HD) == h
        spare = (1 - h) * HD
        near = (lane > spare) & (lane < spare + 4)
        ones = jnp.where(near, 1.0, 0.0)
        k_aug.append(jnp.where(own, k, jnp.where(lane == spare, bias, ones)).astype(BF))
        v_aug.append(jnp.where(own, v, ones).astype(BF))
    lane_q = lanes(rows)
    items = [(blk, h) for blk in range(slots // rows) for h in range(2)]

    def products(item):
        blk, h = item
        sl = slice(blk * rows, (blk + 1) * rows)
        own = (lane_q // HD) == h
        spare = (1 - h) * HD
        g = g_ref[sl, :].astype(F32)
        delta = jnp.sum(jnp.where(own, g * ctx_ref[sl, :].astype(F32), 0.0), axis=-1, keepdims=True)
        hi, mid, lo = split3(-delta)
        ga = jnp.where(own, g, 0.0)
        ga = jnp.where(lane_q == spare + 1, hi, ga)
        ga = jnp.where(lane_q == spare + 2, mid, ga)
        ga = jnp.where(lane_q == spare + 3, lo, ga).astype(BF)
        return dot_nt(k_aug[h], (qa0_ref, qa1_ref)[h][sl, :]), dot_nt(v_aug[h], ga)

    held = products(items[0])
    dk = [jnp.zeros((slots, 2 * HD), F32)] * 2
    dv = [jnp.zeros((slots, 2 * HD), F32)] * 2
    dqs = []
    for i, (blk, h) in enumerate(items):
        sl = slice(blk * rows, (blk + 1) * rows)
        s, gs = held
        if i + 1 < len(items):
            held = products(items[i + 1])
        p = jnp.exp(s)
        ds = (p * gs).astype(BF)
        dv[h] = dv[h] + dot_nn(p.astype(BF), g_ref[sl, :])
        dk[h] = dk[h] + dot_nn(ds, (qa0_ref, qa1_ref)[h][sl, :])
        dqs.append(dot_tn(ds, k_low))
        if h == 1:
            dq_ref[sl, :] = (jnp.where(lane_q < HD, dqs[-2], dqs[-1]) * 0.125).astype(BF)
    dk_ref[...] = jnp.where(lane < HD, dk[0], dk[1]).astype(BF)
    dv_low = jnp.where(lane < HD, dv[0], dv[1]).astype(BF)
    dv_ref[...] = dv_low
    sq_ref[...] = jnp.sum(dq_ref[...].astype(F32), axis=0, keepdims=True)
    sv_ref[...] = jnp.sum(dv_low.astype(F32), axis=0, keepdims=True)


def attn_bwd_call(qa0, qa1, qkv, ctx, grad_ctx, lengths, part, parts, before, rows=256):
    slots, width = ctx.shape
    pairs = width // (2 * HD)
    each = pairs // parts
    col = lambda off: pl.BlockSpec((slots, 2 * HD), lambda j, ln: (0, off * pairs + part * each + j))
    row = pl.BlockSpec((1, 2 * HD), lambda j, ln: (0, part * each + j))
    out = jax.ShapeDtypeStruct((slots, width), BF)
    vec = jax.ShapeDtypeStruct((1, width), F32)
    extra = list(before or ())
    return pl.pallas_call(
        functools.partial(attn_bwd_body, rows),
        name=f"attn_bwd{part}",
        grid_spec=pltpu.PrefetchScalarGridSpec(
            num_scalar_prefetch=1,
            grid=(each,),
            in_specs=[col(0), col(0), col(1), col(2), col(0), col(0)] + [ANY] * len(extra),
            out_specs=[col(0)] * 3 + [row] * 2,
        ),
        out_shape=[out, out, out, vec, vec],
        input_output_aliases={7 + i: i for i in range(5)} if before else {},
        compiler_params=params(32),
        cost_estimate=cost(
            40 * slots * slots * width / parts, 18 * slots * width / parts, slots * slots * 2 * each
        ),
    )(lengths, qa0, qa1, qkv, qkv, ctx, grad_ctx, *extra)


def norm_stats(resid):
    mean = jnp.mean(resid, axis=-1, keepdims=True)
    centred = resid - mean
    inv = lax.rsqrt(jnp.mean(centred * centred, axis=-1, keepdims=True) + 1e-5)
    return centred * inv, inv


def norm_back(u, normed, inv):
    return inv * (u - jnp.mean(u, axis=-1, keepdims=True) - normed * jnp.mean(u * normed, axis=-1, keepdims=True))


def colsum(v):
    return jnp.sum(v, axis=0, keepdims=True)


def row_body(n2, len_ref, place, x_ref, ctx_ref, cot_ref, vec_ref, bin_ref, *rest):
    b2 = rest[:n2]
    (
        out_ref, act_ref, hid_ref, gf_ref, gp_ref, ga_ref, gc_ref, sums_ref, sbin_ref,
        wa, wi, wo, slope, sem,
    ) = rest[n2:]
    step = pl.program_id(0)
    rows, width = x_ref.shape
    nblk = wi.shape[0]
    copies = [
        loads(place, b2, 0, 1, lambda p: wa.at[pl.ds(p, 1)], sem.at[0]),
        loads(place, b2, 1, 1 + nblk, lambda p: wi.at[:, p], sem.at[1]),
        loads(place, b2, 1 + nblk, 5 + nblk, lambda p: wo.at[p], sem.at[2]),
    ]

    @pl.when(step == 0)
    def _():
        for c in copies:
            start_all(c)
        sums_ref[...] = jnp.zeros_like(sums_ref)
        sbin_ref[...] = jnp.zeros_like(sbin_ref)

    def ready(i):
        @pl.when(step == 0)
        def _():
            wait_all(copies[i])

    bao, gain1, shift1, bout, gain2, shift2 = [vec_ref[i : i + 1, :] for i in range(6)]
    ready(0)
    w_ao = wa[...].reshape(width, width)
    resid1 = x_ref[...].astype(F32) + dot_nn(ctx_ref[...], w_ao) + bao
    normed1, inv1 = norm_stats(resid1)
    hidden = normed1 * gain1 + shift1
    low = hidden.astype(BF)
    hid_ref[...] = low
    acc = jnp.zeros((rows, width), F32)
    per = wo.shape[0] // nblk
    ready(1)
    for n in range(nblk):
        pre = dot_nn(low, wi[n].reshape(width, width)) + bin_ref[n : n + 1, :]
        phi = 0.5 + 0.5 * lax.erf(pre * SQRT_HALF)
        slope[n] = (phi + pre * (INV_ROOT_TAU * jnp.exp(-0.5 * pre * pre))).astype(slope.dtype)
        act = (pre * phi).astype(BF)
        act_ref[:, n * width : (n + 1) * width] = act
        if n == 0:
            ready(2)
        acc = acc + dot_nn(act, wo[n * per : (n + 1) * per].reshape(width, width))
    resid2 = hidden + acc + bout
    normed2, inv2 = norm_stats(resid2)
    row_id = lax.broadcasted_iota(jnp.int32, (rows, 1), 0) + step * rows
    valid = (row_id < len_ref[0]).astype(F32)
    out_ref[...] = ((normed2 * gain2 + shift2) * valid).astype(BF)
    gz = cot_ref[...].astype(F32) * valid
    sums_ref[0:1, :] += colsum(gz * normed2)
    sums_ref[1:2, :] += colsum(gz)
    g_resid2 = norm_back(gz * gain2, normed2, inv2)
    gf = g_resid2.astype(BF)
    gf_ref[...] = gf
    sums_ref[2:3, :] += colsum(gf.astype(F32))
    acc = g_resid2
    for n in range(nblk):
        g_act = dot_nt(gf, wo[n * per : (n + 1) * per].reshape(width, width))
        gp = (g_act * slope[n].astype(F32)).astype(BF)
        gp_ref[:, n * width : (n + 1) * width] = gp
        sbin_ref[n : n + 1, :] += colsum(gp.astype(F32))
        acc = acc + dot_nt(gp, wi[n].reshape(width, width))
    sums_ref[3:4, :] += colsum(acc * normed1)
    sums_ref[4:5, :] += colsum(acc)
    g_attn = norm_back(acc * gain1, normed1, inv1).astype(BF)
    ga_ref[...] = g_attn
    sums_ref[5:6, :] += colsum(g_attn.astype(F32))
    gc_ref[...] = dot_nt(g_attn, w_ao).astype(BF)


def row_call(x, ctx, cot, place, w2, vecs, b_in, lengths, rows=256):
    slots, width = x.shape
    pieces, sub = width // SUB, SUB
    nblk = b_in.shape[0]
    ff = nblk * width
    blk = pl.BlockSpec((rows, width), lambda i, ln, p: (i, 0))
    big = pl.BlockSpec((rows, ff), lambda i, ln, p: (i, 0), pipeline_mode=pl.Buffered(1 if rows > 256 else 2))
    const = lambda r: pl.BlockSpec((r, width), lambda i, ln, p: (0, 0))
    o = jax.ShapeDtypeStruct((slots, width), BF)
    ob = jax.ShapeDtypeStruct((slots, ff), BF)
    return pl.pallas_call(
        functools.partial(row_body, len(w2)),
        name="row_local",
        grid_spec=pltpu.PrefetchScalarGridSpec(
            num_scalar_prefetch=2,
            grid=(slots // rows,),
            in_specs=[blk, blk, blk, const(8), const(nblk)] + [ANY] * len(w2),
            out_specs=[blk, big, blk, blk, big, blk, blk, const(8), const(nblk)],
            scratch_shapes=[
                pltpu.VMEM((pieces, sub, width), BF),
                pltpu.VMEM((nblk, pieces, sub, width), BF),
                pltpu.VMEM((pieces, 4, sub, width), BF),
                pltpu.VMEM((nblk, rows, width), BF),
                pltpu.SemaphoreType.DMA((3, pieces)),
            ],
        ),
        out_shape=[
            o, ob, o, o, ob, o, o,
            jax.ShapeDtypeStruct((8, width), F32),
            jax.ShapeDtypeStruct((nblk, width), F32),
        ],
        compiler_params=params(),
        cost_estimate=cost(36 * slots * width * width, 40 * slots * width + 18 * width * width, 2 * slots * ff),
    )(lengths, place, x, ctx, cot, vecs, b_in, *w2)


def halves(core, value, keep_ref, send_ref):
    count, rows, width = keep_ref.shape
    value = value.reshape(count, 2, rows, width)
    even, odd = value[:, 0], value[:, 1]

    @pl.when(core == 0)
    def _():
        keep_ref[...] = even
        send_ref[...] = odd

    @pl.when(core != 0)
    def _():
        keep_ref[...] = odd
        send_ref[...] = even


LINES = 16


def lines_of(*lines):
    width, segments = lines[0][0], [line[1:] for line in lines]
    row = lax.broadcasted_iota(jnp.int32, (LINES, width), 0)
    value = jnp.zeros((LINES, width), F32)
    for i, segs in enumerate(segments):
        used = sum(v.shape[1] for v in segs)
        line = jnp.concatenate(segs + [jnp.zeros((1, width - used), F32)] * (used < width), 1)
        value = jnp.where(row == i, line, value)
    return value.astype(BF)


def wgrad_body(core, a_ref, b_ref, keep_ref, send_ref):
    halves(core[0], dot_tn(a_ref[...], b_ref[...]).astype(BF), keep_ref, send_ref)


def wgrad_call(name, core, a, b, by_rows, tile=1024):
    slots, m = a.shape
    width = a.shape[1] if not by_rows else b.shape[1]
    blocks = m // width if by_rows else b.shape[1] // m
    pieces = width // SUB
    if by_rows:
        grid = (1, m // tile)
        block = (tile // (2 * SUB * blocks), blocks * SUB, width)
        where = lambda j, i, c: (i, 0, 0)
    else:
        grid = (blocks, m // tile)
        block = (tile // (2 * SUB), SUB, width)
        where = lambda j, i, c: (i, j, 0)
    out = jax.ShapeDtypeStruct((pieces // 2, blocks * SUB, width), BF)
    return pl.pallas_call(
        wgrad_body,
        name=name,
        grid_spec=pltpu.PrefetchScalarGridSpec(
            num_scalar_prefetch=1,
            grid=grid,
            in_specs=[
                pl.BlockSpec((slots, tile), lambda j, i, c: (0, i)),
                pl.BlockSpec((slots, width), lambda j, i, c: (0, j)),
            ],
            out_specs=[pl.BlockSpec(block, where)] * 2,
        ),
        out_shape=[out, out],
        compiler_params=params(32),
        cost_estimate=cost(2 * slots * m * b.shape[1], 2 * (slots * (m + b.shape[1]) + m * b.shape[1])),
    )(core, a, b)


def wgrad_ao_body(core, a_ref, b_ref, sums_ref, sbin_ref, keep_ref, send_ref):
    value = dot_tn(a_ref[...], b_ref[...]).astype(BF)
    halves(core[0], value, keep_ref.at[:, pl.ds(0, SUB)], send_ref.at[:, pl.ds(0, SUB)])
    count, _, width = keep_ref.shape
    owners = count // 2
    part, four = width // owners, sbin_ref.shape[0] * width // owners
    for s in range(owners):
        segs = [sums_ref[v : v + 1, s * part : (s + 1) * part] for v in (5, 3, 4, 2, 0, 1)]
        row, col = s * four // width, s * four % width
        value = lines_of([width, *segs], [width, sbin_ref[row : row + 1, col : col + four]])
        for ref in (keep_ref, send_ref):
            for x in (0, 1):
                ref[2 * s + x, SUB : SUB + LINES] = value


def wgrad_ao(core, a, b, sums, sbin):
    slots, m = a.shape
    full = lambda v: pl.BlockSpec(v.shape, lambda t, c: (0, 0))
    shape = (m // SUB // 2, SUB + LINES, m)
    return pl.pallas_call(
        wgrad_ao_body,
        name="wgrad_ao",
        grid_spec=pltpu.PrefetchScalarGridSpec(
            num_scalar_prefetch=1,
            grid=(1,),
            in_specs=[full(v) for v in (a, b, sums, sbin)],
            out_specs=[pl.BlockSpec(shape, lambda t, c: (0, 0, 0))] * 2,
        ),
        out_shape=[jax.ShapeDtypeStruct(shape, BF)] * 2,
        compiler_params=params(32),
        cost_estimate=cost(2 * slots * m * m, 4 * slots * m + 2 * m * m),
    )(core, a, b, sums, sbin)


def wgrad3_body(core, a_ref, q_ref, k_ref, v_ref, sq_ref, sv_ref, keep_ref, send_ref):
    for n, ref in enumerate((q_ref, k_ref, v_ref)):
        value = dot_tn(a_ref[...], ref[...]).astype(BF)
        rows = pl.ds(n * SUB, SUB)
        halves(core[0], value, keep_ref.at[:, rows], send_ref.at[:, rows])
    count, _, width = keep_ref.shape
    line = jnp.where(pl.program_id(0) == 0, sq_ref[...], sv_ref[...])
    part = 2 * width // count
    for s in range(count // 2):
        value = lines_of([width, line[:, s * part : (s + 1) * part]])
        for ref in (keep_ref, send_ref):
            for x in (0, 1):
                ref[2 * s + x, 3 * SUB : 3 * SUB + LINES] = value


def wgrad3(core, a, dq, dk, dv, sq, sv):
    slots, m = a.shape
    tile = m // 2
    full = pl.BlockSpec((slots, m), lambda i, c: (0, 0))
    vec = pl.BlockSpec((1, m), lambda i, c: (0, 0))
    block = pl.BlockSpec((tile // (2 * SUB), 3 * SUB + LINES, m), lambda i, c: (i, 0, 0))
    out = jax.ShapeDtypeStruct((m // SUB // 2, 3 * SUB + LINES, m), BF)
    return pl.pallas_call(
        wgrad3_body,
        name="wgrad_qkv",
        grid_spec=pltpu.PrefetchScalarGridSpec(
            num_scalar_prefetch=1,
            grid=(2,),
            in_specs=[pl.BlockSpec((slots, tile), lambda i, c: (0, i)), full, full, full, vec, vec],
            out_specs=[block, block],
        ),
        out_shape=[out, out],
        compiler_params=params(32),
        cost_estimate=cost(6 * slots * m * m, 14 * slots * m),
    )(core, a, dq, dk, dv, sq, sv)


def tok_body(count, place, g_ref, dq_ref, dk_ref, dv_ref, *rest):
    bufs, (o_ref, w_vm, sem) = rest[:count], rest[count:]
    step = pl.program_id(0)
    width = g_ref.shape[1]
    copies = loads(place, bufs, 0, 3, lambda p: w_vm.at[:, p], sem)

    @pl.when(step == 0)
    def _():
        start_all(copies)
        wait_all(copies)

    acc = g_ref[...].astype(F32)
    for n, ref in enumerate((dq_ref, dk_ref, dv_ref)):
        acc = acc + dot_nt(ref[...], w_vm[n].reshape(width, width))
    o_ref[...] = acc.astype(BF)


def tok_call(g, dq, dk, dv, place, w1, rows=256):
    slots, width = g.shape
    pieces = width // SUB
    blk = pl.BlockSpec((rows, width), lambda i, p: (i, 0))
    return pl.pallas_call(
        functools.partial(tok_body, len(w1)),
        name="grad_tok",
        grid_spec=pltpu.PrefetchScalarGridSpec(
            num_scalar_prefetch=1,
            grid=(slots // rows,),
            in_specs=[blk, blk, blk, blk] + [ANY] * len(w1),
            out_specs=blk,
            scratch_shapes=[pltpu.VMEM((3, pieces, SUB, width), BF), pltpu.SemaphoreType.DMA((pieces,))],
        ),
        out_shape=jax.ShapeDtypeStruct((slots, width), BF),
        compiler_params=params(32),
        cost_estimate=cost(6 * slots * width * width, 16 * slots * width),
    )(place, g, dq, dk, dv, *w1)


def total(*terms):
    acc = terms[0].astype(F32)
    for t in terms[1:]:
        acc = acc + t.astype(F32)
    return acc.astype(BF)


def add1_body(count, here, *refs):
    ins, outs = refs[: 8 * count], refs[8 * count :]
    for view in range(4):
        n0 = 0
        for i in range(count):
            a, b = ins[8 * i + 2 * view], ins[8 * i + 2 * view + 1]
            n = a.shape[3]
            outs[view][0, n0 : n0 + n] = total(a[0, 0, 0], b[0, 0, 0])
            n0 += n


def add1(here, pairs):
    width = pairs[0][0].shape[-1]
    views = []
    for half, own in ((0, 0), (0, 1), (1, 0), (1, 1)):
        def where(t, h, half=half, own=own):
            z, j = 2 * half + t // 2, t % 2
            if half == 0:
                return (z, j, h[0] if own else 1 - h[0], 0, 0)
            return (z, h[1] if own else 1 - h[1], j, 0, 0)
        views.append(where)
    specs, args, rows = [], [], 0
    for keep, got in pairs:
        n = keep.shape[1]
        rows += n
        for where in views:
            for arr in (keep, got):
                specs.append(pl.BlockSpec((1, 1, 1, n, width), where))
                args.append(arr.reshape(4, 2, 2, n, width))
    out = jax.ShapeDtypeStruct((4, rows, width), BF)
    return pl.pallas_call(
        functools.partial(add1_body, len(pairs)),
        name="add_core",
        grid_spec=pltpu.PrefetchScalarGridSpec(
            num_scalar_prefetch=1,
            grid=(4,),
            in_specs=specs,
            out_specs=[pl.BlockSpec((1, rows, width), lambda t, h: (t, 0, 0))] * 4,
        ),
        out_shape=[out] * 4,
        compiler_params=params(28),
        cost_estimate=cost(16 * rows * width, 96 * rows * width),
    )(here, *args)


def add2_body(here, *refs):
    ins, outs = refs[:8], refs[8:]
    for view in range(4):
        outs[view][0] = total(ins[2 * view][0, 0], ins[2 * view + 1][0, 0])


def add2(here, first, second):
    _, rows, width = first[0].shape
    specs, args = [], []
    for axis, pair in ((1, first), (0, second)):
        for own in (0, 1):
            for arr in pair:
                specs.append(pl.BlockSpec(
                    (1, 1, rows, width),
                    lambda t, h, axis=axis, own=own: (t, h[axis] if own else 1 - h[axis], 0, 0),
                ))
                args.append(arr.reshape(2, 2, rows, width))
    out = jax.ShapeDtypeStruct((2, rows, width), BF)
    return pl.pallas_call(
        add2_body,
        name="add_plane",
        grid_spec=pltpu.PrefetchScalarGridSpec(
            num_scalar_prefetch=1,
            grid=(2,),
            in_specs=specs,
            out_specs=[pl.BlockSpec((1, rows, width), lambda t, h: (t, 0, 0))] * 4,
        ),
        out_shape=[out] * 4,
        compiler_params=params(28),
        cost_estimate=cost(8 * rows * width, 48 * rows * width),
    )(here, *args)


def add3_body(here, ak, ag, bk, bg, *outs):
    for k, out in enumerate(outs):
        to = lax.rem(here[2] + k, 4)
        spot = lax.rem(to, 2)

        @pl.when(to < 2)
        def _():
            out[0] = total(ak[spot], ag[spot])

        @pl.when(to >= 2)
        def _():
            out[0] = total(bk[spot], bg[spot])


def add3(here, first, second):
    _, rows, width = first[0].shape
    full = pl.BlockSpec((2, rows, width), lambda t, h: (0, 0, 0))
    one = pl.BlockSpec((1, rows, width), lambda t, h: (0, 0, 0))
    return pl.pallas_call(
        add3_body,
        name="add_z",
        grid_spec=pltpu.PrefetchScalarGridSpec(
            num_scalar_prefetch=1, grid=(1,), in_specs=[full] * 4, out_specs=[one] * 4,
        ),
        out_shape=[jax.ShapeDtypeStruct((1, rows, width), BF)] * 4,
        compiler_params=params(28),
        cost_estimate=cost(4 * rows * width, 24 * rows * width),
    )(here, *first, *second)


def add4_body(*refs):
    ins, out = refs[:-1], refs[-1]
    n0 = 0
    for i in range(0, len(ins), 4):
        n = ins[i].shape[1]
        out[:, n0 : n0 + n] = total(*[r[...] for r in ins[i : i + 4]])
        n0 += n


def add4(*groups):
    spec = lambda shape: pl.BlockSpec(shape, lambda t: (0,) * len(shape))
    width = groups[0][0].shape[-1]
    shape = (1, sum(g[0].shape[1] for g in groups), width)
    parts = [v for g in groups for v in g]
    size = shape[1] * width
    return pl.pallas_call(
        add4_body,
        name="add_last",
        grid=(1,),
        in_specs=[spec(v.shape) for v in parts],
        out_specs=spec(shape),
        out_shape=jax.ShapeDtypeStruct(shape, BF),
        compiler_params=params(28),
        cost_estimate=cost(3 * size, 10 * size),
    )(*parts)


def final_body(kinds, vectors, here, own, core, over_x, both, *outs):
    mine_at = 2 * here[0] + here[3]
    mats, vecs = outs[: len(kinds)], outs[len(kinds) :]
    for flip, ref in enumerate((own, core, over_x, both)):
        share = jnp.bitwise_xor(mine_at, flip)
        n0 = 0
        for (blocks, by_rows), out in zip(kinds, mats):
            width = ref.shape[-1]
            for n in range(blocks):
                value = ref[0, n0 : n0 + SUB].astype(F32)
                n0 += SUB
                if by_rows:
                    out[pl.ds(pl.multiple_of(share * blocks * SUB, SUB) + n * SUB, SUB), :] = value
                else:
                    out[pl.ds(pl.multiple_of(share * SUB, SUB), SUB), n * width : (n + 1) * width] = value

        @pl.when(share == 0)
        def _():
            lines = ref[0, n0 : n0 + LINES].astype(F32)
            for (row, lane, size), out in zip(vectors, vecs):
                out[...] = lines[row : row + 1, lane : lane + size]


def final_call(here, parts, kinds, vectors):
    shape = parts[0].shape
    width = shape[-1]
    shapes = [
        (4 * blocks * SUB, width) if by_rows else (4 * SUB, blocks * width) for blocks, by_rows in kinds
    ] + [(1, size) for _, _, size in vectors]
    return pl.pallas_call(
        functools.partial(final_body, kinds, vectors),
        name="final",
        grid_spec=pltpu.PrefetchScalarGridSpec(
            num_scalar_prefetch=1,
            grid=(1,),
            in_specs=[pl.BlockSpec(shape, lambda t, h: (0, 0, 0))] * 4,
            out_specs=[pl.BlockSpec(sh, lambda t, h: (0, 0)) for sh in shapes],
        ),
        out_shape=[jax.ShapeDtypeStruct(sh, F32) for sh in shapes],
        compiler_params=params(28),
        cost_estimate=cost(1, 24 * parts[0].size),
    )(here, *parts)


BOTH = ("shard", "replica")
AXES = ("replica", "shard")


def table(fn):
    pairs = []
    for r in range(4):
        for s in range(8):
            x, y, z, c = fn(r // 2, s % 2, s // 2, r % 2)
            pairs.append((r * 8 + s, (x * 2 + c) * 8 + z * 2 + y))
    return pairs


TO_CORE = table(lambda x, y, z, c: (x, y, z, 1 - c))
TO_X = table(lambda x, y, z, c: (1 - x, y, z, c))
TO_XCORE = table(lambda x, y, z, c: (1 - x, y, z, 1 - c))
TO_Y = table(lambda x, y, z, c: (x, 1 - y, z, c))
TO_Z = [table(lambda x, y, z, c, k=k: (x, y, (z + k) % 4, c)) for k in range(4)]


def move(v, pairs):
    return lax.ppermute(v, AXES, pairs)


def regular():
    return lax.axis_size("shard") == 8 and lax.axis_size("replica") == 4


def place_of():
    r, s = lax.axis_index("replica"), lax.axis_index("shard")
    return r // 2, s % 2, s // 2, r % 2


def pack_body(share, *refs):
    ins, out = refs[:-1], refs[-1]
    width = out.shape[-1]
    n0 = 0
    for ref in ins:
        rows, cols = ref.shape
        if rows > SUB:
            out[0, n0 : n0 + rows // SUB] = ref[...].reshape(rows // SUB, SUB, width)
            n0 += rows // SUB
        else:
            for n in range(cols // width):
                out[0, n0 + n] = ref[:, n * width : (n + 1) * width]
            n0 += cols // width


def pack(share, mats, width):
    shapes = [(m.shape[0] // 4, m.shape[1]) for m in mats]
    blocks = sum(r * c for r, c in shapes) // (SUB * width)
    return pl.pallas_call(
        pack_body,
        name="pack",
        grid_spec=pltpu.PrefetchScalarGridSpec(
            num_scalar_prefetch=1,
            grid=(1,),
            in_specs=[pl.BlockSpec(sh, lambda t, r: (r[0], 0)) for sh in shapes],
            out_specs=pl.BlockSpec((1, blocks, SUB, width), lambda t, r: (0, 0, 0, 0)),
        ),
        out_shape=jax.ShapeDtypeStruct((1, blocks, SUB, width), BF),
        compiler_params=params(),
        cost_estimate=cost(1, 4 * blocks * SUB * width),
    )(share, *mats)


def pack_first_body(share, w_ref, *refs):
    vecs, out = refs[:-1], refs[-1]
    rows, width = 3 * SUB, out.shape[-1]
    for n in range(3):
        out[0, n * SUB : (n + 1) * SUB] = w_ref[:, n * width : (n + 1) * width]
    segs = [v[...].astype(F32) for v in vecs]
    out[0, rows : rows + LINES] = lines_of([width, *segs[:-1]], [width, segs[-1]])


def pack_first(share, w_qkv, vecs, width):
    rows = w_qkv.shape[0] // 4
    vecs = [v.reshape(1, -1) for v in vecs]
    shape = (1, 3 * rows + LINES, width)
    return pl.pallas_call(
        pack_first_body,
        name="pack_first",
        grid_spec=pltpu.PrefetchScalarGridSpec(
            num_scalar_prefetch=1,
            grid=(1,),
            in_specs=[pl.BlockSpec((rows, 3 * width), lambda t, r: (r[0], 0))]
            + [pl.BlockSpec(v.shape, lambda t, r: (0, 0)) for v in vecs],
            out_specs=pl.BlockSpec(shape, lambda t, r: (0, 0, 0)),
        ),
        out_shape=jax.ShapeDtypeStruct(shape, BF),
        compiler_params=params(),
        cost_estimate=cost(1, 12 * rows * width),
    )(share, w_qkv, *vecs)


def after(v, *deps):
    return lax.optimization_barrier((v,) + deps)[0]


def to_core(bufs):
    return [move(v, TO_CORE) for v in bufs]


def tied(*groups):
    flat = lax.optimization_barrier([v for g in groups for v in g])
    out = []
    for g in groups:
        out.append(flat[: len(g)])
        flat = flat[len(g) :]
    return out


def gather_places(order):
    x, y, z, c = place_of()
    spots = []
    for fc in (0, 1):
        for k, fx, fy in order:
            spots.append((((z - k) % 4) * 2 + (y ^ fy)) * 4 + (x ^ fx) * 2 + (c ^ fc))
    return jnp.stack(spots).astype(jnp.int32)


FIRST = [
    (k0 + k, fx, fy)
    for k0, fx, fy in ((0, 0, 0), (2, 0, 0), (0, 0, 1), (2, 1, 0), (0, 1, 0), (2, 0, 1), (0, 1, 1), (2, 1, 1))
    for k in (0, 1)
]
SECOND = [
    (0, 0, 0), (0, 1, 0), (1, 0, 0), (3, 0, 0), (2, 0, 0), (0, 0, 1), (1, 1, 0), (3, 1, 0),
    (1, 0, 1), (3, 0, 1), (2, 1, 0), (0, 1, 1), (2, 0, 1), (3, 1, 1), (1, 1, 1), (2, 1, 1),
]


def spread(w, blocks, wide):
    full = lax.all_gather(w, "shard", axis=0, tiled=True)
    if full.shape[1] == wide:
        return full.reshape(-1, blocks, SUB, wide)
    return full.reshape(-1, SUB, blocks, wide).transpose(0, 2, 1, 3)


def sum_core(here, pairs):
    a_send, a_keep, b_send, b_keep = add1(here, pairs)
    return (a_keep, move(a_send, TO_X)), (b_keep, move(b_send, TO_Y))


def sum_plane(here, first, second):
    a_send, a_keep, b_send, b_keep = add2(here, first, second)
    return (a_keep, move(a_send, TO_Y)), (b_keep, move(b_send, TO_X))


def sum_z(here, first, second):
    own, *sends = add3(here, first, second)
    return [own] + [move(v, TO_Z[k + 1]) for k, v in enumerate(sends)]


def small_gather(lines):
    x, y, z, c = place_of()
    rows = jnp.concatenate([lines, move(lines, TO_Y)], 0)
    spots = jnp.stack([((z - k) % 4) * 2 + (y ^ f) for f in (0, 1) for k in range(4)])
    pick = (jnp.arange(8)[:, None] == spots[None, :]).astype(BF)
    return dot_nn(pick, rows)


def small_sum(rows):
    return lax.dynamic_index_in_dim(lax.psum(rows, BOTH), lax.axis_index("shard"), 0, keepdims=False)


def reduce_any(keep, send, by_rows):
    half, rows, wide = keep.shape
    full = jnp.stack([keep, send], 1).reshape(2 * half, rows // SUB, SUB, wide)
    full = full.reshape(-1, wide) if by_rows else full.transpose(0, 2, 1, 3).reshape(2 * half * SUB, -1)
    part = lax.psum_scatter(full, "shard", scatter_dimension=0, tiled=True)
    return lax.psum(part, "replica").astype(F32)


def shards(
    tokens, lengths, cotangent, w_qkv, b_qv, w_attn_out, b_attn_out, ln1_gain, ln1_bias,
    w_ffn_in, b_ffn_in, w_ffn_out, b_ffn_out, ln2_gain, ln2_bias,
):
    _, slots, width = tokens.shape
    nblk = w_ffn_in.shape[1] // width
    count = lax.axis_size("shard")
    x = tokens.reshape(slots, width)
    cot = cotangent.reshape(slots, width)
    small = [b_qv, b_attn_out, ln1_gain, ln1_bias, b_ffn_out, ln2_gain, ln2_bias, b_ffn_in]
    sizes = [v.shape[0] for v in small]
    ends = [sum(sizes[: i + 1]) for i in range(len(sizes))]

    if regular():
        share = lax.axis_index("replica").reshape(1).astype(jnp.int32)
        first = pack_first(share, w_qkv, small, width)
        second = pack(share, [after(w_attn_out, first), w_ffn_in, w_ffn_out], width)
        xo, yo = move(second, TO_X), move(second, TO_Y)
        along = [first] + [move(first, TO_Z[k]) for k in (1, 2, 3)]
        *along, xo, yo = lax.optimization_barrier((*along, xo, yo))
        a1, b1 = [
            jnp.concatenate([v[:, : 3 * SUB] for v in pair], 0).reshape(2, 3, SUB, width)
            for pair in (along[:2], along[2:])
        ]
        lines = jnp.concatenate([v[:, 3 * SUB : 3 * SUB + 2] for v in along], 0)
        rows = small_gather(lines.reshape(4, 2 * width)[:, : ends[-1]])
        second = after(second, along[3])
        near, *far = [move(second, TO_Z[k]) for k in (1, 2, 3)]
        plane = [move(a1, TO_Y), move(b1, TO_X), move(a1, TO_X), move(b1, TO_Y)]
        first = [a1, b1]
        cores = to_core(first)
        plane, cores = tied(plane, cores)
        last = [move(plane[0], TO_X), move(plane[1], TO_Y)]
        more = to_core(plane)
        _, [near, far[1]] = tied(last, [near, far[1]])
        w1 = [*first, *plane, *last, *cores, *more, *to_core(last)]
        r13 = jnp.concatenate([near, far[1]], 0)
        x1, y1 = move(r13, TO_X), move(r13, TO_Y)
        place, place2 = gather_places(FIRST), gather_places(SECOND)
        here = jnp.stack(place_of()).astype(jnp.int32)
    else:
        w1 = [spread(w_qkv, 3, width)]
        w2 = [spread(w_attn_out, 1, width), spread(w_ffn_in, nblk, width), spread(w_ffn_out, 4, width)]
        w2 = [jnp.concatenate(w2, 1)]
        place = place2 = jnp.arange(width // SUB, dtype=jnp.int32)
        here = jnp.zeros((4,), jnp.int32)
    core = here[3:]

    if not regular():
        rows = lax.all_gather(jnp.concatenate(small), "shard", axis=0).astype(F32)
    b_qv, bao, gain1, shift1, bout, gain2, shift2, b_in = [
        rows[:, e - s : e].reshape(-1) for s, e in zip(sizes, ends)
    ]
    bias3 = jnp.concatenate([b_qv[:width], jnp.zeros((width,), F32), b_qv[width:]]).reshape(1, -1)
    zero = jnp.zeros((width,), F32)
    vecs = jnp.stack([bao, gain1, shift1, bout, gain2, shift2, zero, zero])

    qkv = qkv_call(x, place, w1, bias3)
    parts = 4
    fwd = lambda i, state: attn_fwd_call(qkv, lengths, i, parts, state)
    state = fwd(0, None)
    if regular():
        [r2], [x1, y1], state = tied([far[0]], [x1, y1], state)
        c2 = jnp.concatenate([r2, yo], 0)
        x2, y2 = move(c2, TO_X), move(jnp.concatenate([r2, x1[1:]], 0), TO_Y)
        cores = to_core([second, xo, r13, x1, y1])
        state = fwd(1, state)
        cores, state = tied(cores, state)
        state = fwd(2, state)
        [x2, y2], state = tied([x2, y2], state)
        x3, y3 = move(y1[:1], TO_X), move(x2[:1], TO_Y)
        more = to_core([c2, x2, y2])
        more, state = tied(more, state)
        state = fwd(3, state)
        last, state = tied([x3, y3], state)
        w2 = [second, xo, r13, c2, x1, y1, x2, y2, *last]
        w2 += [*cores[:3], more[0], *cores[3:], *more[1:], *to_core(last)]
    else:
        for i in range(1, parts):
            state = fwd(i, state)
    ctx, qa0, qa1 = state
    out, act, low, gf, gp, ga, gc, sums, sbin = row_call(
        x, ctx, cot, place2, w2, vecs, b_in.reshape(nblk, width), lengths
    )
    p_wout = wgrad_call("wgrad_out", core, act, gf, True)
    p_win = wgrad_call("wgrad_in", core, low, gp, False)
    state = None
    bwd = lambda i, state, g: attn_bwd_call(qa0, qa1, qkv, ctx, g, lengths, i, parts, state)
    if regular():
        swap = lambda p: (p[0], move(p[1], TO_CORE))
        r_out = sum_core(here, [swap(p_wout)])
        p_wao = wgrad_ao(core, ctx, after(ga, r_out[0][0]), sums, sbin)
        r_in = sum_core(here, [swap(p_win), swap(p_wao)])
        def hold(r, state):
            (k0, g0), second = r
            return (after(k0, state[3]), g0), second

        gc = after(gc, r_in[0][0])
        state = bwd(0, None, gc)
        r_out = sum_plane(here, *hold(r_out, state))
        gc = after(gc, r_out[0][0])
        state = bwd(1, state, gc)
        state = bwd(2, state, gc)
        r_in = sum_plane(here, *hold(r_in, state))
        r_out = sum_z(here, *hold(r_out, state))
        gc = after(gc, r_out[0], r_in[0][0])
        state = bwd(3, state, gc)
        r_in = sum_z(here, *hold(r_in, state))
        dq, dk, dv, sq, sv = state
        p_wqkv = wgrad3(core, after(x, r_in[0], *r_out[1:]), dq, dk, dv, sq, sv)
        keep, send = p_wqkv
        r_qkv = sum_core(here, [swap((keep, after(send, r_in[1], r_in[3])))])
        g_tok = tok_call(after(ga, r_qkv[0][0]), dq, dk, dv, place, w1)
        (k0, g0), second = r_qkv
        r_qkv = sum_plane(here, (after(k0, g_tok, r_in[2]), g0), second)
        rest = add4(r_out, [after(r_in[0], r_qkv[0][0]), *r_in[1:]])
        own, *far = sum_z(here, *r_qkv)
        over_x = move(after(rest, own), TO_X)
        own = add4([own, *far])
        [rest, over_x], [own] = tied([rest, over_x], [own])
        vectors = [(0, 128 * i, 128) for i in range(6)] + [(1, 0, nblk * 128)]
        g_wout, g_win, g_wao, g_bao, g_g1, g_s1, g_bout, g_g2, g_s2, g_bin = final_call(
            here,
            (rest, move(rest, TO_CORE), over_x, move(over_x, TO_CORE)),
            [(4, True), (nblk, False), (1, False)],
            vectors,
        )
        over_x = move(own, TO_X)
        over_x, g_wout = lax.optimization_barrier((over_x, g_wout))
        shares = (own, move(own, TO_CORE), over_x, move(over_x, TO_CORE))
        g_wqkv, g_bqv = final_call(here, shares, [(3, False)], [(0, 0, 256)])
        vecs = [v.reshape(-1) for v in (g_bqv, g_bao, g_g1, g_s1, g_bin, g_bout, g_g2, g_s2)]
    else:
        p_wao = wgrad_call("wgrad_ao", core, ctx, ga, False)
        for i in range(parts):
            state = bwd(i, state, gc)
        dq, dk, dv, sq, sv = state
        p_wqkv = [v[:, : 3 * SUB] for v in wgrad3(core, x, dq, dk, dv, sq, sv)]
        g_tok = tok_call(ga, dq, dk, dv, place, w1)
        g_wout = reduce_any(*p_wout, True)
        g_win, g_wao, g_wqkv = [reduce_any(*p, False) for p in (p_win, p_wao, p_wqkv)]
        vecs = [jnp.concatenate([sq[0], sv[0]]), sums[5], sums[3], sums[4], sums[2], sums[0], sums[1], sbin]
        own = small_sum(jnp.concatenate([v.reshape(count, -1) for v in vecs], 1))
        vecs = [own[e - s : e] for s, e in zip(sizes, ends)]
        vecs.insert(4, vecs.pop())
    g_bqv, g_bao, g_g1, g_s1, g_bin, g_bout, g_g2, g_s2 = vecs
    return (
        out[None], g_tok[None], g_wqkv, g_bqv, g_wao, g_bao, g_g1, g_s1,
        g_win, g_bin, g_wout, g_bout, g_g2, g_s2,
    )


def solution(mesh):
    rows = P(("replica", "shard"), None, None)
    mat, vec = P("shard", None), P("shard")
    return jax.shard_map(
        shards,
        mesh=mesh,
        in_specs=(rows, P(("replica", "shard")), rows, mat, vec, mat, vec, vec, vec, mat, vec, mat, vec, vec, vec),
        out_specs=(rows, rows, mat, vec, mat, vec, vec, vec, mat, vec, mat, vec, vec, vec),
        check_vma=False,
    )
```

```python
import functools
import jax
import jax.numpy as jnp
from jax import lax
from jax.experimental import pallas as pl
from jax.experimental.pallas import tpu as pltpu
from jax.sharding import PartitionSpec as P

HD = 64
F32 = jnp.float32
BF = jnp.bfloat16
SQRT_HALF = 0.7071067811865476
INV_ROOT_TAU = 0.3989422804014327


def params(mib=60):
    return pltpu.CompilerParams(vmem_limit_bytes=mib << 20)


def dot_nn(a, b):
    return jnp.dot(a, b, preferred_element_type=F32)


def dot_nt(a, b):
    return lax.dot_general(a, b, (((1,), (1,)), ((), ())), preferred_element_type=F32)


def dot_tn(a, b):
    return lax.dot_general(a, b, (((0,), (0,)), ((), ())), preferred_element_type=F32)


def cost(flops, nbytes, trans=0):
    return pl.CostEstimate(flops=int(flops), bytes_accessed=int(nbytes), transcendentals=int(trans))


SUB = 32
ANY = pl.BlockSpec(memory_space=pltpu.HBM)


def loads(place, bufs, lo, hi, target, sem):
    found = []
    for buf in bufs:
        for m in range(buf.shape[0]):
            i = len(found)
            found.append(pltpu.make_async_copy(buf.at[m, pl.ds(lo, hi - lo)], target(place[i]), sem.at[i]))
    return found


def start_all(copies):
    for c in copies:
        c.start()


def wait_all(copies):
    for c in copies:
        c.wait()


def qkv_body(count, place, x_ref, b_ref, *rest):
    bufs, (o_ref, w_vm, sem) = rest[:count], rest[count:]
    step = pl.program_id(0)
    blocks, width = w_vm.shape[0], w_vm.shape[-1]
    copies = loads(place, bufs, 0, blocks, lambda p: w_vm.at[:, p], sem)

    @pl.when(step == 0)
    def _():
        start_all(copies)
        wait_all(copies)

    x = x_ref[...]
    for n in range(blocks):
        w = w_vm[n].reshape(-1, width)
        bias = b_ref[:, n * width : (n + 1) * width]
        o_ref[:, n * width : (n + 1) * width] = (dot_nn(x, w) + bias).astype(BF)


def qkv_call(x, place, w1, bias, rows=256):
    slots, width = x.shape
    pieces = width // SUB
    return pl.pallas_call(
        functools.partial(qkv_body, len(w1)),
        name="qkv",
        grid_spec=pltpu.PrefetchScalarGridSpec(
            num_scalar_prefetch=1,
            grid=(slots // rows,),
            in_specs=[
                pl.BlockSpec((rows, width), lambda i, p: (i, 0)),
                pl.BlockSpec((1, 3 * width), lambda i, p: (0, 0)),
            ] + [ANY] * len(w1),
            out_specs=pl.BlockSpec((rows, 3 * width), lambda i, p: (i, 0)),
            scratch_shapes=[
                pltpu.VMEM((3, pieces, SUB, width), BF),
                pltpu.SemaphoreType.DMA((pieces,)),
            ],
        ),
        out_shape=jax.ShapeDtypeStruct((slots, 3 * width), BF),
        compiler_params=params(32),
        cost_estimate=cost(6 * slots * width * width, 8 * slots * width + 6 * width * width),
    )(place, x, bias, *w1)


def lanes(rows):
    return lax.broadcasted_iota(jnp.int32, (rows, 2 * HD), 1)


def split3(v):
    hi = v.astype(BF).astype(F32)
    mid = (v - hi).astype(BF).astype(F32)
    return hi, mid, v - hi - mid


def attn_fwd_body(rows, len_ref, q_ref, k_ref, v_ref, *rest):
    ctx_ref, qa0_ref, qa1_ref = rest[-3:]
    slots = k_ref.shape[0]
    lane = lanes(slots)
    key_row = lax.broadcasted_iota(jnp.int32, (slots, 2 * HD), 0)
    bias = jnp.where(key_row < len_ref[0], 0.0, -1e30)
    k = k_ref[...].astype(F32)
    k_aug = []
    for h in range(2):
        own = (lane // HD) == h
        spare = (1 - h) * HD
        k_aug.append(jnp.where(own, k, jnp.where(lane == spare, bias, 0.0)).astype(BF))
    v_aug = [jnp.where((lane // HD) == h, v_ref[...].astype(F32), 1.0).astype(BF) for h in range(2)]
    lane_q = lanes(rows)

    def scores(item):
        blk, h = item
        q = q_ref[blk * rows : (blk + 1) * rows, :].astype(F32) * 0.125
        qh = jnp.where((lane_q // HD) == h, q, jnp.where(lane_q == (1 - h) * HD, 1.0, 0.0))
        return qh, dot_nt(qh.astype(BF), k_aug[h])

    items = [(blk, h) for blk in range(slots // rows) for h in range(2)]
    held = scores(items[0])
    outs = []
    for i, (blk, h) in enumerate(items):
        sl = slice(blk * rows, (blk + 1) * rows)
        qh, s = held
        if i + 1 < len(items):
            held = scores(items[i + 1])
        spare = (1 - h) * HD
        top = jnp.max(s, axis=-1, keepdims=True)
        o = dot_nn(jnp.exp(s - top).astype(BF), v_aug[h])
        norm = o[:, spare : spare + 1]
        outs.append(o / norm)
        hi, mid, lo = split3(-(top + jnp.log(norm)))
        qh = jnp.where(lane_q == spare + 1, hi, qh)
        qh = jnp.where(lane_q == spare + 2, mid, qh)
        qh = jnp.where(lane_q == spare + 3, lo, qh)
        (qa0_ref, qa1_ref)[h][sl, :] = qh.astype(BF)
        if h == 1:
            ctx_ref[sl, :] = jnp.where(lane_q < HD, outs[-2], outs[-1]).astype(BF)


def attn_fwd_call(qkv, lengths, part, parts, before, rows=256):
    slots, wide = qkv.shape
    width = wide // 3
    pairs = width // (2 * HD)
    each = pairs // parts
    col = lambda off: pl.BlockSpec((slots, 2 * HD), lambda j, ln: (0, off * pairs + part * each + j))
    out = jax.ShapeDtypeStruct((slots, width), BF)
    extra = list(before or ())
    return pl.pallas_call(
        functools.partial(attn_fwd_body, rows),
        name=f"attn_fwd{part}",
        grid_spec=pltpu.PrefetchScalarGridSpec(
            num_scalar_prefetch=1,
            grid=(each,),
            in_specs=[col(0), col(1), col(2)] + [ANY] * len(extra),
            out_specs=[col(0)] * 3,
        ),
        out_shape=[out, out, out],
        input_output_aliases={4 + i: i for i in range(3)} if before else {},
        compiler_params=params(32),
        cost_estimate=cost(
            16 * slots * slots * width / parts, 12 * slots * width / parts, slots * slots * 2 * each
        ),
    )(lengths, qkv, qkv, qkv, *extra)


def attn_bwd_body(rows, len_ref, qa0_ref, qa1_ref, k_ref, v_ref, ctx_ref, g_ref, *rest):
    dq_ref, dk_ref, dv_ref, sq_ref, sv_ref = rest[-5:]
    slots = k_ref.shape[0]
    lane = lanes(slots)
    key_row = lax.broadcasted_iota(jnp.int32, (slots, 2 * HD), 0)
    bias = jnp.where(key_row < len_ref[0], 0.0, -1e30)
    k = k_ref[...].astype(F32)
    v = v_ref[...].astype(F32)
    k_low = k_ref[...]
    k_aug, v_aug = [], []
    for h in range(2):
        own = (lane // HD) == h
        spare = (1 - h) * HD
        near = (lane > spare) & (lane < spare + 4)
        ones = jnp.where(near, 1.0, 0.0)
        k_aug.append(jnp.where(own, k, jnp.where(lane == spare, bias, ones)).astype(BF))
        v_aug.append(jnp.where(own, v, ones).astype(BF))
    lane_q = lanes(rows)
    items = [(blk, h) for blk in range(slots // rows) for h in range(2)]

    def products(item):
        blk, h = item
        sl = slice(blk * rows, (blk + 1) * rows)
        own = (lane_q // HD) == h
        spare = (1 - h) * HD
        g = g_ref[sl, :].astype(F32)
        delta = jnp.sum(jnp.where(own, g * ctx_ref[sl, :].astype(F32), 0.0), axis=-1, keepdims=True)
        hi, mid, lo = split3(-delta)
        ga = jnp.where(own, g, 0.0)
        ga = jnp.where(lane_q == spare + 1, hi, ga)
        ga = jnp.where(lane_q == spare + 2, mid, ga)
        ga = jnp.where(lane_q == spare + 3, lo, ga).astype(BF)
        return dot_nt(k_aug[h], (qa0_ref, qa1_ref)[h][sl, :]), dot_nt(v_aug[h], ga)

    held = products(items[0])
    dk = [jnp.zeros((slots, 2 * HD), F32)] * 2
    dv = [jnp.zeros((slots, 2 * HD), F32)] * 2
    dqs = []
    for i, (blk, h) in enumerate(items):
        sl = slice(blk * rows, (blk + 1) * rows)
        s, gs = held
        if i + 1 < len(items):
            held = products(items[i + 1])
        p = jnp.exp(s)
        ds = (p * gs).astype(BF)
        dv[h] = dv[h] + dot_nn(p.astype(BF), g_ref[sl, :])
        dk[h] = dk[h] + dot_nn(ds, (qa0_ref, qa1_ref)[h][sl, :])
        dqs.append(dot_tn(ds, k_low))
        if h == 1:
            dq_ref[sl, :] = (jnp.where(lane_q < HD, dqs[-2], dqs[-1]) * 0.125).astype(BF)
    dk_ref[...] = jnp.where(lane < HD, dk[0], dk[1]).astype(BF)
    dv_low = jnp.where(lane < HD, dv[0], dv[1]).astype(BF)
    dv_ref[...] = dv_low
    sq_ref[...] = jnp.sum(dq_ref[...].astype(F32), axis=0, keepdims=True)
    sv_ref[...] = jnp.sum(dv_low.astype(F32), axis=0, keepdims=True)


def attn_bwd_call(qa0, qa1, qkv, ctx, grad_ctx, lengths, part, parts, before, rows=256):
    slots, width = ctx.shape
    pairs = width // (2 * HD)
    each = pairs // parts
    col = lambda off: pl.BlockSpec((slots, 2 * HD), lambda j, ln: (0, off * pairs + part * each + j))
    row = pl.BlockSpec((1, 2 * HD), lambda j, ln: (0, part * each + j))
    out = jax.ShapeDtypeStruct((slots, width), BF)
    vec = jax.ShapeDtypeStruct((1, width), F32)
    extra = list(before or ())
    return pl.pallas_call(
        functools.partial(attn_bwd_body, rows),
        name=f"attn_bwd{part}",
        grid_spec=pltpu.PrefetchScalarGridSpec(
            num_scalar_prefetch=1,
            grid=(each,),
            in_specs=[col(0), col(0), col(1), col(2), col(0), col(0)] + [ANY] * len(extra),
            out_specs=[col(0)] * 3 + [row] * 2,
        ),
        out_shape=[out, out, out, vec, vec],
        input_output_aliases={7 + i: i for i in range(5)} if before else {},
        compiler_params=params(32),
        cost_estimate=cost(
            40 * slots * slots * width / parts, 18 * slots * width / parts, slots * slots * 2 * each
        ),
    )(lengths, qa0, qa1, qkv, qkv, ctx, grad_ctx, *extra)


def norm_stats(resid):
    mean = jnp.mean(resid, axis=-1, keepdims=True)
    centred = resid - mean
    inv = lax.rsqrt(jnp.mean(centred * centred, axis=-1, keepdims=True) + 1e-5)
    return centred * inv, inv


def norm_back(u, normed, inv):
    return inv * (u - jnp.mean(u, axis=-1, keepdims=True) - normed * jnp.mean(u * normed, axis=-1, keepdims=True))


def colsum(v):
    return jnp.sum(v, axis=0, keepdims=True)


def row_body(n2, len_ref, place, x_ref, ctx_ref, cot_ref, vec_ref, bin_ref, *rest):
    b2 = rest[:n2]
    (
        out_ref, act_ref, hid_ref, gf_ref, gp_ref, ga_ref, gc_ref, sums_ref, sbin_ref,
        wa, wi, wo, slope, sem,
    ) = rest[n2:]
    step = pl.program_id(0)
    rows, width = x_ref.shape
    nblk = wi.shape[0]
    copies = [
        loads(place, b2, 0, 1, lambda p: wa.at[pl.ds(p, 1)], sem.at[0]),
        loads(place, b2, 1, 1 + nblk, lambda p: wi.at[:, p], sem.at[1]),
        loads(place, b2, 1 + nblk, 5 + nblk, lambda p: wo.at[p], sem.at[2]),
    ]

    @pl.when(step == 0)
    def _():
        for c in copies:
            start_all(c)
        sums_ref[...] = jnp.zeros_like(sums_ref)
        sbin_ref[...] = jnp.zeros_like(sbin_ref)

    def ready(i):
        @pl.when(step == 0)
        def _():
            wait_all(copies[i])

    bao, gain1, shift1, bout, gain2, shift2 = [vec_ref[i : i + 1, :] for i in range(6)]
    ready(0)
    w_ao = wa[...].reshape(width, width)
    resid1 = x_ref[...].astype(F32) + dot_nn(ctx_ref[...], w_ao) + bao
    normed1, inv1 = norm_stats(resid1)
    hidden = normed1 * gain1 + shift1
    low = hidden.astype(BF)
    hid_ref[...] = low
    acc = jnp.zeros((rows, width), F32)
    per = wo.shape[0] // nblk
    ready(1)
    for n in range(nblk):
        pre = dot_nn(low, wi[n].reshape(width, width)) + bin_ref[n : n + 1, :]
        phi = 0.5 + 0.5 * lax.erf(pre * SQRT_HALF)
        slope[n] = (phi + pre * (INV_ROOT_TAU * jnp.exp(-0.5 * pre * pre))).astype(slope.dtype)
        act = (pre * phi).astype(BF)
        act_ref[:, n * width : (n + 1) * width] = act
        if n == 0:
            ready(2)
        acc = acc + dot_nn(act, wo[n * per : (n + 1) * per].reshape(width, width))
    resid2 = hidden + acc + bout
    normed2, inv2 = norm_stats(resid2)
    row_id = lax.broadcasted_iota(jnp.int32, (rows, 1), 0) + step * rows
    valid = (row_id < len_ref[0]).astype(F32)
    out_ref[...] = ((normed2 * gain2 + shift2) * valid).astype(BF)
    gz = cot_ref[...].astype(F32) * valid
    sums_ref[0:1, :] += colsum(gz * normed2)
    sums_ref[1:2, :] += colsum(gz)
    g_resid2 = norm_back(gz * gain2, normed2, inv2)
    gf = g_resid2.astype(BF)
    gf_ref[...] = gf
    sums_ref[2:3, :] += colsum(gf.astype(F32))
    acc = g_resid2
    for n in range(nblk):
        g_act = dot_nt(gf, wo[n * per : (n + 1) * per].reshape(width, width))
        gp = (g_act * slope[n].astype(F32)).astype(BF)
        gp_ref[:, n * width : (n + 1) * width] = gp
        sbin_ref[n : n + 1, :] += colsum(gp.astype(F32))
        acc = acc + dot_nt(gp, wi[n].reshape(width, width))
    sums_ref[3:4, :] += colsum(acc * normed1)
    sums_ref[4:5, :] += colsum(acc)
    g_attn = norm_back(acc * gain1, normed1, inv1).astype(BF)
    ga_ref[...] = g_attn
    sums_ref[5:6, :] += colsum(g_attn.astype(F32))
    gc_ref[...] = dot_nt(g_attn, w_ao).astype(BF)


def row_call(x, ctx, cot, place, w2, vecs, b_in, lengths, rows=256):
    slots, width = x.shape
    pieces, sub = width // SUB, SUB
    nblk = b_in.shape[0]
    ff = nblk * width
    blk = pl.BlockSpec((rows, width), lambda i, ln, p: (i, 0))
    big = pl.BlockSpec((rows, ff), lambda i, ln, p: (i, 0), pipeline_mode=pl.Buffered(1 if rows > 256 else 2))
    const = lambda r: pl.BlockSpec((r, width), lambda i, ln, p: (0, 0))
    o = jax.ShapeDtypeStruct((slots, width), BF)
    ob = jax.ShapeDtypeStruct((slots, ff), BF)
    return pl.pallas_call(
        functools.partial(row_body, len(w2)),
        name="row_local",
        grid_spec=pltpu.PrefetchScalarGridSpec(
            num_scalar_prefetch=2,
            grid=(slots // rows,),
            in_specs=[blk, blk, blk, const(8), const(nblk)] + [ANY] * len(w2),
            out_specs=[blk, big, blk, blk, big, blk, blk, const(8), const(nblk)],
            scratch_shapes=[
                pltpu.VMEM((pieces, sub, width), BF),
                pltpu.VMEM((nblk, pieces, sub, width), BF),
                pltpu.VMEM((pieces, 4, sub, width), BF),
                pltpu.VMEM((nblk, rows, width), BF),
                pltpu.SemaphoreType.DMA((3, pieces)),
            ],
        ),
        out_shape=[
            o, ob, o, o, ob, o, o,
            jax.ShapeDtypeStruct((8, width), F32),
            jax.ShapeDtypeStruct((nblk, width), F32),
        ],
        compiler_params=params(),
        cost_estimate=cost(36 * slots * width * width, 40 * slots * width + 18 * width * width, 2 * slots * ff),
    )(lengths, place, x, ctx, cot, vecs, b_in, *w2)


def halves(core, value, keep_ref, send_ref):
    count, rows, width = keep_ref.shape
    value = value.reshape(count, 2, rows, width)
    even, odd = value[:, 0], value[:, 1]

    @pl.when(core == 0)
    def _():
        keep_ref[...] = even
        send_ref[...] = odd

    @pl.when(core != 0)
    def _():
        keep_ref[...] = odd
        send_ref[...] = even


LINES = 16


def lines_of(*lines):
    width, segments = lines[0][0], [line[1:] for line in lines]
    row = lax.broadcasted_iota(jnp.int32, (LINES, width), 0)
    value = jnp.zeros((LINES, width), F32)
    for i, segs in enumerate(segments):
        used = sum(v.shape[1] for v in segs)
        line = jnp.concatenate(segs + [jnp.zeros((1, width - used), F32)] * (used < width), 1)
        value = jnp.where(row == i, line, value)
    return value.astype(BF)


def wgrad_body(core, a_ref, b_ref, keep_ref, send_ref):
    halves(core[0], dot_tn(a_ref[...], b_ref[...]).astype(BF), keep_ref, send_ref)


def wgrad_call(name, core, a, b, by_rows, tile=1024):
    slots, m = a.shape
    width = a.shape[1] if not by_rows else b.shape[1]
    blocks = m // width if by_rows else b.shape[1] // m
    pieces = width // SUB
    if by_rows:
        grid = (1, m // tile)
        block = (tile // (2 * SUB * blocks), blocks * SUB, width)
        where = lambda j, i, c: (i, 0, 0)
    else:
        grid = (blocks, m // tile)
        block = (tile // (2 * SUB), SUB, width)
        where = lambda j, i, c: (i, j, 0)
    out = jax.ShapeDtypeStruct((pieces // 2, blocks * SUB, width), BF)
    return pl.pallas_call(
        wgrad_body,
        name=name,
        grid_spec=pltpu.PrefetchScalarGridSpec(
            num_scalar_prefetch=1,
            grid=grid,
            in_specs=[
                pl.BlockSpec((slots, tile), lambda j, i, c: (0, i)),
                pl.BlockSpec((slots, width), lambda j, i, c: (0, j)),
            ],
            out_specs=[pl.BlockSpec(block, where)] * 2,
        ),
        out_shape=[out, out],
        compiler_params=params(32),
        cost_estimate=cost(2 * slots * m * b.shape[1], 2 * (slots * (m + b.shape[1]) + m * b.shape[1])),
    )(core, a, b)


def wgrad_ao_body(core, a_ref, b_ref, sums_ref, sbin_ref, keep_ref, send_ref):
    value = dot_tn(a_ref[...], b_ref[...]).astype(BF)
    halves(core[0], value, keep_ref.at[:, pl.ds(0, SUB)], send_ref.at[:, pl.ds(0, SUB)])
    count, _, width = keep_ref.shape
    owners = count // 2
    part, four = width // owners, sbin_ref.shape[0] * width // owners
    for s in range(owners):
        segs = [sums_ref[v : v + 1, s * part : (s + 1) * part] for v in (5, 3, 4, 2, 0, 1)]
        row, col = s * four // width, s * four % width
        value = lines_of([width, *segs], [width, sbin_ref[row : row + 1, col : col + four]])
        for ref in (keep_ref, send_ref):
            for x in (0, 1):
                ref[2 * s + x, SUB : SUB + LINES] = value


def wgrad_ao(core, a, b, sums, sbin):
    slots, m = a.shape
    full = lambda v: pl.BlockSpec(v.shape, lambda t, c: (0, 0))
    shape = (m // SUB // 2, SUB + LINES, m)
    return pl.pallas_call(
        wgrad_ao_body,
        name="wgrad_ao",
        grid_spec=pltpu.PrefetchScalarGridSpec(
            num_scalar_prefetch=1,
            grid=(1,),
            in_specs=[full(v) for v in (a, b, sums, sbin)],
            out_specs=[pl.BlockSpec(shape, lambda t, c: (0, 0, 0))] * 2,
        ),
        out_shape=[jax.ShapeDtypeStruct(shape, BF)] * 2,
        compiler_params=params(32),
        cost_estimate=cost(2 * slots * m * m, 4 * slots * m + 2 * m * m),
    )(core, a, b, sums, sbin)


def wgrad3_body(core, a_ref, q_ref, k_ref, v_ref, sq_ref, sv_ref, keep_ref, send_ref):
    for n, ref in enumerate((q_ref, k_ref, v_ref)):
        value = dot_tn(a_ref[...], ref[...]).astype(BF)
        rows = pl.ds(n * SUB, SUB)
        halves(core[0], value, keep_ref.at[:, rows], send_ref.at[:, rows])
    count, _, width = keep_ref.shape
    line = jnp.where(pl.program_id(0) == 0, sq_ref[...], sv_ref[...])
    part = 2 * width // count
    for s in range(count // 2):
        value = lines_of([width, line[:, s * part : (s + 1) * part]])
        for ref in (keep_ref, send_ref):
            for x in (0, 1):
                ref[2 * s + x, 3 * SUB : 3 * SUB + LINES] = value


def wgrad3(core, a, dq, dk, dv, sq, sv):
    slots, m = a.shape
    tile = m // 2
    full = pl.BlockSpec((slots, m), lambda i, c: (0, 0))
    vec = pl.BlockSpec((1, m), lambda i, c: (0, 0))
    block = pl.BlockSpec((tile // (2 * SUB), 3 * SUB + LINES, m), lambda i, c: (i, 0, 0))
    out = jax.ShapeDtypeStruct((m // SUB // 2, 3 * SUB + LINES, m), BF)
    return pl.pallas_call(
        wgrad3_body,
        name="wgrad_qkv",
        grid_spec=pltpu.PrefetchScalarGridSpec(
            num_scalar_prefetch=1,
            grid=(2,),
            in_specs=[pl.BlockSpec((slots, tile), lambda i, c: (0, i)), full, full, full, vec, vec],
            out_specs=[block, block],
        ),
        out_shape=[out, out],
        compiler_params=params(32),
        cost_estimate=cost(6 * slots * m * m, 14 * slots * m),
    )(core, a, dq, dk, dv, sq, sv)


def tok_body(count, place, g_ref, dq_ref, dk_ref, dv_ref, *rest):
    bufs, (o_ref, w_vm, sem) = rest[:count], rest[count:]
    step = pl.program_id(0)
    width = g_ref.shape[1]
    copies = loads(place, bufs, 0, 3, lambda p: w_vm.at[:, p], sem)

    @pl.when(step == 0)
    def _():
        start_all(copies)
        wait_all(copies)

    acc = g_ref[...].astype(F32)
    for n, ref in enumerate((dq_ref, dk_ref, dv_ref)):
        acc = acc + dot_nt(ref[...], w_vm[n].reshape(width, width))
    o_ref[...] = acc.astype(BF)


def tok_call(g, dq, dk, dv, place, w1, rows=256):
    slots, width = g.shape
    pieces = width // SUB
    blk = pl.BlockSpec((rows, width), lambda i, p: (i, 0))
    return pl.pallas_call(
        functools.partial(tok_body, len(w1)),
        name="grad_tok",
        grid_spec=pltpu.PrefetchScalarGridSpec(
            num_scalar_prefetch=1,
            grid=(slots // rows,),
            in_specs=[blk, blk, blk, blk] + [ANY] * len(w1),
            out_specs=blk,
            scratch_shapes=[pltpu.VMEM((3, pieces, SUB, width), BF), pltpu.SemaphoreType.DMA((pieces,))],
        ),
        out_shape=jax.ShapeDtypeStruct((slots, width), BF),
        compiler_params=params(32),
        cost_estimate=cost(6 * slots * width * width, 16 * slots * width),
    )(place, g, dq, dk, dv, *w1)


def total(*terms):
    acc = terms[0].astype(F32)
    for t in terms[1:]:
        acc = acc + t.astype(F32)
    return acc.astype(BF)


def add1_body(count, here, *refs):
    ins, outs = refs[: 8 * count], refs[8 * count :]
    for view in range(4):
        n0 = 0
        for i in range(count):
            a, b = ins[8 * i + 2 * view], ins[8 * i + 2 * view + 1]
            n = a.shape[3]
            outs[view][0, n0 : n0 + n] = total(a[0, 0, 0], b[0, 0, 0])
            n0 += n


def add1(here, pairs):
    width = pairs[0][0].shape[-1]
    views = []
    for half, own in ((0, 0), (0, 1), (1, 0), (1, 1)):
        def where(t, h, half=half, own=own):
            z, j = 2 * half + t // 2, t % 2
            if half == 0:
                return (z, j, h[0] if own else 1 - h[0], 0, 0)
            return (z, h[1] if own else 1 - h[1], j, 0, 0)
        views.append(where)
    specs, args, rows = [], [], 0
    for keep, got in pairs:
        n = keep.shape[1]
        rows += n
        for where in views:
            for arr in (keep, got):
                specs.append(pl.BlockSpec((1, 1, 1, n, width), where))
                args.append(arr.reshape(4, 2, 2, n, width))
    out = jax.ShapeDtypeStruct((4, rows, width), BF)
    return pl.pallas_call(
        functools.partial(add1_body, len(pairs)),
        name="add_core",
        grid_spec=pltpu.PrefetchScalarGridSpec(
            num_scalar_prefetch=1,
            grid=(4,),
            in_specs=specs,
            out_specs=[pl.BlockSpec((1, rows, width), lambda t, h: (t, 0, 0))] * 4,
        ),
        out_shape=[out] * 4,
        compiler_params=params(24),
        cost_estimate=cost(16 * rows * width, 96 * rows * width),
    )(here, *args)


def add2_body(here, *refs):
    ins, outs = refs[:8], refs[8:]
    for view in range(4):
        outs[view][0] = total(ins[2 * view][0, 0], ins[2 * view + 1][0, 0])


def add2(here, first, second):
    _, rows, width = first[0].shape
    specs, args = [], []
    for axis, pair in ((1, first), (0, second)):
        for own in (0, 1):
            for arr in pair:
                specs.append(pl.BlockSpec(
                    (1, 1, rows, width),
                    lambda t, h, axis=axis, own=own: (t, h[axis] if own else 1 - h[axis], 0, 0),
                ))
                args.append(arr.reshape(2, 2, rows, width))
    out = jax.ShapeDtypeStruct((2, rows, width), BF)
    return pl.pallas_call(
        add2_body,
        name="add_plane",
        grid_spec=pltpu.PrefetchScalarGridSpec(
            num_scalar_prefetch=1,
            grid=(2,),
            in_specs=specs,
            out_specs=[pl.BlockSpec((1, rows, width), lambda t, h: (t, 0, 0))] * 4,
        ),
        out_shape=[out] * 4,
        compiler_params=params(24),
        cost_estimate=cost(8 * rows * width, 48 * rows * width),
    )(here, *args)


def add3_body(here, ak, ag, bk, bg, *outs):
    for k, out in enumerate(outs):
        to = lax.rem(here[2] + k, 4)
        spot = lax.rem(to, 2)

        @pl.when(to < 2)
        def _():
            out[0] = total(ak[spot], ag[spot])

        @pl.when(to >= 2)
        def _():
            out[0] = total(bk[spot], bg[spot])


def add3(here, first, second):
    _, rows, width = first[0].shape
    full = pl.BlockSpec((2, rows, width), lambda t, h: (0, 0, 0))
    one = pl.BlockSpec((1, rows, width), lambda t, h: (0, 0, 0))
    return pl.pallas_call(
        add3_body,
        name="add_z",
        grid_spec=pltpu.PrefetchScalarGridSpec(
            num_scalar_prefetch=1, grid=(1,), in_specs=[full] * 4, out_specs=[one] * 4,
        ),
        out_shape=[jax.ShapeDtypeStruct((1, rows, width), BF)] * 4,
        compiler_params=params(24),
        cost_estimate=cost(4 * rows * width, 24 * rows * width),
    )(here, *first, *second)


def add4_body(*refs):
    ins, out = refs[:-1], refs[-1]
    n0 = 0
    for i in range(0, len(ins), 4):
        n = ins[i].shape[1]
        out[:, n0 : n0 + n] = total(*[r[...] for r in ins[i : i + 4]])
        n0 += n


def add4(*groups):
    spec = lambda shape: pl.BlockSpec(shape, lambda t: (0,) * len(shape))
    width = groups[0][0].shape[-1]
    shape = (1, sum(g[0].shape[1] for g in groups), width)
    parts = [v for g in groups for v in g]
    size = shape[1] * width
    return pl.pallas_call(
        add4_body,
        name="add_last",
        grid=(1,),
        in_specs=[spec(v.shape) for v in parts],
        out_specs=spec(shape),
        out_shape=jax.ShapeDtypeStruct(shape, BF),
        compiler_params=params(24),
        cost_estimate=cost(3 * size, 10 * size),
    )(*parts)


def final_body(kinds, vectors, here, own, core, over_x, both, *outs):
    mine_at = 2 * here[0] + here[3]
    mats, vecs = outs[: len(kinds)], outs[len(kinds) :]
    for flip, ref in enumerate((own, core, over_x, both)):
        share = jnp.bitwise_xor(mine_at, flip)
        n0 = 0
        for (blocks, by_rows), out in zip(kinds, mats):
            width = ref.shape[-1]
            for n in range(blocks):
                value = ref[0, n0 : n0 + SUB].astype(F32)
                n0 += SUB
                if by_rows:
                    out[pl.ds(pl.multiple_of(share * blocks * SUB, SUB) + n * SUB, SUB), :] = value
                else:
                    out[pl.ds(pl.multiple_of(share * SUB, SUB), SUB), n * width : (n + 1) * width] = value

        @pl.when(share == 0)
        def _():
            lines = ref[0, n0 : n0 + LINES].astype(F32)
            for (row, lane, size), out in zip(vectors, vecs):
                out[...] = lines[row : row + 1, lane : lane + size]


def final_call(here, parts, kinds, vectors):
    shape = parts[0].shape
    width = shape[-1]
    shapes = [
        (4 * blocks * SUB, width) if by_rows else (4 * SUB, blocks * width) for blocks, by_rows in kinds
    ] + [(1, size) for _, _, size in vectors]
    return pl.pallas_call(
        functools.partial(final_body, kinds, vectors),
        name="final",
        grid_spec=pltpu.PrefetchScalarGridSpec(
            num_scalar_prefetch=1,
            grid=(1,),
            in_specs=[pl.BlockSpec(shape, lambda t, h: (0, 0, 0))] * 4,
            out_specs=[pl.BlockSpec(sh, lambda t, h: (0, 0)) for sh in shapes],
        ),
        out_shape=[jax.ShapeDtypeStruct(sh, F32) for sh in shapes],
        compiler_params=params(24),
        cost_estimate=cost(1, 24 * parts[0].size),
    )(here, *parts)


BOTH = ("shard", "replica")
AXES = ("replica", "shard")


def table(fn):
    pairs = []
    for r in range(4):
        for s in range(8):
            x, y, z, c = fn(r // 2, s % 2, s // 2, r % 2)
            pairs.append((r * 8 + s, (x * 2 + c) * 8 + z * 2 + y))
    return pairs


TO_CORE = table(lambda x, y, z, c: (x, y, z, 1 - c))
TO_X = table(lambda x, y, z, c: (1 - x, y, z, c))
TO_XCORE = table(lambda x, y, z, c: (1 - x, y, z, 1 - c))
TO_Y = table(lambda x, y, z, c: (x, 1 - y, z, c))
TO_Z = [table(lambda x, y, z, c, k=k: (x, y, (z + k) % 4, c)) for k in range(4)]


def move(v, pairs):
    return lax.ppermute(v, AXES, pairs)


def regular():
    return lax.axis_size("shard") == 8 and lax.axis_size("replica") == 4


def place_of():
    r, s = lax.axis_index("replica"), lax.axis_index("shard")
    return r // 2, s % 2, s // 2, r % 2


def pack_body(share, *refs):
    ins, out = refs[:-1], refs[-1]
    width = out.shape[-1]
    n0 = 0
    for ref in ins:
        rows, cols = ref.shape
        if rows > SUB:
            out[0, n0 : n0 + rows // SUB] = ref[...].reshape(rows // SUB, SUB, width)
            n0 += rows // SUB
        else:
            for n in range(cols // width):
                out[0, n0 + n] = ref[:, n * width : (n + 1) * width]
            n0 += cols // width


def pack(share, mats, width):
    shapes = [(m.shape[0] // 4, m.shape[1]) for m in mats]
    blocks = sum(r * c for r, c in shapes) // (SUB * width)
    return pl.pallas_call(
        pack_body,
        name="pack",
        grid_spec=pltpu.PrefetchScalarGridSpec(
            num_scalar_prefetch=1,
            grid=(1,),
            in_specs=[pl.BlockSpec(sh, lambda t, r: (r[0], 0)) for sh in shapes],
            out_specs=pl.BlockSpec((1, blocks, SUB, width), lambda t, r: (0, 0, 0, 0)),
        ),
        out_shape=jax.ShapeDtypeStruct((1, blocks, SUB, width), BF),
        compiler_params=params(),
        cost_estimate=cost(1, 4 * blocks * SUB * width),
    )(share, *mats)


def pack_first_body(share, w_ref, *refs):
    vecs, out = refs[:-1], refs[-1]
    rows, width = 3 * SUB, out.shape[-1]
    for n in range(3):
        out[0, n * SUB : (n + 1) * SUB] = w_ref[:, n * width : (n + 1) * width]
    segs = [v[...].astype(F32) for v in vecs]
    out[0, rows : rows + LINES] = lines_of([width, *segs[:-1]], [width, segs[-1]])


def pack_first(share, w_qkv, vecs, width):
    rows = w_qkv.shape[0] // 4
    vecs = [v.reshape(1, -1) for v in vecs]
    shape = (1, 3 * rows + LINES, width)
    return pl.pallas_call(
        pack_first_body,
        name="pack_first",
        grid_spec=pltpu.PrefetchScalarGridSpec(
            num_scalar_prefetch=1,
            grid=(1,),
            in_specs=[pl.BlockSpec((rows, 3 * width), lambda t, r: (r[0], 0))]
            + [pl.BlockSpec(v.shape, lambda t, r: (0, 0)) for v in vecs],
            out_specs=pl.BlockSpec(shape, lambda t, r: (0, 0, 0)),
        ),
        out_shape=jax.ShapeDtypeStruct(shape, BF),
        compiler_params=params(),
        cost_estimate=cost(1, 12 * rows * width),
    )(share, w_qkv, *vecs)


def after(v, *deps):
    return lax.optimization_barrier((v,) + deps)[0]


def to_core(bufs):
    return [move(v, TO_CORE) for v in bufs]


def tied(*groups):
    flat = lax.optimization_barrier([v for g in groups for v in g])
    out = []
    for g in groups:
        out.append(flat[: len(g)])
        flat = flat[len(g) :]
    return out


def gather_places(order):
    x, y, z, c = place_of()
    spots = []
    for fc in (0, 1):
        for k, fx, fy in order:
            spots.append((((z - k) % 4) * 2 + (y ^ fy)) * 4 + (x ^ fx) * 2 + (c ^ fc))
    return jnp.stack(spots).astype(jnp.int32)


FIRST = [
    (k0 + k, fx, fy)
    for k0, fx, fy in ((0, 0, 0), (2, 0, 0), (0, 0, 1), (2, 1, 0), (0, 1, 0), (2, 0, 1), (0, 1, 1), (2, 1, 1))
    for k in (0, 1)
]
SECOND = [
    (0, 0, 0), (0, 1, 0), (1, 0, 0), (3, 0, 0), (2, 0, 0), (0, 0, 1), (1, 1, 0), (3, 1, 0),
    (1, 0, 1), (3, 0, 1), (2, 1, 0), (0, 1, 1), (2, 0, 1), (3, 1, 1), (1, 1, 1), (2, 1, 1),
]


def spread(w, blocks, wide):
    full = lax.all_gather(w, "shard", axis=0, tiled=True)
    if full.shape[1] == wide:
        return full.reshape(-1, blocks, SUB, wide)
    return full.reshape(-1, SUB, blocks, wide).transpose(0, 2, 1, 3)


def sum_core(here, pairs):
    a_send, a_keep, b_send, b_keep = add1(here, pairs)
    return (a_keep, move(a_send, TO_X)), (b_keep, move(b_send, TO_Y))


def sum_plane(here, first, second):
    a_send, a_keep, b_send, b_keep = add2(here, first, second)
    return (a_keep, move(a_send, TO_Y)), (b_keep, move(b_send, TO_X))


def sum_z(here, first, second):
    own, *sends = add3(here, first, second)
    return [own] + [move(v, TO_Z[k + 1]) for k, v in enumerate(sends)]


def small_gather(lines):
    x, y, z, c = place_of()
    rows = jnp.concatenate([lines, move(lines, TO_Y)], 0)
    spots = jnp.stack([((z - k) % 4) * 2 + (y ^ f) for f in (0, 1) for k in range(4)])
    pick = (jnp.arange(8)[:, None] == spots[None, :]).astype(BF)
    return dot_nn(pick, rows)


def small_sum(rows):
    return lax.dynamic_index_in_dim(lax.psum(rows, BOTH), lax.axis_index("shard"), 0, keepdims=False)


def reduce_any(keep, send, by_rows):
    half, rows, wide = keep.shape
    full = jnp.stack([keep, send], 1).reshape(2 * half, rows // SUB, SUB, wide)
    full = full.reshape(-1, wide) if by_rows else full.transpose(0, 2, 1, 3).reshape(2 * half * SUB, -1)
    part = lax.psum_scatter(full, "shard", scatter_dimension=0, tiled=True)
    return lax.psum(part, "replica").astype(F32)


def shards(
    tokens, lengths, cotangent, w_qkv, b_qv, w_attn_out, b_attn_out, ln1_gain, ln1_bias,
    w_ffn_in, b_ffn_in, w_ffn_out, b_ffn_out, ln2_gain, ln2_bias,
):
    _, slots, width = tokens.shape
    nblk = w_ffn_in.shape[1] // width
    count = lax.axis_size("shard")
    x = tokens.reshape(slots, width)
    cot = cotangent.reshape(slots, width)
    small = [b_qv, b_attn_out, ln1_gain, ln1_bias, b_ffn_out, ln2_gain, ln2_bias, b_ffn_in]
    sizes = [v.shape[0] for v in small]
    ends = [sum(sizes[: i + 1]) for i in range(len(sizes))]

    if regular():
        share = lax.axis_index("replica").reshape(1).astype(jnp.int32)
        first = pack_first(share, w_qkv, small, width)
        second = pack(share, [after(w_attn_out, first), w_ffn_in, w_ffn_out], width)
        xo, yo = move(second, TO_X), move(second, TO_Y)
        along = [first] + [move(first, TO_Z[k]) for k in (1, 2, 3)]
        *along, xo, yo = lax.optimization_barrier((*along, xo, yo))
        a1, b1 = [
            jnp.concatenate([v[:, : 3 * SUB] for v in pair], 0).reshape(2, 3, SUB, width)
            for pair in (along[:2], along[2:])
        ]
        lines = jnp.concatenate([v[:, 3 * SUB : 3 * SUB + 2] for v in along], 0)
        rows = small_gather(lines.reshape(4, 2 * width)[:, : ends[-1]])
        second = after(second, along[3])
        near, *far = [move(second, TO_Z[k]) for k in (1, 2, 3)]
        plane = [move(a1, TO_Y), move(b1, TO_X), move(a1, TO_X), move(b1, TO_Y)]
        first = [a1, b1]
        cores = to_core(first)
        plane, cores = tied(plane, cores)
        last = [move(plane[0], TO_X), move(plane[1], TO_Y)]
        more = to_core(plane)
        _, [near, far[1]] = tied(last, [near, far[1]])
        w1 = [*first, *plane, *last, *cores, *more, *to_core(last)]
        r13 = jnp.concatenate([near, far[1]], 0)
        x1, y1 = move(r13, TO_X), move(r13, TO_Y)
        place, place2 = gather_places(FIRST), gather_places(SECOND)
        here = jnp.stack(place_of()).astype(jnp.int32)
    else:
        w1 = [spread(w_qkv, 3, width)]
        w2 = [spread(w_attn_out, 1, width), spread(w_ffn_in, nblk, width), spread(w_ffn_out, 4, width)]
        w2 = [jnp.concatenate(w2, 1)]
        place = place2 = jnp.arange(width // SUB, dtype=jnp.int32)
        here = jnp.zeros((4,), jnp.int32)
    core = here[3:]

    if not regular():
        rows = lax.all_gather(jnp.concatenate(small), "shard", axis=0).astype(F32)
    b_qv, bao, gain1, shift1, bout, gain2, shift2, b_in = [
        rows[:, e - s : e].reshape(-1) for s, e in zip(sizes, ends)
    ]
    bias3 = jnp.concatenate([b_qv[:width], jnp.zeros((width,), F32), b_qv[width:]]).reshape(1, -1)
    zero = jnp.zeros((width,), F32)
    vecs = jnp.stack([bao, gain1, shift1, bout, gain2, shift2, zero, zero])

    qkv = qkv_call(x, place, w1, bias3)
    parts = 4
    fwd = lambda i, state: attn_fwd_call(qkv, lengths, i, parts, state)
    state = fwd(0, None)
    if regular():
        [r2], [x1, y1], state = tied([far[0]], [x1, y1], state)
        c2 = jnp.concatenate([r2, yo], 0)
        x2, y2 = move(c2, TO_X), move(jnp.concatenate([r2, x1[1:]], 0), TO_Y)
        cores = to_core([second, xo, r13, x1, y1])
        state = fwd(1, state)
        cores, state = tied(cores, state)
        state = fwd(2, state)
        [x2, y2], state = tied([x2, y2], state)
        x3, y3 = move(y1[:1], TO_X), move(x2[:1], TO_Y)
        more = to_core([c2, x2, y2])
        more, state = tied(more, state)
        state = fwd(3, state)
        last, state = tied([x3, y3], state)
        w2 = [second, xo, r13, c2, x1, y1, x2, y2, *last]
        w2 += [*cores[:3], more[0], *cores[3:], *more[1:], *to_core(last)]
    else:
        for i in range(1, parts):
            state = fwd(i, state)
    ctx, qa0, qa1 = state
    out, act, low, gf, gp, ga, gc, sums, sbin = row_call(
        x, ctx, cot, place2, w2, vecs, b_in.reshape(nblk, width), lengths
    )
    p_wout = wgrad_call("wgrad_out", core, act, gf, True)
    p_win = wgrad_call("wgrad_in", core, low, gp, False)
    state = None
    bwd = lambda i, state, g: attn_bwd_call(qa0, qa1, qkv, ctx, g, lengths, i, parts, state)
    if regular():
        swap = lambda p: (p[0], move(p[1], TO_CORE))
        r_out = sum_core(here, [swap(p_wout)])
        p_wao = wgrad_ao(core, ctx, after(ga, r_out[0][0]), sums, sbin)
        r_in = sum_core(here, [swap(p_win), swap(p_wao)])
        def hold(r, state):
            (k0, g0), second = r
            return (after(k0, state[3]), g0), second

        gc = after(gc, r_in[0][0])
        state = bwd(0, None, gc)
        r_out = sum_plane(here, *hold(r_out, state))
        gc = after(gc, r_out[0][0])
        state = bwd(1, state, gc)
        state = bwd(2, state, gc)
        r_in = sum_plane(here, *hold(r_in, state))
        r_out = sum_z(here, *hold(r_out, state))
        gc = after(gc, r_out[0], r_in[0][0])
        state = bwd(3, state, gc)
        r_in = sum_z(here, *hold(r_in, state))
        dq, dk, dv, sq, sv = state
        p_wqkv = wgrad3(core, after(x, r_in[0], *r_out[1:]), dq, dk, dv, sq, sv)
        keep, send = p_wqkv
        r_qkv = sum_core(here, [swap((keep, after(send, r_in[1], r_in[3])))])
        g_tok = tok_call(after(ga, r_qkv[0][0]), dq, dk, dv, place, w1)
        (k0, g0), second = r_qkv
        r_qkv = sum_plane(here, (after(k0, g_tok, r_in[2]), g0), second)
        rest = add4(r_out, [after(r_in[0], r_qkv[0][0]), *r_in[1:]])
        own, *far = sum_z(here, *r_qkv)
        over_x = move(after(rest, own), TO_X)
        own = add4([own, *far])
        [rest, over_x], [own] = tied([rest, over_x], [own])
        vectors = [(0, 128 * i, 128) for i in range(6)] + [(1, 0, nblk * 128)]
        g_wout, g_win, g_wao, g_bao, g_g1, g_s1, g_bout, g_g2, g_s2, g_bin = final_call(
            here,
            (rest, move(rest, TO_CORE), over_x, move(over_x, TO_CORE)),
            [(4, True), (nblk, False), (1, False)],
            vectors,
        )
        over_x = move(own, TO_X)
        over_x, g_wout = lax.optimization_barrier((over_x, g_wout))
        shares = (own, move(own, TO_CORE), over_x, move(over_x, TO_CORE))
        g_wqkv, g_bqv = final_call(here, shares, [(3, False)], [(0, 0, 256)])
        vecs = [v.reshape(-1) for v in (g_bqv, g_bao, g_g1, g_s1, g_bin, g_bout, g_g2, g_s2)]
    else:
        p_wao = wgrad_call("wgrad_ao", core, ctx, ga, False)
        for i in range(parts):
            state = bwd(i, state, gc)
        dq, dk, dv, sq, sv = state
        p_wqkv = [v[:, : 3 * SUB] for v in wgrad3(core, x, dq, dk, dv, sq, sv)]
        g_tok = tok_call(ga, dq, dk, dv, place, w1)
        g_wout = reduce_any(*p_wout, True)
        g_win, g_wao, g_wqkv = [reduce_any(*p, False) for p in (p_win, p_wao, p_wqkv)]
        vecs = [jnp.concatenate([sq[0], sv[0]]), sums[5], sums[3], sums[4], sums[2], sums[0], sums[1], sbin]
        own = small_sum(jnp.concatenate([v.reshape(count, -1) for v in vecs], 1))
        vecs = [own[e - s : e] for s, e in zip(sizes, ends)]
        vecs.insert(4, vecs.pop())
    g_bqv, g_bao, g_g1, g_s1, g_bin, g_bout, g_g2, g_s2 = vecs
    return (
        out[None], g_tok[None], g_wqkv, g_bqv, g_wao, g_bao, g_g1, g_s1,
        g_win, g_bin, g_wout, g_bout, g_g2, g_s2,
    )


def solution(mesh):
    rows = P(("replica", "shard"), None, None)
    mat, vec = P("shard", None), P("shard")
    return jax.shard_map(
        shards,
        mesh=mesh,
        in_specs=(rows, P(("replica", "shard")), rows, mat, vec, mat, vec, vec, vec, mat, vec, mat, vec, vec, vec),
        out_specs=(rows, rows, mat, vec, mat, vec, vec, vec, mat, vec, mat, vec, vec, vec),
        check_vma=False,
    )
```
